32 devices in a mesh: row: 8 (over z, core), col: 4 (over y, x).
Axes of the slice: x: 2, y: 2, z: 4, core: 2. Of those that a mesh axis runs over, the one named last changes fastest.
Arguments:
- momentum_shards: bfloat16 [7168, 18432], P(('row', 'col')), may hold values from -0.078125 to 0.078125
- shard_starts: int32 [32], replicated, may hold values from 0 to 3528, as said below
Outputs:
- update_shards: bfloat16 [7168, 18432], P(('row', 'col'))
The draws below stay inside these ranges and needn't reach their ends.
Inputs may be any that keep to these rules, and one draw needn't show every extreme that they name: `shard_starts`: starts never fall and the first is 0; shard d starts within 56 rows of d * 112, and the last one exactly 56 rows after it. Every shard has at most 224 rows and some shard has exactly 224; the 4 shards of one index of row hold at most 560 rows together, and on some index exactly 560.
All inputs are finite; a program needn't handle non-finite values.
Results may differ from the reference program's by a relative error of at most 0.02.
Values may be sent and summed in bfloat16 or wider, within the bound.
No kernel may reach another device: no remote copies, remote signals or barrier semaphores. Data moves between devices by JAX's collectives and lax.ppermute only.
A program may use at most 128 MiB of HBM per device.

```python
import math
import jax
import jax.numpy as jnp
from jax import lax

M = 3584
N = 18432
SHARDS = 32
GROUP = 4
BASE = 112
JIT = 56
CAP = 224


def draw_shard_starts(key, part):
    shard_index = jnp.arange(SHARDS, dtype=jnp.int32)
    jitter = jax.random.randint(jax.random.fold_in(key, 11), (SHARDS,), -JIT, JIT + 1, dtype=jnp.int32)
    chosen = jax.random.randint(jax.random.fold_in(key, 12), (), 1, SHARDS // GROUP - 1, dtype=jnp.int32)
    run_start = chosen * GROUP
    jitter = jnp.where(shard_index == run_start, -JIT, jitter)
    jitter = jnp.where(shard_index == run_start + 1, JIT, jitter)
    jitter = jnp.where(shard_index == run_start + GROUP, JIT, jitter)
    jitter = jnp.where(shard_index == SHARDS - 1, JIT, jitter)
    jitter = jnp.where(shard_index == 0, 0, jitter)
    return (shard_index * BASE + jitter).astype(jnp.int32)


def block_levels(rng, dims, pieces, smallest, top_value):
    def one(dim, parts):
        steps = jax.random.uniform(jax.random.fold_in(jax.random.fold_in(rng, 6), dim), (parts,), jnp.float32, smallest / len(pieces), top_value / len(pieces))
        return jnp.repeat(jnp.exp(steps), dims[dim] // parts).reshape((-1,) + (1,) * (len(dims) - dim - 1))

    loudness = one(*pieces[0])
    for cut in pieces[1:]:
        loudness = loudness * one(*cut)
    return loudness


def normal_values(rng, extent, scale, reach, shards=(), kind=jnp.bfloat16):
    array = jax.random.normal(rng, extent, jnp.float32) * scale
    if len(shards) > 0:
        array = block_levels(rng, extent, shards, -0.22, 0.18) * array
    return jnp.clip(array, min=-reach, max=reach).astype(kind)


def setup_inputs(seed: int = 0) -> dict:
    streams_of = jax.random.split(jax.random.key(seed), 3)
    return {
        "momentum_shards": normal_values(streams_of[0], (SHARDS * CAP, N), (1.0 / (M ** 0.5 + N ** 0.5 + 6)), 0.078125, ((0, 32),)),
        "shard_starts": draw_shard_starts(jax.random.fold_in(streams_of[2], 71), 0),
    }


coef_one = 3.4445
coef_two = -4.775
coef_three = 2.0315

def reference(momentum_shards, shard_starts):
    row_ids = jnp.arange(M, dtype=jnp.int32)
    owner_shard = (lax.optimization_barrier(jnp.sum((shard_starts[None, :] <= row_ids[:, None]).astype(jnp.int32), axis=1)) - 1).astype(jnp.int32)
    source = (owner_shard * CAP + row_ids - jnp.take(shard_starts, owner_shard)).astype(jnp.int32)
    matrix = jnp.take(momentum_shards, source, axis=0)
    gram_matrix = jnp.dot(matrix, matrix.T, preferred_element_type=jnp.float32).astype(jnp.bfloat16)
    square = jnp.dot(gram_matrix, gram_matrix, preferred_element_type=jnp.float32)
    poly_matrix = (coef_two * gram_matrix.astype(jnp.float32) + coef_three * square).astype(jnp.bfloat16)
    mixed_part = jnp.dot(poly_matrix, matrix, preferred_element_type=jnp.float32)
    scaled = (math.sqrt(N) * (coef_one * matrix.astype(jnp.float32) + mixed_part)).astype(jnp.bfloat16)
    shard_ends = jnp.concatenate([shard_starts[1:], jnp.full((1,), M, jnp.int32)])
    slot_index = jnp.arange(SHARDS * CAP, dtype=jnp.int32)
    shard_ids = (slot_index // CAP).astype(jnp.int32)
    offset = (slot_index % CAP).astype(jnp.int32)
    shard_length = jnp.take(shard_ends - shard_starts, shard_ids)
    is_valid = offset < shard_length
    target = jnp.clip(jnp.take(shard_starts, shard_ids) + offset, 0, M - 1).astype(jnp.int32)
    picked_rows = jnp.take(scaled, target, axis=0)
    return jnp.where(is_valid[:, None], picked_rows, jnp.zeros_like(picked_rows))
```

```python
import math

import jax
import jax.numpy as jnp
import numpy as np
from jax import lax
from jax.experimental import pallas as pl
from jax.experimental.pallas import tpu as pltpu
from jax.sharding import PartitionSpec as P

M = 3584
N = 18432
TILE = 512
BLOCKS = M // TILE

coef_one = 3.4445
coef_two = -4.775
coef_three = 2.0315

PAIRS = [(i, j) for i in range(BLOCKS) for j in range(i, BLOCKS)]
PAIR_ROWS = np.array([i for i, _ in PAIRS], np.int32)
PAIR_COLS = np.array([j for _, j in PAIRS], np.int32)


def packing(shard_starts, row_block, col_count, shard_rows, window, first_row):
    shard_ends = jnp.concatenate([shard_starts[1:], jnp.full((1,), M, jnp.int32)])
    first_starts = lax.dynamic_slice_in_dim(shard_starts, row_block * col_count, col_count)
    last_ends = lax.dynamic_slice_in_dim(shard_ends, row_block * col_count, col_count)
    slot_index = jnp.arange(col_count * shard_rows, dtype=jnp.int32)
    member = slot_index // shard_rows
    offset = slot_index % shard_rows
    pick = member[:, None] == jnp.arange(col_count, dtype=jnp.int32)[None, :]
    shard_begin = jnp.sum(jnp.where(pick, first_starts[None, :], 0), axis=1)
    length = jnp.sum(jnp.where(pick, (last_ends - first_starts)[None, :], 0), axis=1)
    target = shard_begin - first_row + offset
    is_valid = offset < length
    window_rows = jnp.arange(window, dtype=jnp.int32)
    return ((window_rows[:, None] == target[None, :]) & is_valid[None, :]).astype(jnp.bfloat16)


def gram_kernel(rows_ref, cols_ref, left_ref, right_ref, out_ref):
    out_ref[...] = lax.dot_general(
        left_ref[...], right_ref[...], (((1,), (1,)), ((), ())), preferred_element_type=jnp.float32
    ).astype(jnp.bfloat16)


def gram_tiles(matrix):
    width = matrix.shape[1]
    count = len(PAIRS)
    return pl.pallas_call(
        gram_kernel,
        out_shape=jax.ShapeDtypeStruct((count * TILE, TILE), jnp.bfloat16),
        grid_spec=pltpu.PrefetchScalarGridSpec(
            num_scalar_prefetch=2,
            grid=(count,),
            in_specs=[
                pl.BlockSpec((TILE, width), lambda p, rows, cols: (rows[p], 0)),
                pl.BlockSpec((TILE, width), lambda p, rows, cols: (cols[p], 0)),
            ],
            out_specs=pl.BlockSpec((TILE, TILE), lambda p, rows, cols: (p, 0)),
        ),
        compiler_params=pltpu.CompilerParams(vmem_limit_bytes=32 * 1024 * 1024),
        cost_estimate=pl.CostEstimate(
            flops=2 * count * TILE * TILE * width,
            bytes_accessed=2 * count * TILE * (TILE + width),
            transcendentals=0,
        ),
    )(jnp.asarray(PAIR_ROWS), jnp.asarray(PAIR_COLS), matrix, matrix)


def apply_kernel(rows_ref, cols_ref, tile_ref, matrix_ref, out_ref, total, factor):
    turn = pl.program_id(0)
    pair = pl.program_id(1)
    i = rows_ref[pair]
    j = cols_ref[pair]
    here = pl.ds(pl.multiple_of(i * TILE, TILE), TILE)
    there = pl.ds(pl.multiple_of(j * TILE, TILE), TILE)

    @pl.when((turn == 0) & (pair == 0))
    def _():
        total[...] = jnp.zeros_like(total)
        factor[...] = matrix_ref[...]

    @pl.when((turn == 1) & (pair == 0))
    def _():
        @pl.loop(0, BLOCKS)
        def _(b):
            part = pl.ds(pl.multiple_of(b * TILE, TILE), TILE)
            product = total[part, :]
            factor[part, :] = (coef_three * product).astype(jnp.bfloat16)
            total[part, :] = coef_one * matrix_ref[part, :].astype(jnp.float32) + coef_two * product

    total[here, :] += jnp.dot(tile_ref[...], factor[there, :], preferred_element_type=jnp.float32)

    @pl.when(i != j)
    def _():
        total[there, :] += lax.dot_general(
            tile_ref[...], factor[here, :], (((0,), (0,)), ((), ())), preferred_element_type=jnp.float32
        )

    @pl.when((turn == 1) & (pair == pl.num_programs(1) - 1))
    def _():
        @pl.loop(0, BLOCKS)
        def _(b):
            part = pl.ds(pl.multiple_of(b * TILE, TILE), TILE)
            out_ref[part, :] = (math.sqrt(N) * total[part, :]).astype(jnp.bfloat16)


def apply_polynomial(tiles, matrix):
    rows, width = matrix.shape
    count = len(PAIRS)
    return pl.pallas_call(
        apply_kernel,
        out_shape=jax.ShapeDtypeStruct((rows, width), jnp.bfloat16),
        grid_spec=pltpu.PrefetchScalarGridSpec(
            num_scalar_prefetch=2,
            grid=(2, count),
            in_specs=[
                pl.BlockSpec((TILE, TILE), lambda t, p, rows, cols: (p, 0)),
                pl.BlockSpec((rows, width), lambda t, p, rows, cols: (0, 0)),
            ],
            out_specs=pl.BlockSpec((rows, width), lambda t, p, rows, cols: (0, 0)),
            scratch_shapes=[
                pltpu.VMEM((rows, width), jnp.float32),
                pltpu.VMEM((rows, width), jnp.bfloat16),
            ],
        ),
        compiler_params=pltpu.CompilerParams(vmem_limit_bytes=48 * 1024 * 1024),
        cost_estimate=pl.CostEstimate(
            flops=4 * rows * rows * width,
            bytes_accessed=4 * rows * width + 4 * count * TILE * TILE,
            transcendentals=0,
        ),
    )(jnp.asarray(PAIR_ROWS), jnp.asarray(PAIR_COLS), tiles, matrix)


def body(momentum_shards, shard_starts):
    col_count = lax.axis_size("col")
    row_count = lax.axis_size("row")
    shard_rows = momentum_shards.shape[0]
    mean_rows = M // (row_count * col_count)
    jitter = 4 * (mean_rows // 8)
    even = col_count * mean_rows
    window = even + 2 * jitter
    row_block = lax.axis_index("row")
    packer = packing(
        shard_starts, row_block, col_count, shard_rows, window, row_block * even - jitter
    )
    columns = lax.all_to_all(momentum_shards, "col", split_axis=1, concat_axis=0, tiled=True)
    local_tile = jnp.dot(packer, columns, preferred_element_type=jnp.float32).astype(jnp.bfloat16)
    windows = lax.all_to_all(local_tile, "row", split_axis=1, concat_axis=0, tiled=True)
    width = windows.shape[1]
    windows = windows.reshape(row_count, window, width)
    nothing = jnp.zeros((1, jitter, width), jnp.bfloat16)
    head = jnp.concatenate([nothing, windows[:-1, jitter + even :]], axis=0)
    tail = jnp.concatenate([windows[1:, :jitter], nothing], axis=0)
    middle = windows[:, jitter : jitter + even]
    matrix = jnp.concatenate(
        [
            middle[:, :jitter] + head,
            middle[:, jitter : even - jitter],
            middle[:, even - jitter :] + tail,
        ],
        axis=1,
    ).reshape(M, width)

    tiles = lax.psum(gram_tiles(matrix), ("row", "col"))
    update = apply_polynomial(tiles, matrix).reshape(row_count, even, width)

    before = jnp.concatenate([nothing, update[:-1, even - jitter :]], axis=0)
    after = jnp.concatenate([update[1:, :jitter], nothing], axis=0)
    spread = jnp.concatenate([before, update, after], axis=1).reshape(row_count * window, width)
    own_rows = lax.all_to_all(spread, "row", split_axis=0, concat_axis=1, tiled=True)
    back_rows = lax.dot_general(
        packer, own_rows, (((0,), (0,)), ((), ())), preferred_element_type=jnp.float32
    ).astype(jnp.bfloat16)
    return lax.all_to_all(back_rows, "col", split_axis=0, concat_axis=1, tiled=True)


def solution(mesh):
    in_specs = (P(("row", "col"), None), P())
    out_specs = P(("row", "col"), None)
    return jax.shard_map(body, mesh=mesh, in_specs=in_specs, out_specs=out_specs, check_vma=False)
```

```python
import math

import jax
import jax.numpy as jnp
import numpy as np
from jax import lax
from jax.experimental import pallas as pl
from jax.experimental.pallas import tpu as pltpu
from jax.sharding import PartitionSpec as P

M = 3584
N = 18432
TILE = 512
BLOCKS = M // TILE

coef_one = 3.4445
coef_two = -4.775
coef_three = 2.0315

PAIRS = [(i, j) for i in range(BLOCKS) for j in range(i, BLOCKS)]
PAIR_ROWS = np.array([i for i, _ in PAIRS], np.int32)
PAIR_COLS = np.array([j for _, j in PAIRS], np.int32)


def packing(shard_starts, row_block, col_count, shard_rows, window, first_row):
    shard_ends = jnp.concatenate([shard_starts[1:], jnp.full((1,), M, jnp.int32)])
    first_starts = lax.dynamic_slice_in_dim(shard_starts, row_block * col_count, col_count)
    last_ends = lax.dynamic_slice_in_dim(shard_ends, row_block * col_count, col_count)
    slot_index = jnp.arange(col_count * shard_rows, dtype=jnp.int32)
    member = slot_index // shard_rows
    offset = slot_index % shard_rows
    pick = member[:, None] == jnp.arange(col_count, dtype=jnp.int32)[None, :]
    shard_begin = jnp.sum(jnp.where(pick, first_starts[None, :], 0), axis=1)
    length = jnp.sum(jnp.where(pick, (last_ends - first_starts)[None, :], 0), axis=1)
    target = shard_begin - first_row + offset
    is_valid = offset < length
    window_rows = jnp.arange(window, dtype=jnp.int32)
    return ((window_rows[:, None] == target[None, :]) & is_valid[None, :]).astype(jnp.bfloat16)


def gram_kernel(rows_ref, cols_ref, left_ref, right_ref, out_ref):
    out_ref[...] = lax.dot_general(
        left_ref[...], right_ref[...], (((1,), (1,)), ((), ())), preferred_element_type=jnp.float32
    ).astype(jnp.bfloat16)


def gram_tiles(matrix):
    width = matrix.shape[1]
    count = len(PAIRS)
    return pl.pallas_call(
        gram_kernel,
        out_shape=jax.ShapeDtypeStruct((count * TILE, TILE), jnp.bfloat16),
        grid_spec=pltpu.PrefetchScalarGridSpec(
            num_scalar_prefetch=2,
            grid=(count,),
            in_specs=[
                pl.BlockSpec((TILE, width), lambda p, rows, cols: (rows[p], 0)),
                pl.BlockSpec((TILE, width), lambda p, rows, cols: (cols[p], 0)),
            ],
            out_specs=pl.BlockSpec((TILE, TILE), lambda p, rows, cols: (p, 0)),
        ),
        compiler_params=pltpu.CompilerParams(vmem_limit_bytes=32 * 1024 * 1024),
        cost_estimate=pl.CostEstimate(
            flops=2 * count * TILE * TILE * width,
            bytes_accessed=2 * count * TILE * (TILE + width),
            transcendentals=0,
        ),
    )(jnp.asarray(PAIR_ROWS), jnp.asarray(PAIR_COLS), matrix, matrix)


def apply_kernel(rows_ref, cols_ref, tile_ref, matrix_ref, out_ref, total, factor):
    turn = pl.program_id(0)
    pair = pl.program_id(1)
    i = rows_ref[pair]
    j = cols_ref[pair]
    here = pl.ds(pl.multiple_of(i * TILE, TILE), TILE)
    there = pl.ds(pl.multiple_of(j * TILE, TILE), TILE)

    @pl.when((turn == 0) & (pair == 0))
    def _():
        total[...] = jnp.zeros_like(total)
        factor[...] = matrix_ref[...]

    @pl.when((turn == 1) & (pair == 0))
    def _():
        @pl.loop(0, BLOCKS)
        def _(b):
            part = pl.ds(pl.multiple_of(b * TILE, TILE), TILE)
            product = total[part, :]
            factor[part, :] = (coef_three * product).astype(jnp.bfloat16)
            total[part, :] = coef_one * matrix_ref[part, :].astype(jnp.float32) + coef_two * product

    total[here, :] += jnp.dot(tile_ref[...], factor[there, :], preferred_element_type=jnp.float32)

    @pl.when(i != j)
    def _():
        total[there, :] += lax.dot_general(
            tile_ref[...], factor[here, :], (((0,), (0,)), ((), ())), preferred_element_type=jnp.float32
        )

    @pl.when((turn == 1) & (pair == pl.num_programs(1) - 1))
    def _():
        @pl.loop(0, BLOCKS)
        def _(b):
            part = pl.ds(pl.multiple_of(b * TILE, TILE), TILE)
            out_ref[part, :] = (math.sqrt(N) * total[part, :]).astype(jnp.bfloat16)


def apply_polynomial(tiles, matrix):
    rows, width = matrix.shape
    count = len(PAIRS)
    return pl.pallas_call(
        apply_kernel,
        out_shape=jax.ShapeDtypeStruct((rows, width), jnp.bfloat16),
        grid_spec=pltpu.PrefetchScalarGridSpec(
            num_scalar_prefetch=2,
            grid=(2, count),
            in_specs=[
                pl.BlockSpec((TILE, TILE), lambda t, p, rows, cols: (p, 0)),
                pl.BlockSpec((rows, width), lambda t, p, rows, cols: (0, 0)),
            ],
            out_specs=pl.BlockSpec((rows, width), lambda t, p, rows, cols: (0, 0)),
            scratch_shapes=[
                pltpu.VMEM((rows, width), jnp.float32),
                pltpu.VMEM((rows, width), jnp.bfloat16),
            ],
        ),
        compiler_params=pltpu.CompilerParams(vmem_limit_bytes=48 * 1024 * 1024),
        cost_estimate=pl.CostEstimate(
            flops=4 * rows * rows * width,
            bytes_accessed=4 * rows * width + 4 * count * TILE * TILE,
            transcendentals=0,
        ),
    )(jnp.asarray(PAIR_ROWS), jnp.asarray(PAIR_COLS), tiles, matrix)


def plain_body(momentum_shards, shard_starts):
    col_count = lax.axis_size("col")
    row_count = lax.axis_size("row")
    shard_rows = momentum_shards.shape[0]
    mean_rows = M // (row_count * col_count)
    jitter = 4 * (mean_rows // 8)
    even = col_count * mean_rows
    window = even + 2 * jitter
    row_block = lax.axis_index("row")
    packer = packing(
        shard_starts, row_block, col_count, shard_rows, window, row_block * even - jitter
    )
    columns = lax.all_to_all(momentum_shards, "col", split_axis=1, concat_axis=0, tiled=True)
    local_tile = jnp.dot(packer, columns, preferred_element_type=jnp.float32).astype(jnp.bfloat16)
    windows = lax.all_to_all(local_tile, "row", split_axis=1, concat_axis=0, tiled=True)
    width = windows.shape[1]
    windows = windows.reshape(row_count, window, width)
    nothing = jnp.zeros((1, jitter, width), jnp.bfloat16)
    head = jnp.concatenate([nothing, windows[:-1, jitter + even :]], axis=0)
    tail = jnp.concatenate([windows[1:, :jitter], nothing], axis=0)
    middle = windows[:, jitter : jitter + even]
    matrix = jnp.concatenate(
        [
            middle[:, :jitter] + head,
            middle[:, jitter : even - jitter],
            middle[:, even - jitter :] + tail,
        ],
        axis=1,
    ).reshape(M, width)

    tiles = lax.psum(gram_tiles(matrix), ("row", "col"))
    update = apply_polynomial(tiles, matrix).reshape(row_count, even, width)

    before = jnp.concatenate([nothing, update[:-1, even - jitter :]], axis=0)
    after = jnp.concatenate([update[1:, :jitter], nothing], axis=0)
    spread = jnp.concatenate([before, update, after], axis=1).reshape(row_count * window, width)
    own_rows = lax.all_to_all(spread, "row", split_axis=0, concat_axis=1, tiled=True)
    back_rows = lax.dot_general(
        packer, own_rows, (((0,), (0,)), ((), ())), preferred_element_type=jnp.float32
    ).astype(jnp.bfloat16)
    return lax.all_to_all(back_rows, "col", split_axis=0, concat_axis=1, tiled=True)


CHUNK = 256
LAST = 128
VMEM_LIMIT = 56 * 1024 * 1024


def swap(value, axis, size, distance):
    return lax.ppermute(value, axis, perm=[(i, i ^ distance) for i in range(size)])


def pack_kernel(step, col_count, meta_ref, *refs):
    pieces, outs, choose = refs[:col_count], refs[col_count:-1], refs[-1]
    turn = pl.program_id(0)
    _, window, slots = choose.shape

    @pl.when(turn == 0)
    def _():
        rows = lax.broadcasted_iota(jnp.int32, (window, slots), 0)
        columns = lax.broadcasted_iota(jnp.int32, (window, slots), 1)
        for k in range(col_count):
            hit = (rows == columns + meta_ref[2 + k]) & (columns < meta_ref[2 + col_count + k])
            choose[k] = jnp.where(hit, 1.0, 0.0).astype(jnp.bfloat16)

    total = jnp.dot(choose[0], pieces[0][...], preferred_element_type=jnp.float32)
    for k in range(1, col_count):
        total += jnp.dot(choose[k], pieces[k][...], preferred_element_type=jnp.float32)
    for q, out in enumerate(outs):

        @pl.when(turn == q)
        def _():
            out[...] = total.astype(jnp.bfloat16)


def pack(meta, momentum, received, base, width, step, count, window):
    slots = momentum.shape[0]
    col_count = len(received) + 1
    first = base // width
    return pl.pallas_call(
        lambda *refs: pack_kernel(step, col_count, *refs),
        out_shape=[jax.ShapeDtypeStruct((window, width), jnp.bfloat16)] * count,
        grid_spec=pltpu.PrefetchScalarGridSpec(
            num_scalar_prefetch=1,
            grid=(count,),
            in_specs=[
                pl.BlockSpec(
                    (slots, width),
                    lambda q, meta: (0, first + meta[1] * count + ((meta[0] // step) ^ q)),
                )
            ]
            + [pl.BlockSpec((slots, width), lambda q, meta: (0, (meta[0] // step) ^ q))]
            * (col_count - 1),
            out_specs=[pl.BlockSpec((window, width), lambda q, meta: (0, 0))] * count,
            scratch_shapes=[pltpu.VMEM((col_count, window, slots), jnp.bfloat16)],
        ),
        compiler_params=pltpu.CompilerParams(vmem_limit_bytes=VMEM_LIMIT),
        cost_estimate=pl.CostEstimate(
            flops=2 * window * slots * col_count * width * count,
            bytes_accessed=2 * count * width * (slots * col_count + window),
            transcendentals=0,
        ),
    )(meta, momentum, *received)


def unpack_kernel(col_count, meta_ref, *refs):
    pieces, outs, choose = refs[: -1 - col_count], refs[-1 - col_count : -1], refs[-1]
    turn = pl.program_id(0)
    _, slots, window = choose.shape

    @pl.when(turn == 0)
    def _():
        rows = lax.broadcasted_iota(jnp.int32, (slots, window), 1)
        columns = lax.broadcasted_iota(jnp.int32, (slots, window), 0)
        for k in range(col_count):
            hit = (rows == columns + meta_ref[2 + k]) & (columns < meta_ref[2 + col_count + k])
            choose[k] = jnp.where(hit, 1.0, 0.0).astype(jnp.bfloat16)

    for q, piece in enumerate(pieces):

        @pl.when(turn == q)
        def _():
            for k in range(col_count):
                outs[k][...] = jnp.dot(
                    choose[k], piece[...], preferred_element_type=jnp.float32
                ).astype(jnp.bfloat16)


def unpack(meta, pieces, col_count, slots, step):
    window, width = pieces[0].shape
    count = len(pieces)
    return pl.pallas_call(
        lambda *refs: unpack_kernel(col_count, *refs),
        out_shape=[jax.ShapeDtypeStruct((slots, count * width), jnp.bfloat16)] * col_count,
        grid_spec=pltpu.PrefetchScalarGridSpec(
            num_scalar_prefetch=1,
            grid=(count,),
            in_specs=[pl.BlockSpec((window, width), lambda q, meta: (0, 0))] * count,
            out_specs=[pl.BlockSpec((slots, width), lambda q, meta: (0, (meta[0] // step) ^ q))]
            * col_count,
            scratch_shapes=[pltpu.VMEM((col_count, slots, window), jnp.bfloat16)],
        ),
        compiler_params=pltpu.CompilerParams(vmem_limit_bytes=VMEM_LIMIT),
        cost_estimate=pl.CostEstimate(
            flops=2 * window * slots * col_count * width * count,
            bytes_accessed=2 * count * width * (slots * col_count + window),
            transcendentals=0,
        ),
    )(meta, *pieces)


def merge_kernel(even, jitter, distances, meta_ref, *refs):
    pieces, out_ref, total = refs[:-2], refs[-2], refs[-1]
    window = pieces[0].shape[0]
    total[...] = jnp.zeros_like(total)
    for distance, piece in zip(distances, pieces):
        place = pl.ds(pl.multiple_of((meta_ref[0] ^ distance) * even, 8), window)
        total[place, :] += piece[...].astype(jnp.float32)

    @pl.loop(0, BLOCKS)
    def _(b):
        source = pl.ds(pl.multiple_of(b * TILE + jitter, 8), TILE)
        out_ref[pl.ds(pl.multiple_of(b * TILE, TILE), TILE), :] = total[source, :].astype(
            jnp.bfloat16
        )


def merge(meta, pieces, distances, even, jitter):
    width = pieces[0].shape[1]
    whole = pl.BlockSpec(memory_space=pltpu.VMEM)
    return pl.pallas_call(
        lambda *refs: merge_kernel(even, jitter, distances, *refs),
        out_shape=jax.ShapeDtypeStruct((M, width), jnp.bfloat16),
        in_specs=[pl.BlockSpec(memory_space=pltpu.SMEM)] + [whole] * len(pieces),
        out_specs=whole,
        scratch_shapes=[pltpu.VMEM((M + 2 * jitter, width), jnp.float32)],
        compiler_params=pltpu.CompilerParams(vmem_limit_bytes=VMEM_LIMIT),
        cost_estimate=pl.CostEstimate(
            flops=2 * M * width, bytes_accessed=5 * M * width, transcendentals=0
        ),
    )(meta, *pieces)


def chunk_gram_kernel(rows_ref, cols_ref, meta_ref, *refs):
    out_ref = refs[-1]
    lefts, rights = refs[:-1:2], refs[1:-1:2]
    dims = (((1,), (1,)), ((), ()))
    mine = (pl.program_id(0) + meta_ref[0]) % 2 == 0

    def product(count):
        total = lax.dot_general(
            lefts[0][...], rights[0][...], dims, preferred_element_type=jnp.float32
        )
        for c in range(1, count):
            total += lax.dot_general(
                lefts[c][...], rights[c][...], dims, preferred_element_type=jnp.float32
            )
        out_ref[...] = total.astype(jnp.bfloat16)

    @pl.when(mine)
    def _():
        product(len(lefts))

    @pl.when(jnp.logical_not(mine))
    def _():
        product(len(lefts) - 1)


def chunk_gram(meta, chunks):
    count = len(PAIRS)
    in_specs = []
    operands = []
    width = sum(x.shape[1] for x in chunks)
    for x in chunks:
        in_specs.append(pl.BlockSpec((TILE, x.shape[1]), lambda p, rows, cols, meta: (rows[p], 0)))
        in_specs.append(pl.BlockSpec((TILE, x.shape[1]), lambda p, rows, cols, meta: (cols[p], 0)))
        operands += [x, x]
    return pl.pallas_call(
        chunk_gram_kernel,
        out_shape=jax.ShapeDtypeStruct((count * TILE, TILE), jnp.bfloat16),
        grid_spec=pltpu.PrefetchScalarGridSpec(
            num_scalar_prefetch=3,
            grid=(count,),
            in_specs=in_specs,
            out_specs=pl.BlockSpec((TILE, TILE), lambda p, rows, cols, meta: (p, 0)),
        ),
        compiler_params=pltpu.CompilerParams(vmem_limit_bytes=VMEM_LIMIT),
        cost_estimate=pl.CostEstimate(
            flops=2 * count * TILE * TILE * width,
            bytes_accessed=2 * count * TILE * (TILE + width),
            transcendentals=0,
        ),
    )(jnp.asarray(PAIR_ROWS), jnp.asarray(PAIR_COLS), meta, *operands)


def windows_kernel(even, jitter, sends, rows_ref, cols_ref, meta_ref, tile_ref, *refs):
    chunks = len(sends)
    outs_count = sum(len(s) for s in sends)
    matrices = refs[:chunks]
    outs = refs[chunks : chunks + outs_count]
    gram = refs[chunks + outs_count]
    totals = refs[chunks + outs_count + 1 : 2 * chunks + outs_count + 1]
    factors = refs[2 * chunks + outs_count + 1 :]
    turn = pl.program_id(0)
    count = len(PAIRS)

    @pl.when(turn == 0)
    def _():
        for total in totals:
            edge = jnp.zeros((jitter, total.shape[1]), jnp.float32)
            total[pl.ds(0, jitter), :] = edge
            total[pl.ds(M + jitter, jitter), :] = edge

    @pl.when(turn < count)
    def _():
        i = rows_ref[jnp.minimum(turn, count - 1)]
        j = cols_ref[jnp.minimum(turn, count - 1)]
        gram[i, :, pl.ds(pl.multiple_of(j * TILE, TILE), TILE)] = tile_ref[...]

        @pl.when(i != j)
        def _():
            gram[j, :, pl.ds(pl.multiple_of(i * TILE, TILE), TILE)] = tile_ref[...].T

    @pl.when((turn >= count) & (turn < count + BLOCKS))
    def _():
        b = turn - count
        part = pl.ds(pl.multiple_of(b * TILE, TILE), TILE)
        place = pl.ds(pl.multiple_of(b * TILE + jitter, 8), TILE)
        for matrix, total, factor in zip(matrices, totals, factors):
            product = jnp.dot(gram[b], matrix[...], preferred_element_type=jnp.float32)
            factor[part, :] = (coef_three * product).astype(jnp.bfloat16)
            total[place, :] = (
                coef_one * matrix[part, :].astype(jnp.float32) + coef_two * product
            )

    @pl.when(turn >= count + BLOCKS)
    def _():
        b = turn - count - BLOCKS
        place = pl.ds(pl.multiple_of(b * TILE + jitter, 8), TILE)
        for total, factor in zip(totals, factors):
            total[place, :] = math.sqrt(N) * (
                total[place, :] + jnp.dot(gram[b], factor[...], preferred_element_type=jnp.float32)
            )

    @pl.when(turn == count + 2 * BLOCKS - 1)
    def _():
        number = 0
        for total, send in zip(totals, sends):
            for distance in send:
                window = outs[number].shape[0]
                place = pl.ds(pl.multiple_of((meta_ref[0] ^ distance) * even, 8), window)
                outs[number][...] = total[place, :].astype(jnp.bfloat16)
                number += 1


def apply_windows(meta, tiles, matrices, sends, even, jitter):
    count = len(PAIRS)
    widths = [x.shape[1] for x in matrices]
    shapes = [
        (even + 2 * jitter, width) for width, send in zip(widths, sends) for _ in send
    ]
    whole = lambda t, rows, cols, meta: (0, 0)
    outs = pl.pallas_call(
        lambda *refs: windows_kernel(even, jitter, sends, *refs),
        out_shape=[jax.ShapeDtypeStruct(shape, jnp.bfloat16) for shape in shapes],
        grid_spec=pltpu.PrefetchScalarGridSpec(
            num_scalar_prefetch=3,
            grid=(count + 2 * BLOCKS,),
            in_specs=[
                pl.BlockSpec(
                    (TILE, TILE), lambda t, rows, cols, meta: (jnp.minimum(t, count - 1), 0)
                )
            ]
            + [pl.BlockSpec((M, width), whole) for width in widths],
            out_specs=[pl.BlockSpec(shape, whole) for shape in shapes],
            scratch_shapes=[pltpu.VMEM((BLOCKS, TILE, M), jnp.bfloat16)]
            + [pltpu.VMEM((M + 2 * jitter, width), jnp.float32) for width in widths]
            + [pltpu.VMEM((M, width), jnp.bfloat16) for width in widths],
        ),
        compiler_params=pltpu.CompilerParams(vmem_limit_bytes=VMEM_LIMIT),
        cost_estimate=pl.CostEstimate(
            flops=4 * M * M * sum(widths),
            bytes_accessed=4 * M * sum(widths) + 2 * count * TILE * TILE,
            transcendentals=0,
        ),
    )(jnp.asarray(PAIR_ROWS), jnp.asarray(PAIR_COLS), meta, tiles, *matrices)
    result = []
    for send in sends:
        result.append(outs[: len(send)])
        outs = outs[len(send) :]
    return result


def reduce_tiles(tiles):
    return lax.psum(tiles, ("row", "col"))


def chunk_body(momentum_shards, shard_starts):
    col_count = lax.axis_size("col")
    row_count = lax.axis_size("row")
    pair_count = row_count // 2
    slots = momentum_shards.shape[0]
    mean_rows = M // (row_count * col_count)
    jitter = 4 * (mean_rows // 8)
    even = col_count * mean_rows
    window = even + 2 * jitter
    row = lax.axis_index("row").astype(jnp.int32)
    col = lax.axis_index("col").astype(jnp.int32)
    shard_ends = jnp.concatenate([shard_starts[1:], jnp.full((1,), M, jnp.int32)])
    members = row * col_count + (col ^ jnp.arange(col_count, dtype=jnp.int32))
    begins = shard_starts[members]
    meta = jnp.concatenate(
        [row[None], col[None], begins - (row * even - jitter), shard_ends[members] - begins]
    )

    wide = row_count * col_count * CHUNK
    number = (N // (row_count * col_count)) // CHUNK
    plan = [(c * wide, CHUNK, 1, row_count) for c in range(number)]
    plan.append((number * wide, LAST, 2, pair_count))

    matrices = []
    for base, width, step, count in plan:
        span = count * width
        received = [
            swap(
                lax.dynamic_slice_in_dim(momentum_shards, base + (col ^ k) * span, span, axis=1),
                "col",
                col_count,
                k,
            )
            for k in range(1, col_count)
        ]
        pieces = pack(meta, momentum_shards, received, base, width, step, count, window)
        landed = [pieces[0]] + [
            swap(pieces[q], "row", row_count, q * step) for q in range(1, count)
        ]
        distances = [q * step for q in range(count)]
        if step == 2:
            landed += [swap(piece, "row", row_count, 1) for piece in landed]
            distances += [d ^ 1 for d in distances]
        matrices.append(merge(meta, landed, distances, even, jitter))

    tiles = reduce_tiles(chunk_gram(meta, matrices))

    sends = [[q * step for q in range(count)] for _, _, step, count in plan]
    results = []
    for group in [[c] for c in range(number - 1)] + [[number - 1, number]]:
        results += apply_windows(
            meta, tiles, [matrices[c] for c in group], [sends[c] for c in group], even, jitter
        )

    out = jnp.zeros(momentum_shards.shape, jnp.bfloat16)
    for (base, width, step, count), pieces in zip(plan, results):
        span = count * width
        landed = [pieces[0]] + [
            swap(pieces[q], "row", row_count, q * step) for q in range(1, count)
        ]
        backs = unpack(meta, landed, col_count, slots, step)
        for k in range(col_count):
            back = backs[0] if k == 0 else swap(backs[k], "col", col_count, k)
            out = lax.dynamic_update_slice_in_dim(out, back, base + (col ^ k) * span, axis=1)
    return out


def body(momentum_shards, shard_starts):
    devices = lax.axis_size("col") * lax.axis_size("row")
    chunks = (N // devices) % CHUNK == LAST // 2 and N // devices > CHUNK
    powers = all(lax.axis_size(a) & (lax.axis_size(a) - 1) == 0 for a in ("row", "col"))
    jitter = 4 * (M // devices // 8)
    if chunks and powers and jitter % 8 == 0:
        return chunk_body(momentum_shards, shard_starts)
    return plain_body(momentum_shards, shard_starts)


def solution(mesh):
    in_specs = (P(("row", "col"), None), P())
    out_specs = P(("row", "col"), None)
    return jax.shard_map(body, mesh=mesh, in_specs=in_specs, out_specs=out_specs, check_vma=False)
```

```python
import math

import jax
import jax.numpy as jnp
import numpy as np
from jax import lax
from jax.experimental import pallas as pl
from jax.experimental.pallas import tpu as pltpu
from jax.sharding import PartitionSpec as P

M = 3584
N = 18432
TILE = 512
BLOCKS = M // TILE

coef_one = 3.4445
coef_two = -4.775
coef_three = 2.0315

PAIRS = [(i, j) for i in range(BLOCKS) for j in range(i, BLOCKS)]
PAIR_ROWS = np.array([i for i, _ in PAIRS], np.int32)
PAIR_COLS = np.array([j for _, j in PAIRS], np.int32)


def packing(shard_starts, row_block, col_count, shard_rows, window, first_row):
    shard_ends = jnp.concatenate([shard_starts[1:], jnp.full((1,), M, jnp.int32)])
    first_starts = lax.dynamic_slice_in_dim(shard_starts, row_block * col_count, col_count)
    last_ends = lax.dynamic_slice_in_dim(shard_ends, row_block * col_count, col_count)
    slot_index = jnp.arange(col_count * shard_rows, dtype=jnp.int32)
    member = slot_index // shard_rows
    offset = slot_index % shard_rows
    pick = member[:, None] == jnp.arange(col_count, dtype=jnp.int32)[None, :]
    shard_begin = jnp.sum(jnp.where(pick, first_starts[None, :], 0), axis=1)
    length = jnp.sum(jnp.where(pick, (last_ends - first_starts)[None, :], 0), axis=1)
    target = shard_begin - first_row + offset
    is_valid = offset < length
    window_rows = jnp.arange(window, dtype=jnp.int32)
    return ((window_rows[:, None] == target[None, :]) & is_valid[None, :]).astype(jnp.bfloat16)


def gram_kernel(rows_ref, cols_ref, left_ref, right_ref, out_ref):
    out_ref[...] = lax.dot_general(
        left_ref[...], right_ref[...], (((1,), (1,)), ((), ())), preferred_element_type=jnp.float32
    ).astype(jnp.bfloat16)


def gram_tiles(matrix):
    width = matrix.shape[1]
    count = len(PAIRS)
    return pl.pallas_call(
        gram_kernel,
        out_shape=jax.ShapeDtypeStruct((count * TILE, TILE), jnp.bfloat16),
        grid_spec=pltpu.PrefetchScalarGridSpec(
            num_scalar_prefetch=2,
            grid=(count,),
            in_specs=[
                pl.BlockSpec((TILE, width), lambda p, rows, cols: (rows[p], 0)),
                pl.BlockSpec((TILE, width), lambda p, rows, cols: (cols[p], 0)),
            ],
            out_specs=pl.BlockSpec((TILE, TILE), lambda p, rows, cols: (p, 0)),
        ),
        compiler_params=pltpu.CompilerParams(vmem_limit_bytes=32 * 1024 * 1024),
        cost_estimate=pl.CostEstimate(
            flops=2 * count * TILE * TILE * width,
            bytes_accessed=2 * count * TILE * (TILE + width),
            transcendentals=0,
        ),
    )(jnp.asarray(PAIR_ROWS), jnp.asarray(PAIR_COLS), matrix, matrix)


def apply_kernel(rows_ref, cols_ref, tile_ref, matrix_ref, out_ref, total, factor):
    turn = pl.program_id(0)
    pair = pl.program_id(1)
    i = rows_ref[pair]
    j = cols_ref[pair]
    here = pl.ds(pl.multiple_of(i * TILE, TILE), TILE)
    there = pl.ds(pl.multiple_of(j * TILE, TILE), TILE)

    @pl.when((turn == 0) & (pair == 0))
    def _():
        total[...] = jnp.zeros_like(total)
        factor[...] = matrix_ref[...]

    @pl.when((turn == 1) & (pair == 0))
    def _():
        @pl.loop(0, BLOCKS)
        def _(b):
            part = pl.ds(pl.multiple_of(b * TILE, TILE), TILE)
            product = total[part, :]
            factor[part, :] = (coef_three * product).astype(jnp.bfloat16)
            total[part, :] = coef_one * matrix_ref[part, :].astype(jnp.float32) + coef_two * product

    total[here, :] += jnp.dot(tile_ref[...], factor[there, :], preferred_element_type=jnp.float32)

    @pl.when(i != j)
    def _():
        total[there, :] += lax.dot_general(
            tile_ref[...], factor[here, :], (((0,), (0,)), ((), ())), preferred_element_type=jnp.float32
        )

    @pl.when((turn == 1) & (pair == pl.num_programs(1) - 1))
    def _():
        @pl.loop(0, BLOCKS)
        def _(b):
            part = pl.ds(pl.multiple_of(b * TILE, TILE), TILE)
            out_ref[part, :] = (math.sqrt(N) * total[part, :]).astype(jnp.bfloat16)


def apply_polynomial(tiles, matrix):
    rows, width = matrix.shape
    count = len(PAIRS)
    return pl.pallas_call(
        apply_kernel,
        out_shape=jax.ShapeDtypeStruct((rows, width), jnp.bfloat16),
        grid_spec=pltpu.PrefetchScalarGridSpec(
            num_scalar_prefetch=2,
            grid=(2, count),
            in_specs=[
                pl.BlockSpec((TILE, TILE), lambda t, p, rows, cols: (p, 0)),
                pl.BlockSpec((rows, width), lambda t, p, rows, cols: (0, 0)),
            ],
            out_specs=pl.BlockSpec((rows, width), lambda t, p, rows, cols: (0, 0)),
            scratch_shapes=[
                pltpu.VMEM((rows, width), jnp.float32),
                pltpu.VMEM((rows, width), jnp.bfloat16),
            ],
        ),
        compiler_params=pltpu.CompilerParams(vmem_limit_bytes=48 * 1024 * 1024),
        cost_estimate=pl.CostEstimate(
            flops=4 * rows * rows * width,
            bytes_accessed=4 * rows * width + 4 * count * TILE * TILE,
            transcendentals=0,
        ),
    )(jnp.asarray(PAIR_ROWS), jnp.asarray(PAIR_COLS), tiles, matrix)


def plain_body(momentum_shards, shard_starts):
    col_count = lax.axis_size("col")
    row_count = lax.axis_size("row")
    shard_rows = momentum_shards.shape[0]
    mean_rows = M // (row_count * col_count)
    jitter = 4 * (mean_rows // 8)
    even = col_count * mean_rows
    window = even + 2 * jitter
    row_block = lax.axis_index("row")
    packer = packing(
        shard_starts, row_block, col_count, shard_rows, window, row_block * even - jitter
    )
    columns = lax.all_to_all(momentum_shards, "col", split_axis=1, concat_axis=0, tiled=True)
    local_tile = jnp.dot(packer, columns, preferred_element_type=jnp.float32).astype(jnp.bfloat16)
    windows = lax.all_to_all(local_tile, "row", split_axis=1, concat_axis=0, tiled=True)
    width = windows.shape[1]
    windows = windows.reshape(row_count, window, width)
    nothing = jnp.zeros((1, jitter, width), jnp.bfloat16)
    head = jnp.concatenate([nothing, windows[:-1, jitter + even :]], axis=0)
    tail = jnp.concatenate([windows[1:, :jitter], nothing], axis=0)
    middle = windows[:, jitter : jitter + even]
    matrix = jnp.concatenate(
        [
            middle[:, :jitter] + head,
            middle[:, jitter : even - jitter],
            middle[:, even - jitter :] + tail,
        ],
        axis=1,
    ).reshape(M, width)

    tiles = lax.psum(gram_tiles(matrix), ("row", "col"))
    update = apply_polynomial(tiles, matrix).reshape(row_count, even, width)

    before = jnp.concatenate([nothing, update[:-1, even - jitter :]], axis=0)
    after = jnp.concatenate([update[1:, :jitter], nothing], axis=0)
    spread = jnp.concatenate([before, update, after], axis=1).reshape(row_count * window, width)
    own_rows = lax.all_to_all(spread, "row", split_axis=0, concat_axis=1, tiled=True)
    back_rows = lax.dot_general(
        packer, own_rows, (((0,), (0,)), ((), ())), preferred_element_type=jnp.float32
    ).astype(jnp.bfloat16)
    return lax.all_to_all(back_rows, "col", split_axis=0, concat_axis=1, tiled=True)


CHUNK = 256
LAST = 128
VMEM_LIMIT = 56 * 1024 * 1024


def swap(value, axis, size, distance):
    return lax.ppermute(value, axis, perm=[(i, i ^ distance) for i in range(size)])


def pack_kernel(step, col_count, meta_ref, *refs):
    pieces, outs, choose = refs[:col_count], refs[col_count:-1], refs[-1]
    turn = pl.program_id(0)
    _, window, slots = choose.shape

    @pl.when(turn == 0)
    def _():
        rows = lax.broadcasted_iota(jnp.int32, (window, slots), 0)
        columns = lax.broadcasted_iota(jnp.int32, (window, slots), 1)
        for k in range(col_count):
            hit = (rows == columns + meta_ref[2 + k]) & (columns < meta_ref[2 + col_count + k])
            choose[k] = jnp.where(hit, 1.0, 0.0).astype(jnp.bfloat16)

    total = jnp.dot(choose[0], pieces[0][...], preferred_element_type=jnp.float32)
    for k in range(1, col_count):
        total += jnp.dot(choose[k], pieces[k][...], preferred_element_type=jnp.float32)
    for q, out in enumerate(outs):

        @pl.when(turn == q)
        def _():
            out[...] = total.astype(jnp.bfloat16)


def pack(meta, momentum, received, base, width, step, count, window):
    slots = momentum.shape[0]
    col_count = len(received) + 1
    first = base // width
    return pl.pallas_call(
        lambda *refs: pack_kernel(step, col_count, *refs),
        out_shape=[jax.ShapeDtypeStruct((window, width), jnp.bfloat16)] * count,
        grid_spec=pltpu.PrefetchScalarGridSpec(
            num_scalar_prefetch=1,
            grid=(count,),
            in_specs=[
                pl.BlockSpec(
                    (slots, width),
                    lambda q, meta: (0, first + meta[1] * count + ((meta[0] // step) ^ q)),
                )
            ]
            + [pl.BlockSpec((slots, width), lambda q, meta: (0, (meta[0] // step) ^ q))]
            * (col_count - 1),
            out_specs=[pl.BlockSpec((window, width), lambda q, meta: (0, 0))] * count,
            scratch_shapes=[pltpu.VMEM((col_count, window, slots), jnp.bfloat16)],
        ),
        compiler_params=pltpu.CompilerParams(vmem_limit_bytes=VMEM_LIMIT),
        cost_estimate=pl.CostEstimate(
            flops=2 * window * slots * col_count * width * count,
            bytes_accessed=2 * count * width * (slots * col_count + window),
            transcendentals=0,
        ),
    )(meta, momentum, *received)


def pack_pair_kernel(col_count, meta_ref, *refs):
    pieces, keep, give, choose = refs[:col_count], refs[col_count], refs[col_count + 1], refs[-1]
    other = pl.program_id(0) == 0
    _, window, slots = choose.shape

    @pl.when(other & (pl.program_id(1) == 0))
    def _():
        fill_choose(meta_ref, choose, 0)

    total = jnp.dot(choose[0], pieces[0][...], preferred_element_type=jnp.float32)
    for k in range(1, col_count):
        total += jnp.dot(choose[k], pieces[k][...], preferred_element_type=jnp.float32)

    @pl.when(other)
    def _():
        give[...] = total.astype(jnp.bfloat16)

    @pl.when(jnp.logical_not(other))
    def _():
        keep[...] = total.astype(jnp.bfloat16)


def fill_choose(meta_ref, choose, slot_axis):
    col_count = choose.shape[0]
    shape = choose.shape[1:]
    rows = lax.broadcasted_iota(jnp.int32, shape, slot_axis)
    slots = lax.broadcasted_iota(jnp.int32, shape, 1 - slot_axis)
    for k in range(col_count):
        hit = (rows == slots + meta_ref[2 + k]) & (slots < meta_ref[2 + col_count + k])
        choose[k] = jnp.where(hit, 1.0, 0.0).astype(jnp.bfloat16)


def pack_pair(meta, momentum, received, base, width, row_count, window):
    slots = momentum.shape[0]
    col_count = len(received) + 1
    pairs = row_count // 2
    first = base // width
    block = lambda e, q, meta: meta[0] ^ (2 * q + 1 - e)
    shape = jax.ShapeDtypeStruct((pairs * window, width), jnp.bfloat16)
    return pl.pallas_call(
        lambda *refs: pack_pair_kernel(col_count, *refs),
        out_shape=[shape, shape],
        grid_spec=pltpu.PrefetchScalarGridSpec(
            num_scalar_prefetch=1,
            grid=(2, pairs),
            in_specs=[
                pl.BlockSpec(
                    (slots, width),
                    lambda e, q, meta: (0, first + meta[1] * row_count + block(e, q, meta)),
                )
            ]
            + [pl.BlockSpec((slots, width), lambda e, q, meta: (0, block(e, q, meta)))]
            * (col_count - 1),
            out_specs=[
                pl.BlockSpec((window, width), lambda e, q, meta: (jnp.where(e == 0, 0, q), 0)),
                pl.BlockSpec(
                    (window, width), lambda e, q, meta: (jnp.where(e == 0, q, pairs - 1), 0)
                ),
            ],
            scratch_shapes=[pltpu.VMEM((col_count, window, slots), jnp.bfloat16)],
        ),
        compiler_params=pltpu.CompilerParams(vmem_limit_bytes=VMEM_LIMIT),
        cost_estimate=pl.CostEstimate(
            flops=2 * window * slots * col_count * width * row_count,
            bytes_accessed=2 * row_count * width * (slots * col_count + window),
            transcendentals=0,
        ),
    )(meta, momentum, *received)


def join_kernel(even, window, meta_ref, keep, got, *outs):
    def write(low, high):
        for q, out in enumerate(outs):
            base = q * window
            lap = window - even
            out[:even, :] = low[base : base + even, :]
            out[even:window, :] = (
                low[base + even : base + window, :].astype(jnp.float32)
                + high[base : base + lap, :].astype(jnp.float32)
            ).astype(jnp.bfloat16)
            out[window:, :] = high[base + lap : base + window, :]

    @pl.when(meta_ref[0] % 2 == 0)
    def _():
        write(keep, got)

    @pl.when(meta_ref[0] % 2 == 1)
    def _():
        write(got, keep)


def local_call(kernel, out_shape, operands, moved, scratch=()):
    whole = pl.BlockSpec(memory_space=pltpu.VMEM)
    return pl.pallas_call(
        kernel,
        out_shape=out_shape,
        in_specs=[pl.BlockSpec(memory_space=pltpu.SMEM)] + [whole] * (len(operands) - 1),
        out_specs=jax.tree.map(lambda _: whole, out_shape),
        scratch_shapes=list(scratch),
        compiler_params=pltpu.CompilerParams(vmem_limit_bytes=VMEM_LIMIT),
        cost_estimate=pl.CostEstimate(flops=moved, bytes_accessed=moved, transcendentals=0),
    )(*operands)


def join(meta, keep, got, even, window, pairs):
    width = keep.shape[1]
    shape = jax.ShapeDtypeStruct((even + window, width), jnp.bfloat16)
    return local_call(
        lambda *refs: join_kernel(even, window, *refs),
        [shape] * pairs,
        (meta, keep, got),
        8 * pairs * window * width,
    )


def cut_kernel(even, window, meta_ref, *refs):
    pieces, out = refs[:-1], refs[-1]
    place = pl.ds(pl.multiple_of((1 - meta_ref[0] % 2) * even, 16), window)
    for q, piece in enumerate(pieces):
        out[q * window : (q + 1) * window, :] = piece[place, :]


def cut(meta, pieces, even, window):
    width = pieces[0].shape[1]
    return local_call(
        lambda *refs: cut_kernel(even, window, *refs),
        jax.ShapeDtypeStruct((len(pieces) * window, width), jnp.bfloat16),
        (meta, *pieces),
        4 * len(pieces) * window * width,
    )


def unpack_pair_kernel(col_count, even, window, meta_ref, *refs):
    got, outs, choose = refs[-2 - col_count], refs[-1 - col_count : -1], refs[-1]
    pieces = refs[: -2 - col_count]
    turn = pl.program_id(0)

    @pl.when(turn == 0)
    def _():
        fill_choose(meta_ref, choose, 1)

    def place(block):
        for k in range(col_count):
            outs[k][...] = jnp.dot(
                choose[k], block, preferred_element_type=jnp.float32
            ).astype(jnp.bfloat16)

    for q, piece in enumerate(pieces):

        @pl.when(turn == 2 * q)
        def _():
            own = pl.ds(pl.multiple_of(meta_ref[0] % 2 * even, 16), window)
            place(piece[own, :])

    @pl.when(turn % 2 == 1)
    def _():
        part = pl.ds(pl.multiple_of(turn // 2 * window, 16), window)
        place(got[part, :])


def unpack_pair(meta, pieces, got, col_count, slots, even, window):
    width = got.shape[1]
    count = 2 * len(pieces)
    return pl.pallas_call(
        lambda *refs: unpack_pair_kernel(col_count, even, window, *refs),
        out_shape=[jax.ShapeDtypeStruct((slots, count * width), jnp.bfloat16)] * col_count,
        grid_spec=pltpu.PrefetchScalarGridSpec(
            num_scalar_prefetch=1,
            grid=(count,),
            in_specs=[pl.BlockSpec(x.shape, lambda q, meta: (0, 0)) for x in (*pieces, got)],
            out_specs=[pl.BlockSpec((slots, width), lambda q, meta: (0, meta[0] ^ q))]
            * col_count,
            scratch_shapes=[pltpu.VMEM((col_count, slots, window), jnp.bfloat16)],
        ),
        compiler_params=pltpu.CompilerParams(vmem_limit_bytes=VMEM_LIMIT),
        cost_estimate=pl.CostEstimate(
            flops=2 * window * slots * col_count * width * count,
            bytes_accessed=2 * count * width * (slots * col_count + window),
            transcendentals=0,
        ),
    )(meta, *pieces, got)


def unpack_kernel(col_count, meta_ref, *refs):
    pieces, outs, choose = refs[: -1 - col_count], refs[-1 - col_count : -1], refs[-1]
    turn = pl.program_id(0)
    _, slots, window = choose.shape

    @pl.when(turn == 0)
    def _():
        rows = lax.broadcasted_iota(jnp.int32, (slots, window), 1)
        columns = lax.broadcasted_iota(jnp.int32, (slots, window), 0)
        for k in range(col_count):
            hit = (rows == columns + meta_ref[2 + k]) & (columns < meta_ref[2 + col_count + k])
            choose[k] = jnp.where(hit, 1.0, 0.0).astype(jnp.bfloat16)

    for q, piece in enumerate(pieces):

        @pl.when(turn == q)
        def _():
            for k in range(col_count):
                outs[k][...] = jnp.dot(
                    choose[k], piece[...], preferred_element_type=jnp.float32
                ).astype(jnp.bfloat16)


def unpack(meta, pieces, col_count, slots, step):
    window, width = pieces[0].shape
    count = len(pieces)
    return pl.pallas_call(
        lambda *refs: unpack_kernel(col_count, *refs),
        out_shape=[jax.ShapeDtypeStruct((slots, count * width), jnp.bfloat16)] * col_count,
        grid_spec=pltpu.PrefetchScalarGridSpec(
            num_scalar_prefetch=1,
            grid=(count,),
            in_specs=[pl.BlockSpec((window, width), lambda q, meta: (0, 0))] * count,
            out_specs=[pl.BlockSpec((slots, width), lambda q, meta: (0, (meta[0] // step) ^ q))]
            * col_count,
            scratch_shapes=[pltpu.VMEM((col_count, slots, window), jnp.bfloat16)],
        ),
        compiler_params=pltpu.CompilerParams(vmem_limit_bytes=VMEM_LIMIT),
        cost_estimate=pl.CostEstimate(
            flops=2 * window * slots * col_count * width * count,
            bytes_accessed=2 * count * width * (slots * col_count + window),
            transcendentals=0,
        ),
    )(meta, *pieces)


def merge_kernel(unit, share, distances, meta_ref, *refs):
    pieces, out_ref, total = refs[:-2], refs[-2], refs[-1]
    jitter = (total.shape[0] - M) // 2
    total[...] = jnp.zeros_like(total)
    for places, piece in zip(distances, pieces):
        rows = piece.shape[0] // len(places)
        for n, distance in enumerate(places):
            place = pl.ds(pl.multiple_of(((meta_ref[0] // share) ^ distance) * unit, 8), rows)
            total[place, :] += piece[n * rows : (n + 1) * rows, :].astype(jnp.float32)

    @pl.loop(0, BLOCKS)
    def _(b):
        source = pl.ds(pl.multiple_of(b * TILE + jitter, 8), TILE)
        out_ref[tile_rows(b), :] = total[source, :].astype(jnp.bfloat16)


def merge(meta, pieces, distances, unit, share, jitter):
    width = pieces[0].shape[1]
    return local_call(
        lambda *refs: merge_kernel(unit, share, distances, *refs),
        jax.ShapeDtypeStruct((M, width), jnp.bfloat16),
        (meta, *pieces),
        5 * M * width,
        [pltpu.VMEM((M + 2 * jitter, width), jnp.float32)],
    )


def chunk_gram_kernel(rows_ref, cols_ref, meta_ref, *refs):
    matrices, out_ref, joined = refs[:-2], refs[-2], refs[-1]
    turn = pl.program_id(0)

    @pl.when(turn == 0)
    def _():
        place = 0
        for matrix in matrices[:-1]:
            joined[:, place : place + matrix.shape[1]] = matrix[...]
            place += matrix.shape[1]
        lane = lax.broadcasted_iota(jnp.int32, (TILE, LAST), 1)
        own = lane // (LAST // 2) == meta_ref[0] % 2

        @pl.loop(0, BLOCKS)
        def _(b):
            part = pl.ds(pl.multiple_of(b * TILE, TILE), TILE)
            block = matrices[-1][part, :].astype(jnp.float32)
            joined[part, place:] = jnp.where(own, block, 0.0).astype(jnp.bfloat16)

    here = pl.ds(pl.multiple_of(rows_ref[turn] * TILE, TILE), TILE)
    there = pl.ds(pl.multiple_of(cols_ref[turn] * TILE, TILE), TILE)
    out_ref[...] = lax.dot_general(
        joined[here, :],
        joined[there, :],
        (((1,), (1,)), ((), ())),
        preferred_element_type=jnp.float32,
    ).astype(jnp.bfloat16)


def chunk_gram(meta, chunks):
    count = len(PAIRS)
    width = sum(x.shape[1] for x in chunks)
    return pl.pallas_call(
        chunk_gram_kernel,
        out_shape=jax.ShapeDtypeStruct((count * TILE, TILE), jnp.bfloat16),
        grid_spec=pltpu.PrefetchScalarGridSpec(
            num_scalar_prefetch=3,
            grid=(count,),
            in_specs=[
                pl.BlockSpec((M, x.shape[1]), lambda p, rows, cols, meta: (0, 0)) for x in chunks
            ],
            out_specs=pl.BlockSpec((TILE, TILE), lambda p, rows, cols, meta: (p, 0)),
            scratch_shapes=[pltpu.VMEM((M, width), jnp.bfloat16)],
        ),
        compiler_params=pltpu.CompilerParams(vmem_limit_bytes=VMEM_LIMIT),
        cost_estimate=pl.CostEstimate(
            flops=2 * count * TILE * TILE * width,
            bytes_accessed=2 * count * TILE * TILE + 2 * M * width,
            transcendentals=0,
        ),
    )(jnp.asarray(PAIR_ROWS), jnp.asarray(PAIR_COLS), meta, *chunks)


def tile_rows(b):
    return pl.ds(pl.multiple_of(b * TILE, TILE), TILE)


def first_product(panel, b, jitter, matrix, total, factor):
    product = jnp.dot(panel, matrix[...], preferred_element_type=jnp.float32)
    factor[tile_rows(b), :] = (coef_three * product).astype(jnp.bfloat16)
    total[pl.ds(pl.multiple_of(b * TILE + jitter, 8), TILE), :] = (
        coef_one * matrix[tile_rows(b), :].astype(jnp.float32) + coef_two * product
    )


def second_product(panel, b, jitter, total, factor):
    place = pl.ds(pl.multiple_of(b * TILE + jitter, 8), TILE)
    total[place, :] = math.sqrt(N) * (
        total[place, :] + jnp.dot(panel, factor[...], preferred_element_type=jnp.float32)
    )


def clear_edges(total, jitter):
    edge = jnp.zeros((jitter, total.shape[1]), jnp.float32)
    total[pl.ds(0, jitter), :] = edge
    total[pl.ds(M + jitter, jitter), :] = edge


def store_windows(row, send, total, outs):
    unit, share, rows, distances = send
    for distance, out in zip(distances, outs):
        place = pl.ds(pl.multiple_of(((row // share) ^ distance) * unit, 8), rows)
        out[...] = total[place, :].astype(jnp.bfloat16)


def first_apply_kernel(jitter, send, meta_ref, tiles_ref, matrix, *refs):
    outs, gram_out = refs[:-6], refs[-6]
    gram, total, factor, tile_sems, out_sem = refs[-5:]
    copies = []
    for p, (i, j) in enumerate(PAIRS):
        copies.append(
            pltpu.make_async_copy(
                tiles_ref.at[pl.ds(p * TILE, TILE), :],
                gram.at[i, :, pl.ds(j * TILE, TILE)],
                tile_sems.at[p],
            )
        )
        copies[-1].start()
    clear_edges(total, jitter)
    for p, (i, j) in enumerate(PAIRS):
        copies[p].wait()
        if i != j:
            gram[j, :, pl.ds(i * TILE, TILE)] = gram[i, :, pl.ds(j * TILE, TILE)].T
    back = pltpu.make_async_copy(gram, gram_out, out_sem)
    back.start()

    @pl.loop(0, BLOCKS)
    def _(b):
        first_product(gram[b], b, jitter, matrix, total, factor)

    @pl.loop(0, BLOCKS)
    def _(b):
        second_product(gram[b], b, jitter, total, factor)

    store_windows(meta_ref[0], send, total, outs)
    back.wait()


def first_apply(meta, tiles, matrix, send, jitter):
    width = matrix.shape[1]
    whole = pl.BlockSpec(memory_space=pltpu.VMEM)
    outs = pl.pallas_call(
        lambda *refs: first_apply_kernel(jitter, send, *refs),
        out_shape=[jax.ShapeDtypeStruct((send[2], width), jnp.bfloat16)] * len(send[3])
        + [jax.ShapeDtypeStruct((BLOCKS, TILE, M), jnp.bfloat16)],
        in_specs=[
            pl.BlockSpec(memory_space=pltpu.SMEM),
            pl.BlockSpec(memory_space=pl.ANY),
            whole,
        ],
        out_specs=[whole] * len(send[3]) + [pl.BlockSpec(memory_space=pl.ANY)],
        scratch_shapes=[
            pltpu.VMEM((BLOCKS, TILE, M), jnp.bfloat16),
            pltpu.VMEM((M + 2 * jitter, width), jnp.float32),
            pltpu.VMEM((M, width), jnp.bfloat16),
            pltpu.SemaphoreType.DMA((len(PAIRS),)),
            pltpu.SemaphoreType.DMA,
        ],
        compiler_params=pltpu.CompilerParams(vmem_limit_bytes=VMEM_LIMIT),
        cost_estimate=pl.CostEstimate(
            flops=4 * M * M * width, bytes_accessed=4 * M * width + 4 * M * M, transcendentals=0
        ),
    )(meta, tiles, matrix)
    return outs[:-1], outs[-1]


def next_apply_kernel(jitter, sends, meta_ref, panel_ref, *refs):
    chunks = len(sends)
    outs_count = sum(len(s[3]) for s in sends)
    matrices = refs[:chunks]
    outs = refs[chunks : chunks + outs_count]
    totals = refs[chunks + outs_count : 2 * chunks + outs_count]
    factors = refs[2 * chunks + outs_count :]
    turn = pl.program_id(0)

    @pl.when(turn < BLOCKS)
    def _():
        for matrix, total, factor in zip(matrices, totals, factors):
            first_product(panel_ref[0], turn, jitter, matrix, total, factor)

    @pl.when(turn >= BLOCKS)
    def _():
        for total, factor in zip(totals, factors):
            second_product(panel_ref[0], turn - BLOCKS, jitter, total, factor)

    @pl.when(turn == 2 * BLOCKS - 1)
    def _():
        place = 0
        for total, send in zip(totals, sends):
            clear_edges(total, jitter)
            store_windows(meta_ref[0], send, total, outs[place : place + len(send[3])])
            place += len(send[3])


def next_apply(meta, gram, matrices, sends, jitter):
    widths = [x.shape[1] for x in matrices]
    shapes = [(send[2], width) for width, send in zip(widths, sends) for _ in send[3]]
    whole = lambda t, meta: (0, 0)
    outs = pl.pallas_call(
        lambda *refs: next_apply_kernel(jitter, sends, *refs),
        out_shape=[jax.ShapeDtypeStruct(shape, jnp.bfloat16) for shape in shapes],
        grid_spec=pltpu.PrefetchScalarGridSpec(
            num_scalar_prefetch=1,
            grid=(2 * BLOCKS,),
            in_specs=[pl.BlockSpec((1, TILE, M), lambda t, meta: (t % BLOCKS, 0, 0))]
            + [pl.BlockSpec((M, width), whole) for width in widths],
            out_specs=[pl.BlockSpec(shape, whole) for shape in shapes],
            scratch_shapes=[pltpu.VMEM((M + 2 * jitter, width), jnp.float32) for width in widths]
            + [pltpu.VMEM((M, width), jnp.bfloat16) for width in widths],
        ),
        compiler_params=pltpu.CompilerParams(vmem_limit_bytes=VMEM_LIMIT),
        cost_estimate=pl.CostEstimate(
            flops=4 * M * M * sum(widths),
            bytes_accessed=4 * M * sum(widths) + 4 * M * M,
            transcendentals=0,
        ),
    )(meta, gram, *matrices)
    result = []
    for send in sends:
        result.append(outs[: len(send[3])])
        outs = outs[len(send[3]) :]
    return result


def reduce_tiles(tiles):
    return lax.psum(tiles, ("row", "col"))


def chunk_body(momentum_shards, shard_starts):
    col_count = lax.axis_size("col")
    row_count = lax.axis_size("row")
    pair_count = row_count // 2
    slots = momentum_shards.shape[0]
    mean_rows = M // (row_count * col_count)
    jitter = 4 * (mean_rows // 8)
    even = col_count * mean_rows
    window = even + 2 * jitter
    row = lax.axis_index("row").astype(jnp.int32)
    col = lax.axis_index("col").astype(jnp.int32)
    shard_ends = jnp.concatenate([shard_starts[1:], jnp.full((1,), M, jnp.int32)])
    members = row * col_count + (col ^ jnp.arange(col_count, dtype=jnp.int32))
    begins = shard_starts[members]
    meta = jnp.concatenate(
        [row[None], col[None], begins - (row * even - jitter), shard_ends[members] - begins]
    )

    wide = row_count * col_count * CHUNK
    number = (N // (row_count * col_count)) // CHUNK
    distances = list(range(pair_count))

    def fetch(base, span, after):
        place, after = lax.optimization_barrier((col, after))
        received = [
            swap(
                lax.dynamic_slice_in_dim(
                    momentum_shards, base + (place ^ k) * span, span, axis=1
                ),
                "col",
                col_count,
                k,
            )
            for k in range(1, col_count)
        ]
        return received, after

    def across(pieces):
        return [pieces[0]] + [swap(pieces[q], "row", row_count, 2 * q) for q in distances[1:]]

    def gather_chunk(c, received):
        keep, give = pack_pair(
            meta, momentum_shards, received, c * wide, CHUNK, row_count, window
        )
        return join(meta, keep, swap(give, "row", row_count, 1), even, window, pair_count)

    received, _ = fetch(0, row_count * CHUNK, shard_starts)
    last, received = fetch(number * wide, pair_count * LAST, received)
    joined = gather_chunk(0, received)
    landed = []
    for c in range(1, number):
        received, (last, joined) = fetch(c * wide, row_count * CHUNK, (last, joined))
        crossed, received = lax.optimization_barrier((across(joined), received))
        landed.append(crossed)
        joined = gather_chunk(c, received)
    landed.append(across(joined))
    matrices = [
        merge(meta, pieces, [[q] for q in distances], 2 * even, 2, jitter) for pieces in landed
    ]
    pieces = pack(
        meta, momentum_shards, last, number * wide, LAST, 2, pair_count, window
    )
    stack = jnp.concatenate(across(pieces), axis=0)
    twin = swap(stack, "row", row_count, 1)
    matrices.append(
        merge(
            meta,
            [stack, twin],
            [[2 * q for q in distances], [2 * q + 1 for q in distances]],
            even,
            1,
            jitter,
        )
    )

    tiles = reduce_tiles(chunk_gram(meta, matrices))

    sends = [(2 * even, 2, even + window, distances)] * number
    sends.append((even, 1, window, [2 * q for q in distances]))
    first, gram = first_apply(meta, tiles, matrices[0], sends[0], jitter)
    results = [first] + next_apply(meta, gram, matrices[1:], sends[1:], jitter)

    crossed = [across(results[0])]
    crossed[0], results[1:] = lax.optimization_barrier((crossed[0], results[1:]))
    crossed += [across(pieces) for pieces in results[1:]]
    backs = []
    for c in range(number + 1):
        if c < number:
            got = swap(cut(meta, crossed[c], even, window), "row", row_count, 1)
            parts = unpack_pair(meta, crossed[c], got, col_count, slots, even, window)
        else:
            parts = unpack(meta, crossed[c], col_count, slots, 2)
        back = [parts[0]] + [swap(parts[k], "col", col_count, k) for k in range(1, col_count)]
        if c + 1 < number:
            back, crossed[c + 1 :] = lax.optimization_barrier((back, crossed[c + 1 :]))
        backs.append(back)
    out = jnp.zeros(momentum_shards.shape, jnp.bfloat16)
    for c, back in enumerate(backs):
        span = row_count * CHUNK if c < number else pair_count * LAST
        for k in range(col_count):
            out = lax.dynamic_update_slice_in_dim(
                out, back[k], c * wide + (col ^ k) * span, axis=1
            )
    return out


def body(momentum_shards, shard_starts):
    devices = lax.axis_size("col") * lax.axis_size("row")
    chunks = (N // devices) % CHUNK == LAST // 2 and N // devices > CHUNK
    powers = all(lax.axis_size(a) & (lax.axis_size(a) - 1) == 0 for a in ("row", "col"))
    jitter = 4 * (M // devices // 8)
    if chunks and powers and jitter % 8 == 0:
        return chunk_body(momentum_shards, shard_starts)
    return plain_body(momentum_shards, shard_starts)


def solution(mesh):
    in_specs = (P(("row", "col"), None), P())
    out_specs = P(("row", "col"), None)
    return jax.shard_map(body, mesh=mesh, in_specs=in_specs, out_specs=out_specs, check_vma=False)
```

```python
import math

import jax
import jax.numpy as jnp
import numpy as np
from jax import lax
from jax.experimental import pallas as pl
from jax.experimental.pallas import tpu as pltpu
from jax.sharding import PartitionSpec as P

M = 3584
N = 18432
TILE = 512
BLOCKS = M // TILE

coef_one = 3.4445
coef_two = -4.775
coef_three = 2.0315

PAIRS = [(i, j) for i in range(BLOCKS) for j in range(i, BLOCKS)]
PAIR_ROWS = np.array([i for i, _ in PAIRS], np.int32)
PAIR_COLS = np.array([j for _, j in PAIRS], np.int32)


def packing(shard_starts, row_block, col_count, shard_rows, window, first_row):
    shard_ends = jnp.concatenate([shard_starts[1:], jnp.full((1,), M, jnp.int32)])
    first_starts = lax.dynamic_slice_in_dim(shard_starts, row_block * col_count, col_count)
    last_ends = lax.dynamic_slice_in_dim(shard_ends, row_block * col_count, col_count)
    slot_index = jnp.arange(col_count * shard_rows, dtype=jnp.int32)
    member = slot_index // shard_rows
    offset = slot_index % shard_rows
    pick = member[:, None] == jnp.arange(col_count, dtype=jnp.int32)[None, :]
    shard_begin = jnp.sum(jnp.where(pick, first_starts[None, :], 0), axis=1)
    length = jnp.sum(jnp.where(pick, (last_ends - first_starts)[None, :], 0), axis=1)
    target = shard_begin - first_row + offset
    is_valid = offset < length
    window_rows = jnp.arange(window, dtype=jnp.int32)
    return ((window_rows[:, None] == target[None, :]) & is_valid[None, :]).astype(jnp.bfloat16)


def gram_kernel(rows_ref, cols_ref, left_ref, right_ref, out_ref):
    out_ref[...] = lax.dot_general(
        left_ref[...], right_ref[...], (((1,), (1,)), ((), ())), preferred_element_type=jnp.float32
    ).astype(jnp.bfloat16)


def gram_tiles(matrix):
    width = matrix.shape[1]
    count = len(PAIRS)
    return pl.pallas_call(
        gram_kernel,
        out_shape=jax.ShapeDtypeStruct((count * TILE, TILE), jnp.bfloat16),
        grid_spec=pltpu.PrefetchScalarGridSpec(
            num_scalar_prefetch=2,
            grid=(count,),
            in_specs=[
                pl.BlockSpec((TILE, width), lambda p, rows, cols: (rows[p], 0)),
                pl.BlockSpec((TILE, width), lambda p, rows, cols: (cols[p], 0)),
            ],
            out_specs=pl.BlockSpec((TILE, TILE), lambda p, rows, cols: (p, 0)),
        ),
        compiler_params=pltpu.CompilerParams(vmem_limit_bytes=32 * 1024 * 1024),
        cost_estimate=pl.CostEstimate(
            flops=2 * count * TILE * TILE * width,
            bytes_accessed=2 * count * TILE * (TILE + width),
            transcendentals=0,
        ),
    )(jnp.asarray(PAIR_ROWS), jnp.asarray(PAIR_COLS), matrix, matrix)


def apply_kernel(rows_ref, cols_ref, tile_ref, matrix_ref, out_ref, total, factor):
    turn = pl.program_id(0)
    pair = pl.program_id(1)
    i = rows_ref[pair]
    j = cols_ref[pair]
    here = pl.ds(pl.multiple_of(i * TILE, TILE), TILE)
    there = pl.ds(pl.multiple_of(j * TILE, TILE), TILE)

    @pl.when((turn == 0) & (pair == 0))
    def _():
        total[...] = jnp.zeros_like(total)
        factor[...] = matrix_ref[...]

    @pl.when((turn == 1) & (pair == 0))
    def _():
        @pl.loop(0, BLOCKS)
        def _(b):
            part = pl.ds(pl.multiple_of(b * TILE, TILE), TILE)
            product = total[part, :]
            factor[part, :] = (coef_three * product).astype(jnp.bfloat16)
            total[part, :] = coef_one * matrix_ref[part, :].astype(jnp.float32) + coef_two * product

    total[here, :] += jnp.dot(tile_ref[...], factor[there, :], preferred_element_type=jnp.float32)

    @pl.when(i != j)
    def _():
        total[there, :] += lax.dot_general(
            tile_ref[...], factor[here, :], (((0,), (0,)), ((), ())), preferred_element_type=jnp.float32
        )

    @pl.when((turn == 1) & (pair == pl.num_programs(1) - 1))
    def _():
        @pl.loop(0, BLOCKS)
        def _(b):
            part = pl.ds(pl.multiple_of(b * TILE, TILE), TILE)
            out_ref[part, :] = (math.sqrt(N) * total[part, :]).astype(jnp.bfloat16)


def apply_polynomial(tiles, matrix):
    rows, width = matrix.shape
    count = len(PAIRS)
    return pl.pallas_call(
        apply_kernel,
        out_shape=jax.ShapeDtypeStruct((rows, width), jnp.bfloat16),
        grid_spec=pltpu.PrefetchScalarGridSpec(
            num_scalar_prefetch=2,
            grid=(2, count),
            in_specs=[
                pl.BlockSpec((TILE, TILE), lambda t, p, rows, cols: (p, 0)),
                pl.BlockSpec((rows, width), lambda t, p, rows, cols: (0, 0)),
            ],
            out_specs=pl.BlockSpec((rows, width), lambda t, p, rows, cols: (0, 0)),
            scratch_shapes=[
                pltpu.VMEM((rows, width), jnp.float32),
                pltpu.VMEM((rows, width), jnp.bfloat16),
            ],
        ),
        compiler_params=pltpu.CompilerParams(vmem_limit_bytes=48 * 1024 * 1024),
        cost_estimate=pl.CostEstimate(
            flops=4 * rows * rows * width,
            bytes_accessed=4 * rows * width + 4 * count * TILE * TILE,
            transcendentals=0,
        ),
    )(jnp.asarray(PAIR_ROWS), jnp.asarray(PAIR_COLS), tiles, matrix)


def plain_body(momentum_shards, shard_starts):
    col_count = lax.axis_size("col")
    row_count = lax.axis_size("row")
    shard_rows = momentum_shards.shape[0]
    mean_rows = M // (row_count * col_count)
    jitter = 4 * (mean_rows // 8)
    even = col_count * mean_rows
    window = even + 2 * jitter
    row_block = lax.axis_index("row")
    packer = packing(
        shard_starts, row_block, col_count, shard_rows, window, row_block * even - jitter
    )
    columns = lax.all_to_all(momentum_shards, "col", split_axis=1, concat_axis=0, tiled=True)
    local_tile = jnp.dot(packer, columns, preferred_element_type=jnp.float32).astype(jnp.bfloat16)
    windows = lax.all_to_all(local_tile, "row", split_axis=1, concat_axis=0, tiled=True)
    width = windows.shape[1]
    windows = windows.reshape(row_count, window, width)
    nothing = jnp.zeros((1, jitter, width), jnp.bfloat16)
    head = jnp.concatenate([nothing, windows[:-1, jitter + even :]], axis=0)
    tail = jnp.concatenate([windows[1:, :jitter], nothing], axis=0)
    middle = windows[:, jitter : jitter + even]
    matrix = jnp.concatenate(
        [
            middle[:, :jitter] + head,
            middle[:, jitter : even - jitter],
            middle[:, even - jitter :] + tail,
        ],
        axis=1,
    ).reshape(M, width)

    tiles = lax.psum(gram_tiles(matrix), ("row", "col"))
    update = apply_polynomial(tiles, matrix).reshape(row_count, even, width)

    before = jnp.concatenate([nothing, update[:-1, even - jitter :]], axis=0)
    after = jnp.concatenate([update[1:, :jitter], nothing], axis=0)
    spread = jnp.concatenate([before, update, after], axis=1).reshape(row_count * window, width)
    own_rows = lax.all_to_all(spread, "row", split_axis=0, concat_axis=1, tiled=True)
    back_rows = lax.dot_general(
        packer, own_rows, (((0,), (0,)), ((), ())), preferred_element_type=jnp.float32
    ).astype(jnp.bfloat16)
    return lax.all_to_all(back_rows, "col", split_axis=0, concat_axis=1, tiled=True)


CHUNK = 256
LAST = 128
VMEM_LIMIT = 56 * 1024 * 1024


def swap(value, axis, size, distance):
    return lax.ppermute(value, axis, perm=[(i, i ^ distance) for i in range(size)])


def pack_kernel(step, col_count, meta_ref, *refs):
    pieces, outs, choose = refs[:col_count], refs[col_count:-1], refs[-1]
    turn = pl.program_id(0)
    _, window, slots = choose.shape

    @pl.when(turn == 0)
    def _():
        rows = lax.broadcasted_iota(jnp.int32, (window, slots), 0)
        columns = lax.broadcasted_iota(jnp.int32, (window, slots), 1)
        for k in range(col_count):
            hit = (rows == columns + meta_ref[2 + k]) & (columns < meta_ref[2 + col_count + k])
            choose[k] = jnp.where(hit, 1.0, 0.0).astype(jnp.bfloat16)

    total = jnp.dot(choose[0], pieces[0][...], preferred_element_type=jnp.float32)
    for k in range(1, col_count):
        total += jnp.dot(choose[k], pieces[k][...], preferred_element_type=jnp.float32)
    for q, out in enumerate(outs):

        @pl.when(turn == q)
        def _():
            out[...] = total.astype(jnp.bfloat16)


def pack(meta, momentum, received, base, width, step, count, window):
    slots = momentum.shape[0]
    col_count = len(received) + 1
    first = base // width
    return pl.pallas_call(
        lambda *refs: pack_kernel(step, col_count, *refs),
        out_shape=[jax.ShapeDtypeStruct((window, width), jnp.bfloat16)] * count,
        grid_spec=pltpu.PrefetchScalarGridSpec(
            num_scalar_prefetch=1,
            grid=(count,),
            in_specs=[
                pl.BlockSpec(
                    (slots, width),
                    lambda q, meta: (0, first + meta[1] * count + ((meta[0] // step) ^ q)),
                )
            ]
            + [pl.BlockSpec((slots, width), lambda q, meta: (0, (meta[0] // step) ^ q))]
            * (col_count - 1),
            out_specs=[pl.BlockSpec((window, width), lambda q, meta: (0, 0))] * count,
            scratch_shapes=[pltpu.VMEM((col_count, window, slots), jnp.bfloat16)],
        ),
        compiler_params=pltpu.CompilerParams(vmem_limit_bytes=VMEM_LIMIT),
        cost_estimate=pl.CostEstimate(
            flops=2 * window * slots * col_count * width * count,
            bytes_accessed=2 * count * width * (slots * col_count + window),
            transcendentals=0,
        ),
    )(meta, momentum, *received)


def pack_pair_kernel(col_count, meta_ref, *refs):
    pieces, keep, give, choose = refs[:col_count], refs[col_count], refs[col_count + 1], refs[-1]
    other = pl.program_id(0) == 0
    _, window, slots = choose.shape

    @pl.when(other & (pl.program_id(1) == 0))
    def _():
        fill_choose(meta_ref, choose, 0)

    total = jnp.dot(choose[0], pieces[0][...], preferred_element_type=jnp.float32)
    for k in range(1, col_count):
        total += jnp.dot(choose[k], pieces[k][...], preferred_element_type=jnp.float32)

    @pl.when(other)
    def _():
        give[...] = total.astype(jnp.bfloat16)

    @pl.when(jnp.logical_not(other))
    def _():
        keep[...] = total.astype(jnp.bfloat16)


def fill_choose(meta_ref, choose, slot_axis):
    col_count = choose.shape[0]
    shape = choose.shape[1:]
    rows = lax.broadcasted_iota(jnp.int32, shape, slot_axis)
    slots = lax.broadcasted_iota(jnp.int32, shape, 1 - slot_axis)
    for k in range(col_count):
        hit = (rows == slots + meta_ref[2 + k]) & (slots < meta_ref[2 + col_count + k])
        choose[k] = jnp.where(hit, 1.0, 0.0).astype(jnp.bfloat16)


def pack_pair(meta, momentum, received, base, width, row_count, window):
    slots = momentum.shape[0]
    col_count = len(received) + 1
    pairs = row_count // 2
    first = base // width
    block = lambda e, q, meta: meta[0] ^ (2 * q + 1 - e)
    shape = jax.ShapeDtypeStruct((pairs * window, width), jnp.bfloat16)
    return pl.pallas_call(
        lambda *refs: pack_pair_kernel(col_count, *refs),
        out_shape=[shape, shape],
        grid_spec=pltpu.PrefetchScalarGridSpec(
            num_scalar_prefetch=1,
            grid=(2, pairs),
            in_specs=[
                pl.BlockSpec(
                    (slots, width),
                    lambda e, q, meta: (0, first + meta[1] * row_count + block(e, q, meta)),
                )
            ]
            + [pl.BlockSpec((slots, width), lambda e, q, meta: (0, block(e, q, meta)))]
            * (col_count - 1),
            out_specs=[
                pl.BlockSpec((window, width), lambda e, q, meta: (jnp.where(e == 0, 0, q), 0)),
                pl.BlockSpec(
                    (window, width), lambda e, q, meta: (jnp.where(e == 0, q, pairs - 1), 0)
                ),
            ],
            scratch_shapes=[pltpu.VMEM((col_count, window, slots), jnp.bfloat16)],
        ),
        compiler_params=pltpu.CompilerParams(vmem_limit_bytes=VMEM_LIMIT),
        cost_estimate=pl.CostEstimate(
            flops=2 * window * slots * col_count * width * row_count,
            bytes_accessed=2 * row_count * width * (slots * col_count + window),
            transcendentals=0,
        ),
    )(meta, momentum, *received)


def join_kernel(even, window, meta_ref, keep, got, *outs):
    def write(low, high):
        for q, out in enumerate(outs):
            base = q * window
            lap = window - even
            out[:even, :] = low[base : base + even, :]
            out[even:window, :] = (
                low[base + even : base + window, :].astype(jnp.float32)
                + high[base : base + lap, :].astype(jnp.float32)
            ).astype(jnp.bfloat16)
            out[window:, :] = high[base + lap : base + window, :]

    @pl.when(meta_ref[0] % 2 == 0)
    def _():
        write(keep, got)

    @pl.when(meta_ref[0] % 2 == 1)
    def _():
        write(got, keep)


def local_call(kernel, out_shape, operands, moved, scratch=()):
    whole = pl.BlockSpec(memory_space=pltpu.VMEM)
    return pl.pallas_call(
        kernel,
        out_shape=out_shape,
        in_specs=[pl.BlockSpec(memory_space=pltpu.SMEM)] + [whole] * (len(operands) - 1),
        out_specs=jax.tree.map(lambda _: whole, out_shape),
        scratch_shapes=list(scratch),
        compiler_params=pltpu.CompilerParams(vmem_limit_bytes=VMEM_LIMIT),
        cost_estimate=pl.CostEstimate(flops=moved, bytes_accessed=moved, transcendentals=0),
    )(*operands)


def join(meta, keep, got, even, window, pairs):
    width = keep.shape[1]
    shape = jax.ShapeDtypeStruct((even + window, width), jnp.bfloat16)
    return local_call(
        lambda *refs: join_kernel(even, window, *refs),
        [shape] * pairs,
        (meta, keep, got),
        8 * pairs * window * width,
    )


def cut_kernel(even, window, meta_ref, *refs):
    pieces, out = refs[:-1], refs[-1]
    place = pl.ds(pl.multiple_of((1 - meta_ref[0] % 2) * even, 16), window)
    for q, piece in enumerate(pieces):
        out[q * window : (q + 1) * window, :] = piece[place, :]


def cut(meta, pieces, even, window):
    width = pieces[0].shape[1]
    return local_call(
        lambda *refs: cut_kernel(even, window, *refs),
        jax.ShapeDtypeStruct((len(pieces) * window, width), jnp.bfloat16),
        (meta, *pieces),
        4 * len(pieces) * window * width,
    )


def unpack_pair_kernel(col_count, even, window, meta_ref, *refs):
    got, outs, choose = refs[-2 - col_count], refs[-1 - col_count : -1], refs[-1]
    pieces = refs[: -2 - col_count]
    turn = pl.program_id(0)

    @pl.when(turn == 0)
    def _():
        fill_choose(meta_ref, choose, 1)

    def place(block):
        for k in range(col_count):
            outs[k][...] = jnp.dot(
                choose[k], block, preferred_element_type=jnp.float32
            ).astype(jnp.bfloat16)

    for q, piece in enumerate(pieces):

        @pl.when(turn == 2 * q)
        def _():
            own = pl.ds(pl.multiple_of(meta_ref[0] % 2 * even, 16), window)
            place(piece[own, :])

    @pl.when(turn % 2 == 1)
    def _():
        part = pl.ds(pl.multiple_of(turn // 2 * window, 16), window)
        place(got[part, :])


def unpack_pair(meta, pieces, got, col_count, slots, even, window):
    width = got.shape[1]
    count = 2 * len(pieces)
    return pl.pallas_call(
        lambda *refs: unpack_pair_kernel(col_count, even, window, *refs),
        out_shape=[jax.ShapeDtypeStruct((slots, count * width), jnp.bfloat16)] * col_count,
        grid_spec=pltpu.PrefetchScalarGridSpec(
            num_scalar_prefetch=1,
            grid=(count,),
            in_specs=[pl.BlockSpec(x.shape, lambda q, meta: (0, 0)) for x in (*pieces, got)],
            out_specs=[pl.BlockSpec((slots, width), lambda q, meta: (0, meta[0] ^ q))]
            * col_count,
            scratch_shapes=[pltpu.VMEM((col_count, slots, window), jnp.bfloat16)],
        ),
        compiler_params=pltpu.CompilerParams(vmem_limit_bytes=VMEM_LIMIT),
        cost_estimate=pl.CostEstimate(
            flops=2 * window * slots * col_count * width * count,
            bytes_accessed=2 * count * width * (slots * col_count + window),
            transcendentals=0,
        ),
    )(meta, *pieces, got)


def unpack_kernel(col_count, meta_ref, *refs):
    pieces, outs, choose = refs[: -1 - col_count], refs[-1 - col_count : -1], refs[-1]
    turn = pl.program_id(0)
    _, slots, window = choose.shape

    @pl.when(turn == 0)
    def _():
        rows = lax.broadcasted_iota(jnp.int32, (slots, window), 1)
        columns = lax.broadcasted_iota(jnp.int32, (slots, window), 0)
        for k in range(col_count):
            hit = (rows == columns + meta_ref[2 + k]) & (columns < meta_ref[2 + col_count + k])
            choose[k] = jnp.where(hit, 1.0, 0.0).astype(jnp.bfloat16)

    for q, piece in enumerate(pieces):

        @pl.when(turn == q)
        def _():
            for k in range(col_count):
                outs[k][...] = jnp.dot(
                    choose[k], piece[...], preferred_element_type=jnp.float32
                ).astype(jnp.bfloat16)


def unpack(meta, pieces, col_count, slots, step):
    window, width = pieces[0].shape
    count = len(pieces)
    return pl.pallas_call(
        lambda *refs: unpack_kernel(col_count, *refs),
        out_shape=[jax.ShapeDtypeStruct((slots, count * width), jnp.bfloat16)] * col_count,
        grid_spec=pltpu.PrefetchScalarGridSpec(
            num_scalar_prefetch=1,
            grid=(count,),
            in_specs=[pl.BlockSpec((window, width), lambda q, meta: (0, 0))] * count,
            out_specs=[pl.BlockSpec((slots, width), lambda q, meta: (0, (meta[0] // step) ^ q))]
            * col_count,
            scratch_shapes=[pltpu.VMEM((col_count, slots, window), jnp.bfloat16)],
        ),
        compiler_params=pltpu.CompilerParams(vmem_limit_bytes=VMEM_LIMIT),
        cost_estimate=pl.CostEstimate(
            flops=2 * window * slots * col_count * width * count,
            bytes_accessed=2 * count * width * (slots * col_count + window),
            transcendentals=0,
        ),
    )(meta, *pieces)


def merge_kernel(unit, share, distances, meta_ref, *refs):
    pieces, out_ref, total = refs[:-2], refs[-2], refs[-1]
    jitter = (total.shape[0] - M) // 2
    total[...] = jnp.zeros_like(total)
    for places, piece in zip(distances, pieces):
        rows = piece.shape[0] // len(places)
        for n, distance in enumerate(places):
            place = pl.ds(pl.multiple_of(((meta_ref[0] // share) ^ distance) * unit, 8), rows)
            total[place, :] += piece[n * rows : (n + 1) * rows, :].astype(jnp.float32)

    @pl.loop(0, BLOCKS)
    def _(b):
        source = pl.ds(pl.multiple_of(b * TILE + jitter, 8), TILE)
        out_ref[tile_rows(b), :] = total[source, :].astype(jnp.bfloat16)


def merge(meta, pieces, distances, unit, share, jitter):
    width = pieces[0].shape[1]
    return local_call(
        lambda *refs: merge_kernel(unit, share, distances, *refs),
        jax.ShapeDtypeStruct((M, width), jnp.bfloat16),
        (meta, *pieces),
        5 * M * width,
        [pltpu.VMEM((M + 2 * jitter, width), jnp.float32)],
    )


def collect_kernel(meta_ref, *refs):
    matrices, joined = refs[:-1], refs[-1]
    place = 0
    for matrix in matrices[:-1]:
        joined[:, place : place + matrix.shape[1]] = matrix[...]
        place += matrix.shape[1]
    lane = lax.broadcasted_iota(jnp.int32, (TILE, LAST), 1)
    own = lane // (LAST // 2) == meta_ref[0] % 2

    @pl.loop(0, BLOCKS)
    def _(b):
        block = matrices[-1][tile_rows(b), :].astype(jnp.float32)
        joined[tile_rows(b), place:] = jnp.where(own, block, 0.0).astype(jnp.bfloat16)


def collect(meta, chunks):
    width = sum(x.shape[1] for x in chunks)
    return local_call(
        collect_kernel,
        jax.ShapeDtypeStruct((M, width), jnp.bfloat16),
        (meta, *chunks),
        4 * M * width,
    )


PIECES = 2
HALF = len(PAIRS) // 2
PART = HALF // PIECES


def half_gram_kernel(flip, rows_ref, cols_ref, meta_ref, joined, *outs):
    turn = pl.program_id(0)
    pair = (meta_ref[0] % 2 ^ flip) * HALF + turn
    here = pl.ds(pl.multiple_of(rows_ref[pair] * TILE, TILE), TILE)
    there = pl.ds(pl.multiple_of(cols_ref[pair] * TILE, TILE), TILE)
    tile = lax.dot_general(
        joined[here, :],
        joined[there, :],
        (((1,), (1,)), ((), ())),
        preferred_element_type=jnp.float32,
    ).astype(jnp.bfloat16)
    for n, out in enumerate(outs):

        @pl.when(turn // PART == n)
        def _():
            out[...] = tile


def half_gram(meta, joined, flip):
    width = joined.shape[1]
    place = lambda n: lambda p, rows, cols, meta: (jnp.clip(p - n * PART, 0, PART - 1), 0)
    return pl.pallas_call(
        lambda *refs: half_gram_kernel(flip, *refs),
        out_shape=[jax.ShapeDtypeStruct((PART * TILE, TILE), jnp.bfloat16)] * PIECES,
        grid_spec=pltpu.PrefetchScalarGridSpec(
            num_scalar_prefetch=3,
            grid=(HALF,),
            in_specs=[pl.BlockSpec((M, width), lambda p, rows, cols, meta: (0, 0))],
            out_specs=[pl.BlockSpec((TILE, TILE), place(n)) for n in range(PIECES)],
        ),
        compiler_params=pltpu.CompilerParams(vmem_limit_bytes=VMEM_LIMIT),
        cost_estimate=pl.CostEstimate(
            flops=2 * HALF * TILE * TILE * width,
            bytes_accessed=2 * HALF * TILE * TILE + 2 * M * width,
            transcendentals=0,
        ),
    )(jnp.asarray(PAIR_ROWS), jnp.asarray(PAIR_COLS), meta, joined)


def lane_block(block, lanes):
    return pl.ds(pl.multiple_of(block * lanes, lanes), lanes)


def add_halves_kernel(meta_ref, keep, got, *outs):
    lanes = outs[0].shape[1]
    for k, out in enumerate(outs):
        part = lane_block(meta_ref[1] ^ k, lanes)
        out[...] = (keep[:, part].astype(jnp.float32) + got[:, part].astype(jnp.float32)).astype(
            jnp.bfloat16
        )


def gridded(kernel, meta, operands, outs, moved):
    rows = operands[0].shape[0]
    block = lambda x: pl.BlockSpec((TILE, x.shape[1]), lambda t, meta: (t, 0))
    return pl.pallas_call(
        kernel,
        out_shape=outs,
        grid_spec=pltpu.PrefetchScalarGridSpec(
            num_scalar_prefetch=1,
            grid=(rows // TILE,),
            in_specs=[block(x) for x in operands],
            out_specs=jax.tree.map(block, outs),
        ),
        compiler_params=pltpu.CompilerParams(vmem_limit_bytes=VMEM_LIMIT),
        cost_estimate=pl.CostEstimate(flops=moved, bytes_accessed=moved, transcendentals=0),
    )(meta, *operands)


def add_halves(meta, keep, got, col_count):
    rows, lanes = keep.shape
    shape = jax.ShapeDtypeStruct((rows, lanes // col_count), jnp.bfloat16)
    return gridded(add_halves_kernel, meta, (keep, got), [shape] * col_count, 6 * rows * lanes)


def total_of(refs, part):
    total = refs[0][part, :].astype(jnp.float32)
    for ref in refs[1:]:
        total += ref[part, :].astype(jnp.float32)
    return total.astype(jnp.bfloat16)


def add_quarters_kernel(col_count, meta_ref, *refs):
    blocks, outs = refs[:col_count], refs[col_count:]
    rows = outs[0].shape[0]
    for q, out in enumerate(outs):
        place = (meta_ref[0] // 2 ^ q) * rows
        out[...] = total_of(blocks, pl.ds(pl.multiple_of(place, rows), rows))


def add_quarters(meta, blocks, pair_count):
    rows, lanes = blocks[0].shape
    shape = jax.ShapeDtypeStruct((rows // pair_count, lanes), jnp.bfloat16)
    return local_call(
        lambda *refs: add_quarters_kernel(len(blocks), *refs),
        [shape] * pair_count,
        (meta, *blocks),
        10 * rows * lanes,
    )


def add_parts_kernel(meta_ref, *refs):
    rows = refs[-1].shape[0]
    refs[-1][...] = total_of(refs[:-1], pl.ds(0, rows))


def add_parts(meta, parts):
    return local_call(
        add_parts_kernel,
        jax.ShapeDtypeStruct(parts[0].shape, jnp.bfloat16),
        (meta, *parts),
        10 * parts[0].size,
    )


def stack_kernel(meta_ref, *refs):
    parts, out = refs[:-1], refs[-1]
    rows = parts[0].shape[0]
    for q, part in enumerate(parts):
        out[pl.ds(pl.multiple_of((meta_ref[0] // 2 ^ q) * rows, rows), rows), :] = part[...]


def stack(meta, parts):
    rows, lanes = parts[0].shape
    return local_call(
        stack_kernel,
        jax.ShapeDtypeStruct((rows * len(parts), lanes), jnp.bfloat16),
        (meta, *parts),
        4 * rows * lanes * len(parts),
    )


def widen_kernel(meta_ref, *refs):
    blocks, out = refs[:-1], refs[-1]
    for k, block in enumerate(blocks):
        out[:, lane_block(meta_ref[1] ^ k, block.shape[1])] = block[...]


def widen(meta, blocks):
    rows, lanes = blocks[0].shape
    shape = jax.ShapeDtypeStruct((rows, lanes * len(blocks)), jnp.bfloat16)
    return gridded(widen_kernel, meta, blocks, shape, 4 * rows * lanes * len(blocks))


def tile_rows(b):
    return pl.ds(pl.multiple_of(b * TILE, TILE), TILE)


def first_product(panel, b, jitter, matrix, total, factor):
    product = jnp.dot(panel, matrix[...], preferred_element_type=jnp.float32)
    factor[tile_rows(b), :] = (coef_three * product).astype(jnp.bfloat16)
    total[pl.ds(pl.multiple_of(b * TILE + jitter, 8), TILE), :] = (
        coef_one * matrix[tile_rows(b), :].astype(jnp.float32) + coef_two * product
    )


def second_product(panel, b, jitter, total, factor):
    place = pl.ds(pl.multiple_of(b * TILE + jitter, 8), TILE)
    total[place, :] = math.sqrt(N) * (
        total[place, :] + jnp.dot(panel, factor[...], preferred_element_type=jnp.float32)
    )


def clear_edges(total, jitter):
    edge = jnp.zeros((jitter, total.shape[1]), jnp.float32)
    total[pl.ds(0, jitter), :] = edge
    total[pl.ds(M + jitter, jitter), :] = edge


def store_windows(row, send, total, outs):
    unit, share, rows, distances = send
    for distance, out in zip(distances, outs):
        place = pl.ds(pl.multiple_of(((row // share) ^ distance) * unit, 8), rows)
        out[...] = total[place, :].astype(jnp.bfloat16)


def first_apply_kernel(jitter, send, rows_ref, cols_ref, meta_ref, *refs):
    pieces, matrix = refs[: 2 * PIECES], refs[2 * PIECES]
    outs, gram_out = refs[2 * PIECES + 1 : -6], refs[-6]
    gram, total, factor, tile_sems, out_sem = refs[-5:]
    copies = []
    for n in range(2 * HALF):
        half, part = divmod(n, HALF)
        pair = (meta_ref[0] % 2 ^ half) * HALF + part
        i, j = rows_ref[pair], cols_ref[pair]
        copy = pltpu.make_async_copy(
            pieces[half * PIECES + part // PART].at[pl.ds(part % PART * TILE, TILE), :],
            gram.at[i, :, lane_block(j, TILE)],
            tile_sems.at[n],
        )
        copy.start()
        copies.append((copy, i, j))
    clear_edges(total, jitter)
    for copy, i, j in copies:
        copy.wait()

        @pl.when(i != j)
        def _():
            gram[j, :, lane_block(i, TILE)] = gram[i, :, lane_block(j, TILE)].T

    back = pltpu.make_async_copy(gram, gram_out, out_sem)
    back.start()

    @pl.loop(0, BLOCKS)
    def _(b):
        first_product(gram[b], b, jitter, matrix, total, factor)

    @pl.loop(0, BLOCKS)
    def _(b):
        second_product(gram[b], b, jitter, total, factor)

    store_windows(meta_ref[0], send, total, outs)
    back.wait()


def first_apply(meta, pieces, matrix, send, jitter):
    width = matrix.shape[1]
    whole = pl.BlockSpec(memory_space=pltpu.VMEM)
    outs = pl.pallas_call(
        lambda *refs: first_apply_kernel(jitter, send, *refs),
        out_shape=[jax.ShapeDtypeStruct((send[2], width), jnp.bfloat16)] * len(send[3])
        + [jax.ShapeDtypeStruct((BLOCKS, TILE, M), jnp.bfloat16)],
        in_specs=[pl.BlockSpec(memory_space=pltpu.SMEM)] * 3
        + [pl.BlockSpec(memory_space=pl.ANY)] * len(pieces)
        + [whole],
        out_specs=[whole] * len(send[3]) + [pl.BlockSpec(memory_space=pl.ANY)],
        scratch_shapes=[
            pltpu.VMEM((BLOCKS, TILE, M), jnp.bfloat16),
            pltpu.VMEM((M + 2 * jitter, width), jnp.float32),
            pltpu.VMEM((M, width), jnp.bfloat16),
            pltpu.SemaphoreType.DMA((len(PAIRS),)),
            pltpu.SemaphoreType.DMA,
        ],
        compiler_params=pltpu.CompilerParams(vmem_limit_bytes=VMEM_LIMIT),
        cost_estimate=pl.CostEstimate(
            flops=4 * M * M * width, bytes_accessed=4 * M * width + 4 * M * M, transcendentals=0
        ),
    )(jnp.asarray(PAIR_ROWS), jnp.asarray(PAIR_COLS), meta, *pieces, matrix)
    return outs[:-1], outs[-1]


def next_apply_kernel(jitter, sends, meta_ref, panel_ref, *refs):
    chunks = len(sends)
    outs_count = sum(len(s[3]) for s in sends)
    matrices = refs[:chunks]
    outs = refs[chunks : chunks + outs_count]
    totals = refs[chunks + outs_count : 2 * chunks + outs_count]
    factors = refs[2 * chunks + outs_count :]
    turn = pl.program_id(0)

    @pl.when(turn < BLOCKS)
    def _():
        for matrix, total, factor in zip(matrices, totals, factors):
            first_product(panel_ref[0], turn, jitter, matrix, total, factor)

    @pl.when(turn >= BLOCKS)
    def _():
        for total, factor in zip(totals, factors):
            second_product(panel_ref[0], turn - BLOCKS, jitter, total, factor)

    @pl.when(turn == 2 * BLOCKS - 1)
    def _():
        place = 0
        for total, send in zip(totals, sends):
            clear_edges(total, jitter)
            store_windows(meta_ref[0], send, total, outs[place : place + len(send[3])])
            place += len(send[3])


def next_apply(meta, gram, matrices, sends, jitter):
    widths = [x.shape[1] for x in matrices]
    shapes = [(send[2], width) for width, send in zip(widths, sends) for _ in send[3]]
    whole = lambda t, meta: (0, 0)
    outs = pl.pallas_call(
        lambda *refs: next_apply_kernel(jitter, sends, *refs),
        out_shape=[jax.ShapeDtypeStruct(shape, jnp.bfloat16) for shape in shapes],
        grid_spec=pltpu.PrefetchScalarGridSpec(
            num_scalar_prefetch=1,
            grid=(2 * BLOCKS,),
            in_specs=[pl.BlockSpec((1, TILE, M), lambda t, meta: (t % BLOCKS, 0, 0))]
            + [pl.BlockSpec((M, width), whole) for width in widths],
            out_specs=[pl.BlockSpec(shape, whole) for shape in shapes],
            scratch_shapes=[pltpu.VMEM((M + 2 * jitter, width), jnp.float32) for width in widths]
            + [pltpu.VMEM((M, width), jnp.bfloat16) for width in widths],
        ),
        compiler_params=pltpu.CompilerParams(vmem_limit_bytes=VMEM_LIMIT),
        cost_estimate=pl.CostEstimate(
            flops=4 * M * M * sum(widths),
            bytes_accessed=4 * M * sum(widths) + 4 * M * M,
            transcendentals=0,
        ),
    )(meta, gram, *matrices)
    result = []
    for send in sends:
        result.append(outs[: len(send[3])])
        outs = outs[len(send[3]) :]
    return result


def sum_tiles(meta, joined, row_count, col_count):
    pair_count = row_count // 2
    tie = lax.optimization_barrier

    def over_cols(blocks):
        return [swap(blocks[k], "col", col_count, k) for k in range(1, col_count)]

    def over_pairs(blocks):
        return [swap(blocks[q], "row", row_count, 2 * q) for q in range(1, pair_count)]

    give = half_gram(meta, joined, 1)
    got = [swap(piece, "row", row_count, 1) for piece in give]
    keep = half_gram(meta, joined, 0)

    early = add_halves(meta, keep[0], got[0], col_count)
    early_in = over_cols(early)
    late = add_halves(meta, keep[1], got[1], col_count)
    late, early_in = tie((late, early_in))
    late_in = over_cols(late)
    early_parts = add_quarters(meta, [early[0]] + early_in, pair_count)
    early_in = over_pairs(early_parts)
    late_in, early_in = tie((late_in, early_in))
    early_part = add_parts(meta, [early_parts[0]] + early_in)
    early_in = over_pairs([early_part] * pair_count)
    late_parts = add_quarters(meta, [late[0]] + late_in, pair_count)
    late_parts, early_in = tie((late_parts, early_in))
    early_block = stack(meta, [early_part] + early_in)
    early_in = over_cols([early_block] * col_count)
    late_in = over_pairs(late_parts)
    late_part = add_parts(meta, [late_parts[0]] + late_in)
    late_in = over_pairs([late_part] * pair_count)
    late_in, early_in = tie((late_in, early_in))
    late_block = stack(meta, [late_part] + late_in)
    late_in = over_cols([late_block] * col_count)
    early = widen(meta, [early_block] + early_in)
    early_twin = swap(early, "row", row_count, 1)
    late = widen(meta, [late_block] + late_in)
    late_twin = swap(late, "row", row_count, 1)
    return [early, late, early_twin, late_twin]


def chunk_body(momentum_shards, shard_starts):
    col_count = lax.axis_size("col")
    row_count = lax.axis_size("row")
    pair_count = row_count // 2
    slots = momentum_shards.shape[0]
    mean_rows = M // (row_count * col_count)
    jitter = 4 * (mean_rows // 8)
    even = col_count * mean_rows
    window = even + 2 * jitter
    row = lax.axis_index("row").astype(jnp.int32)
    col = lax.axis_index("col").astype(jnp.int32)
    shard_ends = jnp.concatenate([shard_starts[1:], jnp.full((1,), M, jnp.int32)])
    members = row * col_count + (col ^ jnp.arange(col_count, dtype=jnp.int32))
    begins = shard_starts[members]
    meta = jnp.concatenate(
        [row[None], col[None], begins - (row * even - jitter), shard_ends[members] - begins]
    )

    wide = row_count * col_count * CHUNK
    number = (N // (row_count * col_count)) // CHUNK
    distances = list(range(pair_count))

    def fetch(base, span, after):
        place, after = lax.optimization_barrier((col, after))
        received = [
            swap(
                lax.dynamic_slice_in_dim(
                    momentum_shards, base + (place ^ k) * span, span, axis=1
                ),
                "col",
                col_count,
                k,
            )
            for k in range(1, col_count)
        ]
        return received, after

    def across(pieces):
        return [pieces[0]] + [swap(pieces[q], "row", row_count, 2 * q) for q in distances[1:]]

    def gather_chunk(c, received):
        keep, give = pack_pair(
            meta, momentum_shards, received, c * wide, CHUNK, row_count, window
        )
        return join(meta, keep, swap(give, "row", row_count, 1), even, window, pair_count)

    received, _ = fetch(0, row_count * CHUNK, shard_starts)
    last, received = fetch(number * wide, pair_count * LAST, received)
    joined = gather_chunk(0, received)
    landed = []
    for c in range(1, number):
        received, (last, joined) = fetch(c * wide, row_count * CHUNK, (last, joined))
        crossed, received = lax.optimization_barrier((across(joined), received))
        landed.append(crossed)
        joined = gather_chunk(c, received)
    landed.append(across(joined))
    matrices = [
        merge(meta, pieces, [[q] for q in distances], 2 * even, 2, jitter) for pieces in landed
    ]
    pieces = pack(
        meta, momentum_shards, last, number * wide, LAST, 2, pair_count, window
    )
    stack = jnp.concatenate(across(pieces), axis=0)
    twin = swap(stack, "row", row_count, 1)
    matrices.append(
        merge(
            meta,
            [stack, twin],
            [[2 * q for q in distances], [2 * q + 1 for q in distances]],
            even,
            1,
            jitter,
        )
    )

    tiles = sum_tiles(meta, collect(meta, matrices), row_count, col_count)

    sends = [(2 * even, 2, even + window, distances)] * number
    sends.append((even, 1, window, [2 * q for q in distances]))
    first, gram = first_apply(meta, tiles, matrices[0], sends[0], jitter)
    results = [first] + next_apply(meta, gram, matrices[1:], sends[1:], jitter)

    crossed = [across(results[0])]
    crossed[0], results[1:] = lax.optimization_barrier((crossed[0], results[1:]))
    crossed += [across(pieces) for pieces in results[1:]]
    backs = []
    for c in range(number + 1):
        if c < number:
            got = swap(cut(meta, crossed[c], even, window), "row", row_count, 1)
            parts = unpack_pair(meta, crossed[c], got, col_count, slots, even, window)
        else:
            parts = unpack(meta, crossed[c], col_count, slots, 2)
        back = [parts[0]] + [swap(parts[k], "col", col_count, k) for k in range(1, col_count)]
        if c + 1 < number:
            back, crossed[c + 1 :] = lax.optimization_barrier((back, crossed[c + 1 :]))
        backs.append(back)
    out = jnp.zeros(momentum_shards.shape, jnp.bfloat16)
    for c, back in enumerate(backs):
        span = row_count * CHUNK if c < number else pair_count * LAST
        for k in range(col_count):
            out = lax.dynamic_update_slice_in_dim(
                out, back[k], c * wide + (col ^ k) * span, axis=1
            )
    return out


def body(momentum_shards, shard_starts):
    devices = lax.axis_size("col") * lax.axis_size("row")
    chunks = (N // devices) % CHUNK == LAST // 2 and N // devices > CHUNK
    powers = all(lax.axis_size(a) & (lax.axis_size(a) - 1) == 0 for a in ("row", "col"))
    jitter = 4 * (M // devices // 8)
    if chunks and powers and jitter % 8 == 0:
        return chunk_body(momentum_shards, shard_starts)
    return plain_body(momentum_shards, shard_starts)


def solution(mesh):
    in_specs = (P(("row", "col"), None), P())
    out_specs = P(("row", "col"), None)
    return jax.shard_map(body, mesh=mesh, in_specs=in_specs, out_specs=out_specs, check_vma=False)
```

```python
import math

import jax
import jax.numpy as jnp
import numpy as np
from jax import lax
from jax.experimental import pallas as pl
from jax.experimental.pallas import tpu as pltpu
from jax.sharding import PartitionSpec as P

M = 3584
N = 18432
TILE = 512
BLOCKS = M // TILE

coef_one = 3.4445
coef_two = -4.775
coef_three = 2.0315

PAIRS = [(i, j) for i in range(BLOCKS) for j in range(i, BLOCKS)]
PAIR_ROWS = np.array([i for i, _ in PAIRS], np.int32)
PAIR_COLS = np.array([j for _, j in PAIRS], np.int32)


def packing(shard_starts, row_block, col_count, shard_rows, window, first_row):
    shard_ends = jnp.concatenate([shard_starts[1:], jnp.full((1,), M, jnp.int32)])
    first_starts = lax.dynamic_slice_in_dim(shard_starts, row_block * col_count, col_count)
    last_ends = lax.dynamic_slice_in_dim(shard_ends, row_block * col_count, col_count)
    slot_index = jnp.arange(col_count * shard_rows, dtype=jnp.int32)
    member = slot_index // shard_rows
    offset = slot_index % shard_rows
    pick = member[:, None] == jnp.arange(col_count, dtype=jnp.int32)[None, :]
    shard_begin = jnp.sum(jnp.where(pick, first_starts[None, :], 0), axis=1)
    length = jnp.sum(jnp.where(pick, (last_ends - first_starts)[None, :], 0), axis=1)
    target = shard_begin - first_row + offset
    is_valid = offset < length
    window_rows = jnp.arange(window, dtype=jnp.int32)
    return ((window_rows[:, None] == target[None, :]) & is_valid[None, :]).astype(jnp.bfloat16)


def gram_kernel(rows_ref, cols_ref, left_ref, right_ref, out_ref):
    out_ref[...] = lax.dot_general(
        left_ref[...], right_ref[...], (((1,), (1,)), ((), ())), preferred_element_type=jnp.float32
    ).astype(jnp.bfloat16)


def gram_tiles(matrix):
    width = matrix.shape[1]
    count = len(PAIRS)
    return pl.pallas_call(
        gram_kernel,
        out_shape=jax.ShapeDtypeStruct((count * TILE, TILE), jnp.bfloat16),
        grid_spec=pltpu.PrefetchScalarGridSpec(
            num_scalar_prefetch=2,
            grid=(count,),
            in_specs=[
                pl.BlockSpec((TILE, width), lambda p, rows, cols: (rows[p], 0)),
                pl.BlockSpec((TILE, width), lambda p, rows, cols: (cols[p], 0)),
            ],
            out_specs=pl.BlockSpec((TILE, TILE), lambda p, rows, cols: (p, 0)),
        ),
        compiler_params=pltpu.CompilerParams(vmem_limit_bytes=32 * 1024 * 1024),
        cost_estimate=pl.CostEstimate(
            flops=2 * count * TILE * TILE * width,
            bytes_accessed=2 * count * TILE * (TILE + width),
            transcendentals=0,
        ),
    )(jnp.asarray(PAIR_ROWS), jnp.asarray(PAIR_COLS), matrix, matrix)


def apply_kernel(rows_ref, cols_ref, tile_ref, matrix_ref, out_ref, total, factor):
    turn = pl.program_id(0)
    pair = pl.program_id(1)
    i = rows_ref[pair]
    j = cols_ref[pair]
    here = pl.ds(pl.multiple_of(i * TILE, TILE), TILE)
    there = pl.ds(pl.multiple_of(j * TILE, TILE), TILE)

    @pl.when((turn == 0) & (pair == 0))
    def _():
        total[...] = jnp.zeros_like(total)
        factor[...] = matrix_ref[...]

    @pl.when((turn == 1) & (pair == 0))
    def _():
        @pl.loop(0, BLOCKS)
        def _(b):
            part = pl.ds(pl.multiple_of(b * TILE, TILE), TILE)
            product = total[part, :]
            factor[part, :] = (coef_three * product).astype(jnp.bfloat16)
            total[part, :] = coef_one * matrix_ref[part, :].astype(jnp.float32) + coef_two * product

    total[here, :] += jnp.dot(tile_ref[...], factor[there, :], preferred_element_type=jnp.float32)

    @pl.when(i != j)
    def _():
        total[there, :] += lax.dot_general(
            tile_ref[...], factor[here, :], (((0,), (0,)), ((), ())), preferred_element_type=jnp.float32
        )

    @pl.when((turn == 1) & (pair == pl.num_programs(1) - 1))
    def _():
        @pl.loop(0, BLOCKS)
        def _(b):
            part = pl.ds(pl.multiple_of(b * TILE, TILE), TILE)
            out_ref[part, :] = (math.sqrt(N) * total[part, :]).astype(jnp.bfloat16)


def apply_polynomial(tiles, matrix):
    rows, width = matrix.shape
    count = len(PAIRS)
    return pl.pallas_call(
        apply_kernel,
        out_shape=jax.ShapeDtypeStruct((rows, width), jnp.bfloat16),
        grid_spec=pltpu.PrefetchScalarGridSpec(
            num_scalar_prefetch=2,
            grid=(2, count),
            in_specs=[
                pl.BlockSpec((TILE, TILE), lambda t, p, rows, cols: (p, 0)),
                pl.BlockSpec((rows, width), lambda t, p, rows, cols: (0, 0)),
            ],
            out_specs=pl.BlockSpec((rows, width), lambda t, p, rows, cols: (0, 0)),
            scratch_shapes=[
                pltpu.VMEM((rows, width), jnp.float32),
                pltpu.VMEM((rows, width), jnp.bfloat16),
            ],
        ),
        compiler_params=pltpu.CompilerParams(vmem_limit_bytes=48 * 1024 * 1024),
        cost_estimate=pl.CostEstimate(
            flops=4 * rows * rows * width,
            bytes_accessed=4 * rows * width + 4 * count * TILE * TILE,
            transcendentals=0,
        ),
    )(jnp.asarray(PAIR_ROWS), jnp.asarray(PAIR_COLS), tiles, matrix)


def plain_body(momentum_shards, shard_starts):
    col_count = lax.axis_size("col")
    row_count = lax.axis_size("row")
    shard_rows = momentum_shards.shape[0]
    mean_rows = M // (row_count * col_count)
    jitter = 4 * (mean_rows // 8)
    even = col_count * mean_rows
    window = even + 2 * jitter
    row_block = lax.axis_index("row")
    packer = packing(
        shard_starts, row_block, col_count, shard_rows, window, row_block * even - jitter
    )
    columns = lax.all_to_all(momentum_shards, "col", split_axis=1, concat_axis=0, tiled=True)
    local_tile = jnp.dot(packer, columns, preferred_element_type=jnp.float32).astype(jnp.bfloat16)
    windows = lax.all_to_all(local_tile, "row", split_axis=1, concat_axis=0, tiled=True)
    width = windows.shape[1]
    windows = windows.reshape(row_count, window, width)
    nothing = jnp.zeros((1, jitter, width), jnp.bfloat16)
    head = jnp.concatenate([nothing, windows[:-1, jitter + even :]], axis=0)
    tail = jnp.concatenate([windows[1:, :jitter], nothing], axis=0)
    middle = windows[:, jitter : jitter + even]
    matrix = jnp.concatenate(
        [
            middle[:, :jitter] + head,
            middle[:, jitter : even - jitter],
            middle[:, even - jitter :] + tail,
        ],
        axis=1,
    ).reshape(M, width)

    tiles = lax.psum(gram_tiles(matrix), ("row", "col"))
    update = apply_polynomial(tiles, matrix).reshape(row_count, even, width)

    before = jnp.concatenate([nothing, update[:-1, even - jitter :]], axis=0)
    after = jnp.concatenate([update[1:, :jitter], nothing], axis=0)
    spread = jnp.concatenate([before, update, after], axis=1).reshape(row_count * window, width)
    own_rows = lax.all_to_all(spread, "row", split_axis=0, concat_axis=1, tiled=True)
    back_rows = lax.dot_general(
        packer, own_rows, (((0,), (0,)), ((), ())), preferred_element_type=jnp.float32
    ).astype(jnp.bfloat16)
    return lax.all_to_all(back_rows, "col", split_axis=0, concat_axis=1, tiled=True)


CHUNK = 256
LAST = 128
VMEM_LIMIT = 56 * 1024 * 1024


def swap(value, axis, size, distance):
    return lax.ppermute(value, axis, perm=[(i, i ^ distance) for i in range(size)])


def pack_kernel(step, col_count, meta_ref, *refs):
    pieces, outs, choose = refs[:col_count], refs[col_count:-1], refs[-1]
    turn = pl.program_id(0)
    _, window, slots = choose.shape

    @pl.when(turn == 0)
    def _():
        rows = lax.broadcasted_iota(jnp.int32, (window, slots), 0)
        columns = lax.broadcasted_iota(jnp.int32, (window, slots), 1)
        for k in range(col_count):
            hit = (rows == columns + meta_ref[2 + k]) & (columns < meta_ref[2 + col_count + k])
            choose[k] = jnp.where(hit, 1.0, 0.0).astype(jnp.bfloat16)

    total = jnp.dot(choose[0], pieces[0][...], preferred_element_type=jnp.float32)
    for k in range(1, col_count):
        total += jnp.dot(choose[k], pieces[k][...], preferred_element_type=jnp.float32)
    for q, out in enumerate(outs):

        @pl.when(turn == q)
        def _():
            out[...] = total.astype(jnp.bfloat16)


def pack(meta, momentum, received, base, width, step, count, window):
    slots = momentum.shape[0]
    col_count = len(received) + 1
    first = base // width
    return pl.pallas_call(
        lambda *refs: pack_kernel(step, col_count, *refs),
        out_shape=[jax.ShapeDtypeStruct((window, width), jnp.bfloat16)] * count,
        grid_spec=pltpu.PrefetchScalarGridSpec(
            num_scalar_prefetch=1,
            grid=(count,),
            in_specs=[
                pl.BlockSpec(
                    (slots, width),
                    lambda q, meta: (0, first + meta[1] * count + ((meta[0] // step) ^ q)),
                )
            ]
            + [pl.BlockSpec((slots, width), lambda q, meta: (0, (meta[0] // step) ^ q))]
            * (col_count - 1),
            out_specs=[pl.BlockSpec((window, width), lambda q, meta: (0, 0))] * count,
            scratch_shapes=[pltpu.VMEM((col_count, window, slots), jnp.bfloat16)],
        ),
        compiler_params=pltpu.CompilerParams(vmem_limit_bytes=VMEM_LIMIT),
        cost_estimate=pl.CostEstimate(
            flops=2 * window * slots * col_count * width * count,
            bytes_accessed=2 * count * width * (slots * col_count + window),
            transcendentals=0,
        ),
    )(meta, momentum, *received)


def pack_pair_kernel(meta_ref, *refs):
    pieces, (keep, give, choose, joined) = refs[:-4], refs[-4:]
    other = pl.program_id(0) == 0

    @pl.when(other & (pl.program_id(1) == 0))
    def _():
        fill_wide(meta_ref, choose, 1, len(pieces))

    slots = pieces[0].shape[0]
    for k, piece in enumerate(pieces):
        joined[k * slots : (k + 1) * slots, :] = piece[...]
    block = jnp.dot(choose[...], joined[...], preferred_element_type=jnp.float32).astype(
        jnp.bfloat16
    )

    @pl.when(other)
    def _():
        give[...] = block

    @pl.when(jnp.logical_not(other))
    def _():
        keep[...] = block


def fill_wide(meta_ref, choose, slot_axis, col_count):
    shape = choose.shape
    slots = shape[slot_axis] // col_count
    rows = lax.broadcasted_iota(jnp.int32, shape, 1 - slot_axis)
    slot = lax.broadcasted_iota(jnp.int32, shape, slot_axis)
    hit = jnp.zeros(shape, jnp.bool_)
    for k in range(col_count):
        first = k * slots
        hit |= (
            (rows == slot + (meta_ref[2 + k] - first))
            & (slot >= first)
            & (slot < first + meta_ref[2 + col_count + k])
        )
    choose[...] = jnp.where(hit, 1.0, 0.0).astype(jnp.bfloat16)


def fill_choose(meta_ref, choose, slot_axis):
    col_count = choose.shape[0]
    shape = choose.shape[1:]
    rows = lax.broadcasted_iota(jnp.int32, shape, slot_axis)
    slots = lax.broadcasted_iota(jnp.int32, shape, 1 - slot_axis)
    for k in range(col_count):
        hit = (rows == slots + meta_ref[2 + k]) & (slots < meta_ref[2 + col_count + k])
        choose[k] = jnp.where(hit, 1.0, 0.0).astype(jnp.bfloat16)


def pack_pair(meta, momentum, received, base, width, row_count, window):
    slots = momentum.shape[0]
    col_count = len(received) + 1
    pairs = row_count // 2
    first = base // width
    block = lambda e, q, meta: meta[0] ^ (2 * q + 1 - e)
    shape = jax.ShapeDtypeStruct((pairs * window, width), jnp.bfloat16)
    return pl.pallas_call(
        pack_pair_kernel,
        out_shape=[shape, shape],
        grid_spec=pltpu.PrefetchScalarGridSpec(
            num_scalar_prefetch=1,
            grid=(2, pairs),
            in_specs=[
                pl.BlockSpec(
                    (slots, width),
                    lambda e, q, meta: (0, first + meta[1] * row_count + block(e, q, meta)),
                )
            ]
            + [pl.BlockSpec((slots, width), lambda e, q, meta: (0, block(e, q, meta)))]
            * (col_count - 1),
            out_specs=[
                pl.BlockSpec((window, width), lambda e, q, meta: (jnp.where(e == 0, 0, q), 0)),
                pl.BlockSpec(
                    (window, width), lambda e, q, meta: (jnp.where(e == 0, q, pairs - 1), 0)
                ),
            ],
            scratch_shapes=[
                pltpu.VMEM((window, col_count * slots), jnp.bfloat16),
                pltpu.VMEM((col_count * slots, width), jnp.bfloat16),
            ],
        ),
        compiler_params=pltpu.CompilerParams(vmem_limit_bytes=VMEM_LIMIT),
        cost_estimate=pl.CostEstimate(
            flops=2 * window * slots * col_count * width * row_count,
            bytes_accessed=2 * row_count * width * (slots * col_count + window),
            transcendentals=0,
        ),
    )(meta, momentum, *received)


def join_kernel(even, window, meta_ref, keep, got, *outs):
    def write(low, high):
        for q, out in enumerate(outs):
            base = q * window
            lap = window - even
            out[:even, :] = low[base : base + even, :]
            out[even:window, :] = (
                low[base + even : base + window, :].astype(jnp.float32)
                + high[base : base + lap, :].astype(jnp.float32)
            ).astype(jnp.bfloat16)
            out[window:, :] = high[base + lap : base + window, :]

    @pl.when(meta_ref[0] % 2 == 0)
    def _():
        write(keep, got)

    @pl.when(meta_ref[0] % 2 == 1)
    def _():
        write(got, keep)


def local_call(kernel, out_shape, operands, moved, scratch=()):
    whole = pl.BlockSpec(memory_space=pltpu.VMEM)
    return pl.pallas_call(
        kernel,
        out_shape=out_shape,
        in_specs=[pl.BlockSpec(memory_space=pltpu.SMEM)] + [whole] * (len(operands) - 1),
        out_specs=jax.tree.map(lambda _: whole, out_shape),
        scratch_shapes=list(scratch),
        compiler_params=pltpu.CompilerParams(vmem_limit_bytes=VMEM_LIMIT),
        cost_estimate=pl.CostEstimate(flops=moved, bytes_accessed=moved, transcendentals=0),
    )(*operands)


def join(meta, keep, got, even, window, pairs):
    width = keep.shape[1]
    shape = jax.ShapeDtypeStruct((even + window, width), jnp.bfloat16)
    return local_call(
        lambda *refs: join_kernel(even, window, *refs),
        [shape] * pairs,
        (meta, keep, got),
        8 * pairs * window * width,
    )


def cut_kernel(even, window, meta_ref, *refs):
    pieces, out = refs[:-1], refs[-1]
    place = pl.ds(pl.multiple_of((1 - meta_ref[0] % 2) * even, 16), window)
    for q, piece in enumerate(pieces):
        out[q * window : (q + 1) * window, :] = piece[place, :]


def cut(meta, pieces, even, window):
    width = pieces[0].shape[1]
    return local_call(
        lambda *refs: cut_kernel(even, window, *refs),
        jax.ShapeDtypeStruct((len(pieces) * window, width), jnp.bfloat16),
        (meta, *pieces),
        4 * len(pieces) * window * width,
    )


def unpack_pair_kernel(col_count, even, window, meta_ref, *refs):
    got, outs, choose = refs[-2 - col_count], refs[-1 - col_count : -1], refs[-1]
    pieces = refs[: -2 - col_count]
    turn = pl.program_id(0)

    @pl.when(turn == 0)
    def _():
        fill_wide(meta_ref, choose, 0, col_count)

    def place(block):
        rows = jnp.dot(choose[...], block, preferred_element_type=jnp.float32)
        slots = outs[0].shape[0]
        for k in range(col_count):
            outs[k][...] = rows[k * slots : (k + 1) * slots, :].astype(jnp.bfloat16)

    for q, piece in enumerate(pieces):

        @pl.when(turn == 2 * q)
        def _():
            own = pl.ds(pl.multiple_of(meta_ref[0] % 2 * even, 16), window)
            place(piece[own, :])

    @pl.when(turn % 2 == 1)
    def _():
        part = pl.ds(pl.multiple_of(turn // 2 * window, 16), window)
        place(got[part, :])


def unpack_pair(meta, pieces, got, col_count, slots, even, window):
    width = got.shape[1]
    count = 2 * len(pieces)
    return pl.pallas_call(
        lambda *refs: unpack_pair_kernel(col_count, even, window, *refs),
        out_shape=[jax.ShapeDtypeStruct((slots, count * width), jnp.bfloat16)] * col_count,
        grid_spec=pltpu.PrefetchScalarGridSpec(
            num_scalar_prefetch=1,
            grid=(count,),
            in_specs=[pl.BlockSpec(x.shape, lambda q, meta: (0, 0)) for x in (*pieces, got)],
            out_specs=[pl.BlockSpec((slots, width), lambda q, meta: (0, meta[0] ^ q))]
            * col_count,
            scratch_shapes=[pltpu.VMEM((col_count * slots, window), jnp.bfloat16)],
        ),
        compiler_params=pltpu.CompilerParams(vmem_limit_bytes=VMEM_LIMIT),
        cost_estimate=pl.CostEstimate(
            flops=2 * window * slots * col_count * width * count,
            bytes_accessed=2 * count * width * (slots * col_count + window),
            transcendentals=0,
        ),
    )(meta, *pieces, got)


def unpack_kernel(col_count, meta_ref, *refs):
    pieces, outs, choose = refs[: -1 - col_count], refs[-1 - col_count : -1], refs[-1]
    turn = pl.program_id(0)
    _, slots, window = choose.shape

    @pl.when(turn == 0)
    def _():
        rows = lax.broadcasted_iota(jnp.int32, (slots, window), 1)
        columns = lax.broadcasted_iota(jnp.int32, (slots, window), 0)
        for k in range(col_count):
            hit = (rows == columns + meta_ref[2 + k]) & (columns < meta_ref[2 + col_count + k])
            choose[k] = jnp.where(hit, 1.0, 0.0).astype(jnp.bfloat16)

    for q, piece in enumerate(pieces):

        @pl.when(turn == q)
        def _():
            for k in range(col_count):
                outs[k][...] = jnp.dot(
                    choose[k], piece[...], preferred_element_type=jnp.float32
                ).astype(jnp.bfloat16)


def unpack(meta, pieces, col_count, slots, step):
    window, width = pieces[0].shape
    count = len(pieces)
    return pl.pallas_call(
        lambda *refs: unpack_kernel(col_count, *refs),
        out_shape=[jax.ShapeDtypeStruct((slots, count * width), jnp.bfloat16)] * col_count,
        grid_spec=pltpu.PrefetchScalarGridSpec(
            num_scalar_prefetch=1,
            grid=(count,),
            in_specs=[pl.BlockSpec((window, width), lambda q, meta: (0, 0))] * count,
            out_specs=[pl.BlockSpec((slots, width), lambda q, meta: (0, (meta[0] // step) ^ q))]
            * col_count,
            scratch_shapes=[pltpu.VMEM((col_count, slots, window), jnp.bfloat16)],
        ),
        compiler_params=pltpu.CompilerParams(vmem_limit_bytes=VMEM_LIMIT),
        cost_estimate=pl.CostEstimate(
            flops=2 * window * slots * col_count * width * count,
            bytes_accessed=2 * count * width * (slots * col_count + window),
            transcendentals=0,
        ),
    )(meta, *pieces)


def merge_kernel(unit, share, distances, meta_ref, *refs):
    pieces, out_ref, total = refs[:-2], refs[-2], refs[-1]
    jitter = (total.shape[0] - M) // 2
    total[...] = jnp.zeros_like(total)
    for places, piece in zip(distances, pieces):
        rows = piece.shape[0] // len(places)
        for n, distance in enumerate(places):
            place = pl.ds(pl.multiple_of(((meta_ref[0] // share) ^ distance) * unit, 8), rows)
            total[place, :] += piece[n * rows : (n + 1) * rows, :].astype(jnp.float32)

    @pl.loop(0, BLOCKS)
    def _(b):
        source = pl.ds(pl.multiple_of(b * TILE + jitter, 8), TILE)
        out_ref[tile_rows(b), :] = total[source, :].astype(jnp.bfloat16)


def merge(meta, pieces, distances, unit, share, jitter):
    width = pieces[0].shape[1]
    return local_call(
        lambda *refs: merge_kernel(unit, share, distances, *refs),
        jax.ShapeDtypeStruct((M, width), jnp.bfloat16),
        (meta, *pieces),
        5 * M * width,
        [pltpu.VMEM((M + 2 * jitter, width), jnp.float32)],
    )


def collect_kernel(meta_ref, *refs):
    matrices, joined, turned = refs[:-2], refs[-2], refs[-1]
    place = 0
    for matrix in matrices[:-1]:
        joined[:, place : place + matrix.shape[1]] = matrix[...]
        place += matrix.shape[1]
    lane = lax.broadcasted_iota(jnp.int32, (TILE, LAST), 1)
    own = lane // (LAST // 2) == meta_ref[0] % 2

    @pl.loop(0, BLOCKS)
    def _(b):
        block = matrices[-1][tile_rows(b), :].astype(jnp.float32)
        joined[tile_rows(b), place:] = jnp.where(own, block, 0.0).astype(jnp.bfloat16)
        turned[:, lane_block(b, TILE)] = joined[tile_rows(b), :].T


def collect(meta, chunks):
    width = sum(x.shape[1] for x in chunks)
    return local_call(
        collect_kernel,
        [jax.ShapeDtypeStruct(shape, jnp.bfloat16) for shape in ((M, width), (width, M))],
        (meta, *chunks),
        4 * M * width,
    )


PIECES = 2
HALF = len(PAIRS) // 2
PART = HALF // PIECES


def some_gram_kernel(flip, piece, rows_ref, cols_ref, meta_ref, joined, turned, out):
    pair = (meta_ref[0] % 2 ^ flip) * HALF + piece * PART + pl.program_id(0)
    here = pl.ds(pl.multiple_of(rows_ref[pair] * TILE, TILE), TILE)
    out[...] = jnp.dot(
        joined[here, :],
        turned[:, lane_block(cols_ref[pair], TILE)],
        preferred_element_type=jnp.float32,
    ).astype(jnp.bfloat16)


def some_gram(meta, joined, turned, flip, piece):
    count = PART
    width = joined.shape[1]
    return pl.pallas_call(
        lambda *refs: some_gram_kernel(flip, piece, *refs),
        out_shape=jax.ShapeDtypeStruct((count * TILE, TILE), jnp.bfloat16),
        grid_spec=pltpu.PrefetchScalarGridSpec(
            num_scalar_prefetch=3,
            grid=(count,),
            in_specs=[
                pl.BlockSpec(x.shape, lambda p, rows, cols, meta: (0, 0)) for x in (joined, turned)
            ],
            out_specs=pl.BlockSpec((TILE, TILE), lambda p, rows, cols, meta: (p, 0)),
        ),
        compiler_params=pltpu.CompilerParams(vmem_limit_bytes=VMEM_LIMIT),
        cost_estimate=pl.CostEstimate(
            flops=2 * count * TILE * TILE * width,
            bytes_accessed=2 * count * TILE * TILE + 4 * M * width,
            transcendentals=0,
        ),
    )(jnp.asarray(PAIR_ROWS), jnp.asarray(PAIR_COLS), meta, joined, turned)


def lane_block(block, lanes):
    return pl.ds(pl.multiple_of(block * lanes, lanes), lanes)


def add_halves_kernel(meta_ref, keep, got, *outs):
    lanes = outs[0].shape[1]
    for k, out in enumerate(outs):
        part = lane_block(meta_ref[1] ^ k, lanes)
        out[...] = (keep[:, part].astype(jnp.float32) + got[:, part].astype(jnp.float32)).astype(
            jnp.bfloat16
        )


def gridded(kernel, meta, operands, outs, moved):
    rows = operands[0].shape[0]
    block = lambda x: pl.BlockSpec((TILE, x.shape[1]), lambda t, meta: (t, 0))
    return pl.pallas_call(
        kernel,
        out_shape=outs,
        grid_spec=pltpu.PrefetchScalarGridSpec(
            num_scalar_prefetch=1,
            grid=(rows // TILE,),
            in_specs=[block(x) for x in operands],
            out_specs=jax.tree.map(block, outs),
        ),
        compiler_params=pltpu.CompilerParams(vmem_limit_bytes=VMEM_LIMIT),
        cost_estimate=pl.CostEstimate(flops=moved, bytes_accessed=moved, transcendentals=0),
    )(meta, *operands)


def add_halves(meta, keep, got, col_count):
    rows, lanes = keep.shape
    shape = jax.ShapeDtypeStruct((rows, lanes // col_count), jnp.bfloat16)
    return gridded(add_halves_kernel, meta, (keep, got), [shape] * col_count, 6 * rows * lanes)


def total_of(refs, part):
    total = refs[0][part, :].astype(jnp.float32)
    for ref in refs[1:]:
        total += ref[part, :].astype(jnp.float32)
    return total.astype(jnp.bfloat16)


def add_quarters_kernel(col_count, meta_ref, *refs):
    blocks, outs = refs[:col_count], refs[col_count:]
    rows = outs[0].shape[0]
    for q, out in enumerate(outs):
        place = (meta_ref[0] // 2 ^ q) * rows
        out[...] = total_of(blocks, pl.ds(pl.multiple_of(place, rows), rows))


def add_quarters(meta, blocks, pair_count):
    rows, lanes = blocks[0].shape
    shape = jax.ShapeDtypeStruct((rows // pair_count, lanes), jnp.bfloat16)
    return local_call(
        lambda *refs: add_quarters_kernel(len(blocks), *refs),
        [shape] * pair_count,
        (meta, *blocks),
        10 * rows * lanes,
    )


def add_parts_kernel(meta_ref, *refs):
    rows = refs[-1].shape[0]
    refs[-1][...] = total_of(refs[:-1], pl.ds(0, rows))


def add_parts(meta, parts):
    return local_call(
        add_parts_kernel,
        jax.ShapeDtypeStruct(parts[0].shape, jnp.bfloat16),
        (meta, *parts),
        10 * parts[0].size,
    )


def stack_kernel(meta_ref, *refs):
    parts, out = refs[:-1], refs[-1]
    rows = parts[0].shape[0]
    for q, part in enumerate(parts):
        out[pl.ds(pl.multiple_of((meta_ref[0] // 2 ^ q) * rows, rows), rows), :] = part[...]


def stack(meta, parts):
    rows, lanes = parts[0].shape
    return local_call(
        stack_kernel,
        jax.ShapeDtypeStruct((rows * len(parts), lanes), jnp.bfloat16),
        (meta, *parts),
        4 * rows * lanes * len(parts),
    )


def widen_kernel(meta_ref, *refs):
    blocks, out = refs[:-1], refs[-1]
    for k, block in enumerate(blocks):
        out[:, lane_block(meta_ref[1] ^ k, block.shape[1])] = block[...]


def widen(meta, blocks):
    rows, lanes = blocks[0].shape
    shape = jax.ShapeDtypeStruct((rows, lanes * len(blocks)), jnp.bfloat16)
    return gridded(widen_kernel, meta, blocks, shape, 4 * rows * lanes * len(blocks))


def tile_rows(b):
    return pl.ds(pl.multiple_of(b * TILE, TILE), TILE)


def first_product(panel, b, jitter, matrix, total, factor):
    product = jnp.dot(panel, matrix[...], preferred_element_type=jnp.float32)
    factor[tile_rows(b), :] = (coef_three * product).astype(jnp.bfloat16)
    total[pl.ds(pl.multiple_of(b * TILE + jitter, 8), TILE), :] = (
        coef_one * matrix[tile_rows(b), :].astype(jnp.float32) + coef_two * product
    )


def second_product(panel, b, jitter, total, factor):
    place = pl.ds(pl.multiple_of(b * TILE + jitter, 8), TILE)
    total[place, :] = math.sqrt(N) * (
        total[place, :] + jnp.dot(panel, factor[...], preferred_element_type=jnp.float32)
    )


def clear_edges(total, jitter):
    edge = jnp.zeros((jitter, total.shape[1]), jnp.float32)
    total[pl.ds(0, jitter), :] = edge
    total[pl.ds(M + jitter, jitter), :] = edge


def store_windows(row, send, total, outs):
    unit, share, rows, distances = send
    for distance, out in zip(distances, outs):
        place = pl.ds(pl.multiple_of(((row // share) ^ distance) * unit, 8), rows)
        out[...] = total[place, :].astype(jnp.bfloat16)


def first_apply_kernel(jitter, send, rows_ref, cols_ref, meta_ref, *refs):
    pieces, matrix = refs[: 2 * PIECES], refs[2 * PIECES]
    outs, gram_out = refs[2 * PIECES + 1 : -6], refs[-6]
    gram, total, factor, tile_sems, out_sem = refs[-5:]
    copies = []
    for n in range(2 * HALF):
        half, part = divmod(n, HALF)
        pair = (meta_ref[0] % 2 ^ half) * HALF + part
        i, j = rows_ref[pair], cols_ref[pair]
        copy = pltpu.make_async_copy(
            pieces[half * PIECES + part // PART].at[pl.ds(part % PART * TILE, TILE), :],
            gram.at[i, :, lane_block(j, TILE)],
            tile_sems.at[n],
        )
        copy.start()
        copies.append((copy, i, j))
    clear_edges(total, jitter)
    for copy, i, j in copies:
        copy.wait()

        @pl.when(i != j)
        def _():
            gram[j, :, lane_block(i, TILE)] = gram[i, :, lane_block(j, TILE)].T

    back = pltpu.make_async_copy(gram, gram_out, out_sem)
    back.start()

    @pl.loop(0, BLOCKS)
    def _(b):
        first_product(gram[b], b, jitter, matrix, total, factor)

    @pl.loop(0, BLOCKS)
    def _(b):
        second_product(gram[b], b, jitter, total, factor)

    store_windows(meta_ref[0], send, total, outs)
    back.wait()


def first_apply(meta, pieces, matrix, send, jitter):
    width = matrix.shape[1]
    whole = pl.BlockSpec(memory_space=pltpu.VMEM)
    outs = pl.pallas_call(
        lambda *refs: first_apply_kernel(jitter, send, *refs),
        out_shape=[jax.ShapeDtypeStruct((send[2], width), jnp.bfloat16)] * len(send[3])
        + [jax.ShapeDtypeStruct((BLOCKS, TILE, M), jnp.bfloat16)],
        in_specs=[pl.BlockSpec(memory_space=pltpu.SMEM)] * 3
        + [pl.BlockSpec(memory_space=pl.ANY)] * len(pieces)
        + [whole],
        out_specs=[whole] * len(send[3]) + [pl.BlockSpec(memory_space=pl.ANY)],
        scratch_shapes=[
            pltpu.VMEM((BLOCKS, TILE, M), jnp.bfloat16),
            pltpu.VMEM((M + 2 * jitter, width), jnp.float32),
            pltpu.VMEM((M, width), jnp.bfloat16),
            pltpu.SemaphoreType.DMA((len(PAIRS),)),
            pltpu.SemaphoreType.DMA,
        ],
        compiler_params=pltpu.CompilerParams(vmem_limit_bytes=VMEM_LIMIT),
        cost_estimate=pl.CostEstimate(
            flops=4 * M * M * width, bytes_accessed=4 * M * width + 4 * M * M, transcendentals=0
        ),
    )(jnp.asarray(PAIR_ROWS), jnp.asarray(PAIR_COLS), meta, *pieces, matrix)
    return outs[:-1], outs[-1]


def next_apply_kernel(jitter, sends, meta_ref, panel_ref, *refs):
    chunks = len(sends)
    outs_count = sum(len(s[3]) for s in sends)
    matrices = refs[:chunks]
    outs = refs[chunks : chunks + outs_count]
    totals = refs[chunks + outs_count : 2 * chunks + outs_count]
    factors = refs[2 * chunks + outs_count :]
    turn = pl.program_id(0)

    @pl.when(turn < BLOCKS)
    def _():
        for matrix, total, factor in zip(matrices, totals, factors):
            first_product(panel_ref[0], turn, jitter, matrix, total, factor)

    @pl.when(turn >= BLOCKS)
    def _():
        for total, factor in zip(totals, factors):
            second_product(panel_ref[0], turn - BLOCKS, jitter, total, factor)

    @pl.when(turn == 2 * BLOCKS - 1)
    def _():
        place = 0
        for total, send in zip(totals, sends):
            clear_edges(total, jitter)
            store_windows(meta_ref[0], send, total, outs[place : place + len(send[3])])
            place += len(send[3])


def next_apply(meta, gram, matrices, sends, jitter):
    widths = [x.shape[1] for x in matrices]
    shapes = [(send[2], width) for width, send in zip(widths, sends) for _ in send[3]]
    whole = lambda t, meta: (0, 0)
    outs = pl.pallas_call(
        lambda *refs: next_apply_kernel(jitter, sends, *refs),
        out_shape=[jax.ShapeDtypeStruct(shape, jnp.bfloat16) for shape in shapes],
        grid_spec=pltpu.PrefetchScalarGridSpec(
            num_scalar_prefetch=1,
            grid=(2 * BLOCKS,),
            in_specs=[pl.BlockSpec((1, TILE, M), lambda t, meta: (t % BLOCKS, 0, 0))]
            + [pl.BlockSpec((M, width), whole) for width in widths],
            out_specs=[pl.BlockSpec(shape, whole) for shape in shapes],
            scratch_shapes=[pltpu.VMEM((M + 2 * jitter, width), jnp.float32) for width in widths]
            + [pltpu.VMEM((M, width), jnp.bfloat16) for width in widths],
        ),
        compiler_params=pltpu.CompilerParams(vmem_limit_bytes=VMEM_LIMIT),
        cost_estimate=pl.CostEstimate(
            flops=4 * M * M * sum(widths),
            bytes_accessed=4 * M * sum(widths) + 4 * M * M,
            transcendentals=0,
        ),
    )(meta, gram, *matrices)
    result = []
    for send in sends:
        result.append(outs[: len(send[3])])
        outs = outs[len(send[3]) :]
    return result


def sum_tiles(meta, joined, turned, row_count, col_count):
    pair_count = row_count // 2
    tie = lax.optimization_barrier

    def over_cols(blocks):
        return [swap(blocks[k], "col", col_count, k) for k in range(1, col_count)]

    def over_pairs(blocks):
        return [swap(blocks[q], "row", row_count, 2 * q) for q in range(1, pair_count)]

    def halves(piece):
        got = swap(some_gram(meta, joined, turned, 1, piece), "row", row_count, 1)
        keep = some_gram(meta, joined, turned, 0, piece)
        return add_halves(meta, keep, got, col_count)

    early = halves(0)
    early, (joined, turned) = tie((early, (joined, turned)))
    early_in = over_cols(early)
    late = halves(1)
    late, early_in = tie((late, early_in))
    late_in = over_cols(late)
    early_parts = add_quarters(meta, [early[0]] + early_in, pair_count)
    early_in = over_pairs(early_parts)
    late_in, early_in = tie((late_in, early_in))
    early_part = add_parts(meta, [early_parts[0]] + early_in)
    early_in = over_pairs([early_part] * pair_count)
    late_parts = add_quarters(meta, [late[0]] + late_in, pair_count)
    late_parts, early_in = tie((late_parts, early_in))
    early_block = stack(meta, [early_part] + early_in)
    early_in = over_cols([early_block] * col_count)
    late_in = over_pairs(late_parts)
    late_part = add_parts(meta, [late_parts[0]] + late_in)
    late_in = over_pairs([late_part] * pair_count)
    late_in, early_in = tie((late_in, early_in))
    late_block = stack(meta, [late_part] + late_in)
    late_in = over_cols([late_block] * col_count)
    early = widen(meta, [early_block] + early_in)
    early_twin = swap(early, "row", row_count, 1)
    late = widen(meta, [late_block] + late_in)
    late_twin = swap(late, "row", row_count, 1)
    return [early, late, early_twin, late_twin]


def chunk_body(momentum_shards, shard_starts):
    col_count = lax.axis_size("col")
    row_count = lax.axis_size("row")
    pair_count = row_count // 2
    slots = momentum_shards.shape[0]
    mean_rows = M // (row_count * col_count)
    jitter = 4 * (mean_rows // 8)
    even = col_count * mean_rows
    window = even + 2 * jitter
    row = lax.axis_index("row").astype(jnp.int32)
    col = lax.axis_index("col").astype(jnp.int32)
    shard_ends = jnp.concatenate([shard_starts[1:], jnp.full((1,), M, jnp.int32)])
    members = row * col_count + (col ^ jnp.arange(col_count, dtype=jnp.int32))
    begins = shard_starts[members]
    meta = jnp.concatenate(
        [row[None], col[None], begins - (row * even - jitter), shard_ends[members] - begins]
    )

    wide = row_count * col_count * CHUNK
    number = (N // (row_count * col_count)) // CHUNK
    distances = list(range(pair_count))

    def fetch(base, span, steps, after):
        place, after = lax.optimization_barrier((col, after))
        received = [
            swap(
                lax.dynamic_slice_in_dim(
                    momentum_shards, base + (place ^ k) * span, span, axis=1
                ),
                "col",
                col_count,
                k,
            )
            for k in steps
        ]
        return received, after

    def across(pieces):
        return [pieces[0]] + [swap(pieces[q], "row", row_count, 2 * q) for q in distances[1:]]

    def gather_chunk(c, received):
        keep, give = pack_pair(
            meta, momentum_shards, received, c * wide, CHUNK, row_count, window
        )
        return join(meta, keep, swap(give, "row", row_count, 1), even, window, pair_count)

    half, span = col_count // 2, row_count * CHUNK
    received, _ = fetch(0, span, range(1, col_count), shard_starts)
    landed = []
    for c in range(1, number):
        some, received = fetch(c * wide, span, range(1, half + 1), received)
        joined = gather_chunk(c - 1, received)
        rest, (some, joined) = fetch(
            c * wide, span, range(half + 1, col_count), (some, joined)
        )
        crossed = across(joined)
        received = some + rest
        crossed[pair_count // 2], received = lax.optimization_barrier(
            (crossed[pair_count // 2], received)
        )
        landed.append(crossed)
    last, received = fetch(number * wide, pair_count * LAST, range(1, col_count), received)
    joined = gather_chunk(number - 1, received)
    joined, last, landed = lax.optimization_barrier((joined, last, landed))
    landed.append(across(joined))
    matrices = [
        merge(meta, pieces, [[q] for q in distances], 2 * even, 2, jitter) for pieces in landed
    ]
    pieces = pack(
        meta, momentum_shards, last, number * wide, LAST, 2, pair_count, window
    )
    stack = jnp.concatenate(across(pieces), axis=0)
    twin = swap(stack, "row", row_count, 1)
    matrices.append(
        merge(
            meta,
            [stack, twin],
            [[2 * q for q in distances], [2 * q + 1 for q in distances]],
            even,
            1,
            jitter,
        )
    )

    tiles = sum_tiles(meta, *collect(meta, matrices), row_count, col_count)

    sends = [(2 * even, 2, even + window, distances)] * number
    sends.append((even, 1, window, [2 * q for q in distances]))
    first, gram = first_apply(meta, tiles, matrices[0], sends[0], jitter)
    results = [first] + next_apply(meta, gram, matrices[1:], sends[1:], jitter)

    crossed = [across(results[0])]
    crossed[0], results[1:] = lax.optimization_barrier((crossed[0], results[1:]))
    crossed += [across(pieces) for pieces in results[1:]]
    backs = []
    for c in range(number + 1):
        if c < number:
            got = swap(cut(meta, crossed[c], even, window), "row", row_count, 1)
            parts = unpack_pair(meta, crossed[c], got, col_count, slots, even, window)
        else:
            parts = unpack(meta, crossed[c], col_count, slots, 2)
        back = [parts[0]] + [swap(parts[k], "col", col_count, k) for k in range(1, col_count)]
        if c + 1 < number:
            back, crossed[c + 1 :] = lax.optimization_barrier((back, crossed[c + 1 :]))
        backs.append(back)
    out = jnp.zeros(momentum_shards.shape, jnp.bfloat16)
    for c, back in enumerate(backs):
        span = row_count * CHUNK if c < number else pair_count * LAST
        for k in range(col_count):
            out = lax.dynamic_update_slice_in_dim(
                out, back[k], c * wide + (col ^ k) * span, axis=1
            )
    return out


def body(momentum_shards, shard_starts):
    devices = lax.axis_size("col") * lax.axis_size("row")
    chunks = (N // devices) % CHUNK == LAST // 2 and N // devices > CHUNK
    powers = all(lax.axis_size(a) & (lax.axis_size(a) - 1) == 0 for a in ("row", "col"))
    jitter = 4 * (M // devices // 8)
    if chunks and powers and jitter % 8 == 0:
        return chunk_body(momentum_shards, shard_starts)
    return plain_body(momentum_shards, shard_starts)


def solution(mesh):
    in_specs = (P(("row", "col"), None), P())
    out_specs = P(("row", "col"), None)
    return jax.shard_map(body, mesh=mesh, in_specs=in_specs, out_specs=out_specs, check_vma=False)
```

```python
import math

import jax
import jax.numpy as jnp
import numpy as np
from jax import lax
from jax.experimental import pallas as pl
from jax.experimental.pallas import tpu as pltpu
from jax.sharding import PartitionSpec as P

M = 3584
N = 18432
TILE = 512
BLOCKS = M // TILE

coef_one = 3.4445
coef_two = -4.775
coef_three = 2.0315

PAIRS = [(i, j) for i in range(BLOCKS) for j in range(i, BLOCKS)]
PAIR_ROWS = np.array([i for i, _ in PAIRS], np.int32)
PAIR_COLS = np.array([j for _, j in PAIRS], np.int32)


def packing(shard_starts, row_block, col_count, shard_rows, window, first_row):
    shard_ends = jnp.concatenate([shard_starts[1:], jnp.full((1,), M, jnp.int32)])
    first_starts = lax.dynamic_slice_in_dim(shard_starts, row_block * col_count, col_count)
    last_ends = lax.dynamic_slice_in_dim(shard_ends, row_block * col_count, col_count)
    slot_index = jnp.arange(col_count * shard_rows, dtype=jnp.int32)
    member = slot_index // shard_rows
    offset = slot_index % shard_rows
    pick = member[:, None] == jnp.arange(col_count, dtype=jnp.int32)[None, :]
    shard_begin = jnp.sum(jnp.where(pick, first_starts[None, :], 0), axis=1)
    length = jnp.sum(jnp.where(pick, (last_ends - first_starts)[None, :], 0), axis=1)
    target = shard_begin - first_row + offset
    is_valid = offset < length
    window_rows = jnp.arange(window, dtype=jnp.int32)
    return ((window_rows[:, None] == target[None, :]) & is_valid[None, :]).astype(jnp.bfloat16)


def gram_kernel(rows_ref, cols_ref, left_ref, right_ref, out_ref):
    out_ref[...] = lax.dot_general(
        left_ref[...], right_ref[...], (((1,), (1,)), ((), ())), preferred_element_type=jnp.float32
    ).astype(jnp.bfloat16)


def gram_tiles(matrix):
    width = matrix.shape[1]
    count = len(PAIRS)
    return pl.pallas_call(
        gram_kernel,
        out_shape=jax.ShapeDtypeStruct((count * TILE, TILE), jnp.bfloat16),
        grid_spec=pltpu.PrefetchScalarGridSpec(
            num_scalar_prefetch=2,
            grid=(count,),
            in_specs=[
                pl.BlockSpec((TILE, width), lambda p, rows, cols: (rows[p], 0)),
                pl.BlockSpec((TILE, width), lambda p, rows, cols: (cols[p], 0)),
            ],
            out_specs=pl.BlockSpec((TILE, TILE), lambda p, rows, cols: (p, 0)),
        ),
        compiler_params=pltpu.CompilerParams(vmem_limit_bytes=32 * 1024 * 1024),
        cost_estimate=pl.CostEstimate(
            flops=2 * count * TILE * TILE * width,
            bytes_accessed=2 * count * TILE * (TILE + width),
            transcendentals=0,
        ),
    )(jnp.asarray(PAIR_ROWS), jnp.asarray(PAIR_COLS), matrix, matrix)


def apply_kernel(rows_ref, cols_ref, tile_ref, matrix_ref, out_ref, total, factor):
    turn = pl.program_id(0)
    pair = pl.program_id(1)
    i = rows_ref[pair]
    j = cols_ref[pair]
    here = pl.ds(pl.multiple_of(i * TILE, TILE), TILE)
    there = pl.ds(pl.multiple_of(j * TILE, TILE), TILE)

    @pl.when((turn == 0) & (pair == 0))
    def _():
        total[...] = jnp.zeros_like(total)
        factor[...] = matrix_ref[...]

    @pl.when((turn == 1) & (pair == 0))
    def _():
        @pl.loop(0, BLOCKS)
        def _(b):
            part = pl.ds(pl.multiple_of(b * TILE, TILE), TILE)
            product = total[part, :]
            factor[part, :] = (coef_three * product).astype(jnp.bfloat16)
            total[part, :] = coef_one * matrix_ref[part, :].astype(jnp.float32) + coef_two * product

    total[here, :] += jnp.dot(tile_ref[...], factor[there, :], preferred_element_type=jnp.float32)

    @pl.when(i != j)
    def _():
        total[there, :] += lax.dot_general(
            tile_ref[...], factor[here, :], (((0,), (0,)), ((), ())), preferred_element_type=jnp.float32
        )

    @pl.when((turn == 1) & (pair == pl.num_programs(1) - 1))
    def _():
        @pl.loop(0, BLOCKS)
        def _(b):
            part = pl.ds(pl.multiple_of(b * TILE, TILE), TILE)
            out_ref[part, :] = (math.sqrt(N) * total[part, :]).astype(jnp.bfloat16)


def apply_polynomial(tiles, matrix):
    rows, width = matrix.shape
    count = len(PAIRS)
    return pl.pallas_call(
        apply_kernel,
        out_shape=jax.ShapeDtypeStruct((rows, width), jnp.bfloat16),
        grid_spec=pltpu.PrefetchScalarGridSpec(
            num_scalar_prefetch=2,
            grid=(2, count),
            in_specs=[
                pl.BlockSpec((TILE, TILE), lambda t, p, rows, cols: (p, 0)),
                pl.BlockSpec((rows, width), lambda t, p, rows, cols: (0, 0)),
            ],
            out_specs=pl.BlockSpec((rows, width), lambda t, p, rows, cols: (0, 0)),
            scratch_shapes=[
                pltpu.VMEM((rows, width), jnp.float32),
                pltpu.VMEM((rows, width), jnp.bfloat16),
            ],
        ),
        compiler_params=pltpu.CompilerParams(vmem_limit_bytes=48 * 1024 * 1024),
        cost_estimate=pl.CostEstimate(
            flops=4 * rows * rows * width,
            bytes_accessed=4 * rows * width + 4 * count * TILE * TILE,
            transcendentals=0,
        ),
    )(jnp.asarray(PAIR_ROWS), jnp.asarray(PAIR_COLS), tiles, matrix)


def plain_body(momentum_shards, shard_starts):
    col_count = lax.axis_size("col")
    row_count = lax.axis_size("row")
    shard_rows = momentum_shards.shape[0]
    mean_rows = M // (row_count * col_count)
    jitter = 4 * (mean_rows // 8)
    even = col_count * mean_rows
    window = even + 2 * jitter
    row_block = lax.axis_index("row")
    packer = packing(
        shard_starts, row_block, col_count, shard_rows, window, row_block * even - jitter
    )
    columns = lax.all_to_all(momentum_shards, "col", split_axis=1, concat_axis=0, tiled=True)
    local_tile = jnp.dot(packer, columns, preferred_element_type=jnp.float32).astype(jnp.bfloat16)
    windows = lax.all_to_all(local_tile, "row", split_axis=1, concat_axis=0, tiled=True)
    width = windows.shape[1]
    windows = windows.reshape(row_count, window, width)
    nothing = jnp.zeros((1, jitter, width), jnp.bfloat16)
    head = jnp.concatenate([nothing, windows[:-1, jitter + even :]], axis=0)
    tail = jnp.concatenate([windows[1:, :jitter], nothing], axis=0)
    middle = windows[:, jitter : jitter + even]
    matrix = jnp.concatenate(
        [
            middle[:, :jitter] + head,
            middle[:, jitter : even - jitter],
            middle[:, even - jitter :] + tail,
        ],
        axis=1,
    ).reshape(M, width)

    tiles = lax.psum(gram_tiles(matrix), ("row", "col"))
    update = apply_polynomial(tiles, matrix).reshape(row_count, even, width)

    before = jnp.concatenate([nothing, update[:-1, even - jitter :]], axis=0)
    after = jnp.concatenate([update[1:, :jitter], nothing], axis=0)
    spread = jnp.concatenate([before, update, after], axis=1).reshape(row_count * window, width)
    own_rows = lax.all_to_all(spread, "row", split_axis=0, concat_axis=1, tiled=True)
    back_rows = lax.dot_general(
        packer, own_rows, (((0,), (0,)), ((), ())), preferred_element_type=jnp.float32
    ).astype(jnp.bfloat16)
    return lax.all_to_all(back_rows, "col", split_axis=0, concat_axis=1, tiled=True)


CHUNK = 256
LAST = 128
VMEM_LIMIT = 56 * 1024 * 1024


def swap(value, axis, size, distance):
    return lax.ppermute(value, axis, perm=[(i, i ^ distance) for i in range(size)])


def pack_kernel(step, col_count, meta_ref, *refs):
    pieces, outs, choose = refs[:col_count], refs[col_count:-1], refs[-1]
    turn = pl.program_id(0)
    _, window, slots = choose.shape

    @pl.when(turn == 0)
    def _():
        rows = lax.broadcasted_iota(jnp.int32, (window, slots), 0)
        columns = lax.broadcasted_iota(jnp.int32, (window, slots), 1)
        for k in range(col_count):
            hit = (rows == columns + meta_ref[2 + k]) & (columns < meta_ref[2 + col_count + k])
            choose[k] = jnp.where(hit, 1.0, 0.0).astype(jnp.bfloat16)

    total = jnp.dot(choose[0], pieces[0][...], preferred_element_type=jnp.float32)
    for k in range(1, col_count):
        total += jnp.dot(choose[k], pieces[k][...], preferred_element_type=jnp.float32)
    for q, out in enumerate(outs):

        @pl.when(turn == q)
        def _():
            out[...] = total.astype(jnp.bfloat16)


def pack(meta, momentum, received, base, width, step, count, window):
    slots = momentum.shape[0]
    col_count = len(received) + 1
    first = base // width
    return pl.pallas_call(
        lambda *refs: pack_kernel(step, col_count, *refs),
        out_shape=[jax.ShapeDtypeStruct((window, width), jnp.bfloat16)] * count,
        grid_spec=pltpu.PrefetchScalarGridSpec(
            num_scalar_prefetch=1,
            grid=(count,),
            in_specs=[
                pl.BlockSpec(
                    (slots, width),
                    lambda q, meta: (0, first + meta[1] * count + ((meta[0] // step) ^ q)),
                )
            ]
            + [pl.BlockSpec((slots, width), lambda q, meta: (0, (meta[0] // step) ^ q))]
            * (col_count - 1),
            out_specs=[pl.BlockSpec((window, width), lambda q, meta: (0, 0))] * count,
            scratch_shapes=[pltpu.VMEM((col_count, window, slots), jnp.bfloat16)],
        ),
        compiler_params=pltpu.CompilerParams(vmem_limit_bytes=VMEM_LIMIT),
        cost_estimate=pl.CostEstimate(
            flops=2 * window * slots * col_count * width * count,
            bytes_accessed=2 * count * width * (slots * col_count + window),
            transcendentals=0,
        ),
    )(meta, momentum, *received)


def pack_pair_kernel(col_count, meta_ref, *refs):
    pieces, keep, give, choose = refs[:col_count], refs[col_count], refs[col_count + 1], refs[-1]
    other = pl.program_id(0) == 0
    _, window, slots = choose.shape

    @pl.when(other & (pl.program_id(1) == 0))
    def _():
        fill_choose(meta_ref, choose, 0)

    total = jnp.dot(choose[0], pieces[0][...], preferred_element_type=jnp.float32)
    for k in range(1, col_count):
        total += jnp.dot(choose[k], pieces[k][...], preferred_element_type=jnp.float32)

    @pl.when(other)
    def _():
        give[...] = total.astype(jnp.bfloat16)

    @pl.when(jnp.logical_not(other))
    def _():
        keep[...] = total.astype(jnp.bfloat16)


def fill_choose(meta_ref, choose, slot_axis):
    col_count = choose.shape[0]
    shape = choose.shape[1:]
    rows = lax.broadcasted_iota(jnp.int32, shape, slot_axis)
    slots = lax.broadcasted_iota(jnp.int32, shape, 1 - slot_axis)
    for k in range(col_count):
        hit = (rows == slots + meta_ref[2 + k]) & (slots < meta_ref[2 + col_count + k])
        choose[k] = jnp.where(hit, 1.0, 0.0).astype(jnp.bfloat16)


def pack_pair(meta, momentum, received, base, width, row_count, window):
    slots = momentum.shape[0]
    col_count = len(received) + 1
    pairs = row_count // 2
    first = base // width
    block = lambda e, q, meta: meta[0] ^ (2 * q + 1 - e)
    shape = jax.ShapeDtypeStruct((pairs * window, width), jnp.bfloat16)
    return pl.pallas_call(
        lambda *refs: pack_pair_kernel(col_count, *refs),
        out_shape=[shape, shape],
        grid_spec=pltpu.PrefetchScalarGridSpec(
            num_scalar_prefetch=1,
            grid=(2, pairs),
            in_specs=[
                pl.BlockSpec(
                    (slots, width),
                    lambda e, q, meta: (0, first + meta[1] * row_count + block(e, q, meta)),
                )
            ]
            + [pl.BlockSpec((slots, width), lambda e, q, meta: (0, block(e, q, meta)))]
            * (col_count - 1),
            out_specs=[
                pl.BlockSpec((window, width), lambda e, q, meta: (jnp.where(e == 0, 0, q), 0)),
                pl.BlockSpec(
                    (window, width), lambda e, q, meta: (jnp.where(e == 0, q, pairs - 1), 0)
                ),
            ],
            scratch_shapes=[pltpu.VMEM((col_count, window, slots), jnp.bfloat16)],
        ),
        compiler_params=pltpu.CompilerParams(vmem_limit_bytes=VMEM_LIMIT),
        cost_estimate=pl.CostEstimate(
            flops=2 * window * slots * col_count * width * row_count,
            bytes_accessed=2 * row_count * width * (slots * col_count + window),
            transcendentals=0,
        ),
    )(meta, momentum, *received)


def join_kernel(even, window, meta_ref, keep, got, *outs):
    def write(low, high):
        for q, out in enumerate(outs):
            base = q * window
            lap = window - even
            out[:even, :] = low[base : base + even, :]
            out[even:window, :] = (
                low[base + even : base + window, :].astype(jnp.float32)
                + high[base : base + lap, :].astype(jnp.float32)
            ).astype(jnp.bfloat16)
            out[window:, :] = high[base + lap : base + window, :]

    @pl.when(meta_ref[0] % 2 == 0)
    def _():
        write(keep, got)

    @pl.when(meta_ref[0] % 2 == 1)
    def _():
        write(got, keep)


def local_call(kernel, out_shape, operands, moved, scratch=()):
    whole = pl.BlockSpec(memory_space=pltpu.VMEM)
    return pl.pallas_call(
        kernel,
        out_shape=out_shape,
        in_specs=[pl.BlockSpec(memory_space=pltpu.SMEM)] + [whole] * (len(operands) - 1),
        out_specs=jax.tree.map(lambda _: whole, out_shape),
        scratch_shapes=list(scratch),
        compiler_params=pltpu.CompilerParams(vmem_limit_bytes=VMEM_LIMIT),
        cost_estimate=pl.CostEstimate(flops=moved, bytes_accessed=moved, transcendentals=0),
    )(*operands)


def join(meta, keep, got, even, window, pairs):
    width = keep.shape[1]
    shape = jax.ShapeDtypeStruct((even + window, width), jnp.bfloat16)
    return local_call(
        lambda *refs: join_kernel(even, window, *refs),
        [shape] * pairs,
        (meta, keep, got),
        8 * pairs * window * width,
    )


def cut_kernel(even, window, meta_ref, *refs):
    pieces, out = refs[:-1], refs[-1]
    place = pl.ds(pl.multiple_of((1 - meta_ref[0] % 2) * even, 16), window)
    for q, piece in enumerate(pieces):
        out[q * window : (q + 1) * window, :] = piece[place, :]


def cut(meta, pieces, even, window):
    width = pieces[0].shape[1]
    return local_call(
        lambda *refs: cut_kernel(even, window, *refs),
        jax.ShapeDtypeStruct((len(pieces) * window, width), jnp.bfloat16),
        (meta, *pieces),
        4 * len(pieces) * window * width,
    )


def unpack_pair_kernel(col_count, even, window, meta_ref, *refs):
    got, outs, choose = refs[-2 - col_count], refs[-1 - col_count : -1], refs[-1]
    pieces = refs[: -2 - col_count]
    turn = pl.program_id(0)

    @pl.when(turn == 0)
    def _():
        fill_choose(meta_ref, choose, 1)

    def place(block):
        for k in range(col_count):
            outs[k][...] = jnp.dot(
                choose[k], block, preferred_element_type=jnp.float32
            ).astype(jnp.bfloat16)

    for q, piece in enumerate(pieces):

        @pl.when(turn == 2 * q)
        def _():
            own = pl.ds(pl.multiple_of(meta_ref[0] % 2 * even, 16), window)
            place(piece[own, :])

    @pl.when(turn % 2 == 1)
    def _():
        part = pl.ds(pl.multiple_of(turn // 2 * window, 16), window)
        place(got[part, :])


def unpack_pair(meta, pieces, got, col_count, slots, even, window):
    width = got.shape[1]
    count = 2 * len(pieces)
    return pl.pallas_call(
        lambda *refs: unpack_pair_kernel(col_count, even, window, *refs),
        out_shape=[jax.ShapeDtypeStruct((slots, count * width), jnp.bfloat16)] * col_count,
        grid_spec=pltpu.PrefetchScalarGridSpec(
            num_scalar_prefetch=1,
            grid=(count,),
            in_specs=[pl.BlockSpec(x.shape, lambda q, meta: (0, 0)) for x in (*pieces, got)],
            out_specs=[pl.BlockSpec((slots, width), lambda q, meta: (0, meta[0] ^ q))]
            * col_count,
            scratch_shapes=[pltpu.VMEM((col_count, slots, window), jnp.bfloat16)],
        ),
        compiler_params=pltpu.CompilerParams(vmem_limit_bytes=VMEM_LIMIT),
        cost_estimate=pl.CostEstimate(
            flops=2 * window * slots * col_count * width * count,
            bytes_accessed=2 * count * width * (slots * col_count + window),
            transcendentals=0,
        ),
    )(meta, *pieces, got)


def unpack_kernel(col_count, meta_ref, *refs):
    pieces, outs, choose = refs[: -1 - col_count], refs[-1 - col_count : -1], refs[-1]
    turn = pl.program_id(0)
    _, slots, window = choose.shape

    @pl.when(turn == 0)
    def _():
        rows = lax.broadcasted_iota(jnp.int32, (slots, window), 1)
        columns = lax.broadcasted_iota(jnp.int32, (slots, window), 0)
        for k in range(col_count):
            hit = (rows == columns + meta_ref[2 + k]) & (columns < meta_ref[2 + col_count + k])
            choose[k] = jnp.where(hit, 1.0, 0.0).astype(jnp.bfloat16)

    for q, piece in enumerate(pieces):

        @pl.when(turn == q)
        def _():
            for k in range(col_count):
                outs[k][...] = jnp.dot(
                    choose[k], piece[...], preferred_element_type=jnp.float32
                ).astype(jnp.bfloat16)


def unpack(meta, pieces, col_count, slots, step):
    window, width = pieces[0].shape
    count = len(pieces)
    return pl.pallas_call(
        lambda *refs: unpack_kernel(col_count, *refs),
        out_shape=[jax.ShapeDtypeStruct((slots, count * width), jnp.bfloat16)] * col_count,
        grid_spec=pltpu.PrefetchScalarGridSpec(
            num_scalar_prefetch=1,
            grid=(count,),
            in_specs=[pl.BlockSpec((window, width), lambda q, meta: (0, 0))] * count,
            out_specs=[pl.BlockSpec((slots, width), lambda q, meta: (0, (meta[0] // step) ^ q))]
            * col_count,
            scratch_shapes=[pltpu.VMEM((col_count, slots, window), jnp.bfloat16)],
        ),
        compiler_params=pltpu.CompilerParams(vmem_limit_bytes=VMEM_LIMIT),
        cost_estimate=pl.CostEstimate(
            flops=2 * window * slots * col_count * width * count,
            bytes_accessed=2 * count * width * (slots * col_count + window),
            transcendentals=0,
        ),
    )(meta, *pieces)


def merge_kernel(unit, share, distances, meta_ref, *refs):
    pieces, out_ref, total = refs[:-2], refs[-2], refs[-1]
    jitter = (total.shape[0] - M) // 2
    total[...] = jnp.zeros_like(total)
    for places, piece in zip(distances, pieces):
        rows = piece.shape[0] // len(places)
        for n, distance in enumerate(places):
            place = pl.ds(pl.multiple_of(((meta_ref[0] // share) ^ distance) * unit, 8), rows)
            total[place, :] += piece[n * rows : (n + 1) * rows, :].astype(jnp.float32)

    @pl.loop(0, BLOCKS)
    def _(b):
        source = pl.ds(pl.multiple_of(b * TILE + jitter, 8), TILE)
        out_ref[tile_rows(b), :] = total[source, :].astype(jnp.bfloat16)


def merge(meta, pieces, distances, unit, share, jitter):
    width = pieces[0].shape[1]
    return local_call(
        lambda *refs: merge_kernel(unit, share, distances, *refs),
        jax.ShapeDtypeStruct((M, width), jnp.bfloat16),
        (meta, *pieces),
        5 * M * width,
        [pltpu.VMEM((M + 2 * jitter, width), jnp.float32)],
    )


def collect_kernel(meta_ref, *refs):
    matrices, joined = refs[:-1], refs[-1]
    place = 0
    for matrix in matrices[:-1]:
        joined[:, place : place + matrix.shape[1]] = matrix[...]
        place += matrix.shape[1]
    lane = lax.broadcasted_iota(jnp.int32, (TILE, LAST), 1)
    own = lane // (LAST // 2) == meta_ref[0] % 2

    @pl.loop(0, BLOCKS)
    def _(b):
        block = matrices[-1][tile_rows(b), :].astype(jnp.float32)
        joined[tile_rows(b), place:] = jnp.where(own, block, 0.0).astype(jnp.bfloat16)


def collect(meta, chunks):
    width = sum(x.shape[1] for x in chunks)
    return local_call(
        collect_kernel,
        jax.ShapeDtypeStruct((M, width), jnp.bfloat16),
        (meta, *chunks),
        4 * M * width,
    )


PIECES = 2
HALF = len(PAIRS) // 2
PART = HALF // PIECES


def half_gram_kernel(flip, rows_ref, cols_ref, meta_ref, joined, *outs):
    turn = pl.program_id(0)
    pair = (meta_ref[0] % 2 ^ flip) * HALF + turn
    here = pl.ds(pl.multiple_of(rows_ref[pair] * TILE, TILE), TILE)
    there = pl.ds(pl.multiple_of(cols_ref[pair] * TILE, TILE), TILE)
    tile = lax.dot_general(
        joined[here, :],
        joined[there, :],
        (((1,), (1,)), ((), ())),
        preferred_element_type=jnp.float32,
    ).astype(jnp.bfloat16)
    for n, out in enumerate(outs):

        @pl.when(turn // PART == n)
        def _():
            out[...] = tile


def half_gram(meta, joined, flip):
    width = joined.shape[1]
    place = lambda n: lambda p, rows, cols, meta: (jnp.clip(p - n * PART, 0, PART - 1), 0)
    return pl.pallas_call(
        lambda *refs: half_gram_kernel(flip, *refs),
        out_shape=[jax.ShapeDtypeStruct((PART * TILE, TILE), jnp.bfloat16)] * PIECES,
        grid_spec=pltpu.PrefetchScalarGridSpec(
            num_scalar_prefetch=3,
            grid=(HALF,),
            in_specs=[pl.BlockSpec((M, width), lambda p, rows, cols, meta: (0, 0))],
            out_specs=[pl.BlockSpec((TILE, TILE), place(n)) for n in range(PIECES)],
        ),
        compiler_params=pltpu.CompilerParams(vmem_limit_bytes=VMEM_LIMIT),
        cost_estimate=pl.CostEstimate(
            flops=2 * HALF * TILE * TILE * width,
            bytes_accessed=2 * HALF * TILE * TILE + 2 * M * width,
            transcendentals=0,
        ),
    )(jnp.asarray(PAIR_ROWS), jnp.asarray(PAIR_COLS), meta, joined)


def lane_block(block, lanes):
    return pl.ds(pl.multiple_of(block * lanes, lanes), lanes)


def add_halves_kernel(meta_ref, keep, got, *outs):
    lanes = outs[0].shape[1]
    for k, out in enumerate(outs):
        part = lane_block(meta_ref[1] ^ k, lanes)
        out[...] = (keep[:, part].astype(jnp.float32) + got[:, part].astype(jnp.float32)).astype(
            jnp.bfloat16
        )


def gridded(kernel, meta, operands, outs, moved):
    rows = operands[0].shape[0]
    block = lambda x: pl.BlockSpec((TILE, x.shape[1]), lambda t, meta: (t, 0))
    return pl.pallas_call(
        kernel,
        out_shape=outs,
        grid_spec=pltpu.PrefetchScalarGridSpec(
            num_scalar_prefetch=1,
            grid=(rows // TILE,),
            in_specs=[block(x) for x in operands],
            out_specs=jax.tree.map(block, outs),
        ),
        compiler_params=pltpu.CompilerParams(vmem_limit_bytes=VMEM_LIMIT),
        cost_estimate=pl.CostEstimate(flops=moved, bytes_accessed=moved, transcendentals=0),
    )(meta, *operands)


def add_halves(meta, keep, got, col_count):
    rows, lanes = keep.shape
    shape = jax.ShapeDtypeStruct((rows, lanes // col_count), jnp.bfloat16)
    return gridded(add_halves_kernel, meta, (keep, got), [shape] * col_count, 6 * rows * lanes)


def total_of(refs, part):
    total = refs[0][part, :].astype(jnp.float32)
    for ref in refs[1:]:
        total += ref[part, :].astype(jnp.float32)
    return total.astype(jnp.bfloat16)


def add_quarters_kernel(col_count, meta_ref, *refs):
    blocks, outs = refs[:col_count], refs[col_count:]
    rows = outs[0].shape[0]
    for q, out in enumerate(outs):
        place = (meta_ref[0] // 2 ^ q) * rows
        out[...] = total_of(blocks, pl.ds(pl.multiple_of(place, rows), rows))


def add_quarters(meta, blocks, pair_count):
    rows, lanes = blocks[0].shape
    shape = jax.ShapeDtypeStruct((rows // pair_count, lanes), jnp.bfloat16)
    return local_call(
        lambda *refs: add_quarters_kernel(len(blocks), *refs),
        [shape] * pair_count,
        (meta, *blocks),
        10 * rows * lanes,
    )


def add_parts_kernel(meta_ref, *refs):
    rows = refs[-1].shape[0]
    refs[-1][...] = total_of(refs[:-1], pl.ds(0, rows))


def add_parts(meta, parts):
    return local_call(
        add_parts_kernel,
        jax.ShapeDtypeStruct(parts[0].shape, jnp.bfloat16),
        (meta, *parts),
        10 * parts[0].size,
    )


def stack_kernel(meta_ref, *refs):
    parts, out = refs[:-1], refs[-1]
    rows = parts[0].shape[0]
    for q, part in enumerate(parts):
        out[pl.ds(pl.multiple_of((meta_ref[0] // 2 ^ q) * rows, rows), rows), :] = part[...]


def stack(meta, parts):
    rows, lanes = parts[0].shape
    return local_call(
        stack_kernel,
        jax.ShapeDtypeStruct((rows * len(parts), lanes), jnp.bfloat16),
        (meta, *parts),
        4 * rows * lanes * len(parts),
    )


def widen_kernel(meta_ref, *refs):
    blocks, out = refs[:-1], refs[-1]
    for k, block in enumerate(blocks):
        out[:, lane_block(meta_ref[1] ^ k, block.shape[1])] = block[...]


def widen(meta, blocks):
    rows, lanes = blocks[0].shape
    shape = jax.ShapeDtypeStruct((rows, lanes * len(blocks)), jnp.bfloat16)
    return gridded(widen_kernel, meta, blocks, shape, 4 * rows * lanes * len(blocks))


def tile_rows(b):
    return pl.ds(pl.multiple_of(b * TILE, TILE), TILE)


def first_product(panel, b, jitter, matrix, total, factor):
    product = jnp.dot(panel, matrix[...], preferred_element_type=jnp.float32)
    factor[tile_rows(b), :] = (coef_three * product).astype(jnp.bfloat16)
    total[pl.ds(pl.multiple_of(b * TILE + jitter, 8), TILE), :] = (
        coef_one * matrix[tile_rows(b), :].astype(jnp.float32) + coef_two * product
    )


def second_product(panel, b, jitter, total, factor):
    place = pl.ds(pl.multiple_of(b * TILE + jitter, 8), TILE)
    total[place, :] = math.sqrt(N) * (
        total[place, :] + jnp.dot(panel, factor[...], preferred_element_type=jnp.float32)
    )


def clear_edges(total, jitter):
    edge = jnp.zeros((jitter, total.shape[1]), jnp.float32)
    total[pl.ds(0, jitter), :] = edge
    total[pl.ds(M + jitter, jitter), :] = edge


def store_windows(row, send, total, outs):
    unit, share, rows, distances = send
    for distance, out in zip(distances, outs):
        place = pl.ds(pl.multiple_of(((row // share) ^ distance) * unit, 8), rows)
        out[...] = total[place, :].astype(jnp.bfloat16)


def first_apply_kernel(jitter, send, rows_ref, cols_ref, meta_ref, *refs):
    pieces, matrix = refs[: 2 * PIECES], refs[2 * PIECES]
    outs, gram_out = refs[2 * PIECES + 1 : -6], refs[-6]
    gram, total, factor, tile_sems, out_sem = refs[-5:]
    copies = []
    for n in range(2 * HALF):
        half, part = divmod(n, HALF)
        pair = (meta_ref[0] % 2 ^ half) * HALF + part
        i, j = rows_ref[pair], cols_ref[pair]
        copy = pltpu.make_async_copy(
            pieces[half * PIECES + part // PART].at[pl.ds(part % PART * TILE, TILE), :],
            gram.at[i, :, lane_block(j, TILE)],
            tile_sems.at[n],
        )
        copy.start()
        copies.append((copy, i, j))
    clear_edges(total, jitter)
    for copy, i, j in copies:
        copy.wait()

        @pl.when(i != j)
        def _():
            gram[j, :, lane_block(i, TILE)] = gram[i, :, lane_block(j, TILE)].T

    back = pltpu.make_async_copy(gram, gram_out, out_sem)
    back.start()

    @pl.loop(0, BLOCKS)
    def _(b):
        first_product(gram[b], b, jitter, matrix, total, factor)

    @pl.loop(0, BLOCKS)
    def _(b):
        second_product(gram[b], b, jitter, total, factor)

    store_windows(meta_ref[0], send, total, outs)
    back.wait()


def first_apply(meta, pieces, matrix, send, jitter):
    width = matrix.shape[1]
    whole = pl.BlockSpec(memory_space=pltpu.VMEM)
    outs = pl.pallas_call(
        lambda *refs: first_apply_kernel(jitter, send, *refs),
        out_shape=[jax.ShapeDtypeStruct((send[2], width), jnp.bfloat16)] * len(send[3])
        + [jax.ShapeDtypeStruct((BLOCKS, TILE, M), jnp.bfloat16)],
        in_specs=[pl.BlockSpec(memory_space=pltpu.SMEM)] * 3
        + [pl.BlockSpec(memory_space=pl.ANY)] * len(pieces)
        + [whole],
        out_specs=[whole] * len(send[3]) + [pl.BlockSpec(memory_space=pl.ANY)],
        scratch_shapes=[
            pltpu.VMEM((BLOCKS, TILE, M), jnp.bfloat16),
            pltpu.VMEM((M + 2 * jitter, width), jnp.float32),
            pltpu.VMEM((M, width), jnp.bfloat16),
            pltpu.SemaphoreType.DMA((len(PAIRS),)),
            pltpu.SemaphoreType.DMA,
        ],
        compiler_params=pltpu.CompilerParams(vmem_limit_bytes=VMEM_LIMIT),
        cost_estimate=pl.CostEstimate(
            flops=4 * M * M * width, bytes_accessed=4 * M * width + 4 * M * M, transcendentals=0
        ),
    )(jnp.asarray(PAIR_ROWS), jnp.asarray(PAIR_COLS), meta, *pieces, matrix)
    return outs[:-1], outs[-1]


def next_apply_kernel(jitter, sends, meta_ref, panel_ref, *refs):
    chunks = len(sends)
    outs_count = sum(len(s[3]) for s in sends)
    matrices = refs[:chunks]
    outs = refs[chunks : chunks + outs_count]
    totals = refs[chunks + outs_count : 2 * chunks + outs_count]
    factors = refs[2 * chunks + outs_count :]
    turn = pl.program_id(0)

    @pl.when(turn < BLOCKS)
    def _():
        for matrix, total, factor in zip(matrices, totals, factors):
            first_product(panel_ref[0], turn, jitter, matrix, total, factor)

    @pl.when(turn >= BLOCKS)
    def _():
        for total, factor in zip(totals, factors):
            second_product(panel_ref[0], turn - BLOCKS, jitter, total, factor)

    @pl.when(turn == 2 * BLOCKS - 1)
    def _():
        place = 0
        for total, send in zip(totals, sends):
            clear_edges(total, jitter)
            store_windows(meta_ref[0], send, total, outs[place : place + len(send[3])])
            place += len(send[3])


def next_apply(meta, gram, matrices, sends, jitter):
    widths = [x.shape[1] for x in matrices]
    shapes = [(send[2], width) for width, send in zip(widths, sends) for _ in send[3]]
    whole = lambda t, meta: (0, 0)
    outs = pl.pallas_call(
        lambda *refs: next_apply_kernel(jitter, sends, *refs),
        out_shape=[jax.ShapeDtypeStruct(shape, jnp.bfloat16) for shape in shapes],
        grid_spec=pltpu.PrefetchScalarGridSpec(
            num_scalar_prefetch=1,
            grid=(2 * BLOCKS,),
            in_specs=[pl.BlockSpec((1, TILE, M), lambda t, meta: (t % BLOCKS, 0, 0))]
            + [pl.BlockSpec((M, width), whole) for width in widths],
            out_specs=[pl.BlockSpec(shape, whole) for shape in shapes],
            scratch_shapes=[pltpu.VMEM((M + 2 * jitter, width), jnp.float32) for width in widths]
            + [pltpu.VMEM((M, width), jnp.bfloat16) for width in widths],
        ),
        compiler_params=pltpu.CompilerParams(vmem_limit_bytes=VMEM_LIMIT),
        cost_estimate=pl.CostEstimate(
            flops=4 * M * M * sum(widths),
            bytes_accessed=4 * M * sum(widths) + 4 * M * M,
            transcendentals=0,
        ),
    )(meta, gram, *matrices)
    result = []
    for send in sends:
        result.append(outs[: len(send[3])])
        outs = outs[len(send[3]) :]
    return result


def sum_tiles(meta, joined, row_count, col_count):
    pair_count = row_count // 2
    tie = lax.optimization_barrier

    def over_cols(blocks):
        return [swap(blocks[k], "col", col_count, k) for k in range(1, col_count)]

    def over_pairs(blocks):
        return [swap(blocks[q], "row", row_count, 2 * q) for q in range(1, pair_count)]

    give = half_gram(meta, joined, 1)
    got = [swap(piece, "row", row_count, 1) for piece in give]
    keep = half_gram(meta, joined, 0)

    early = add_halves(meta, keep[0], got[0], col_count)
    early_in = over_cols(early)
    late = add_halves(meta, keep[1], got[1], col_count)
    late, early_in = tie((late, early_in))
    late_in = over_cols(late)
    early_parts = add_quarters(meta, [early[0]] + early_in, pair_count)
    early_in = over_pairs(early_parts)
    late_in, early_in = tie((late_in, early_in))
    early_part = add_parts(meta, [early_parts[0]] + early_in)
    early_in = over_pairs([early_part] * pair_count)
    late_parts = add_quarters(meta, [late[0]] + late_in, pair_count)
    late_parts, early_in = tie((late_parts, early_in))
    early_block = stack(meta, [early_part] + early_in)
    early_in = over_cols([early_block] * col_count)
    late_in = over_pairs(late_parts)
    late_part = add_parts(meta, [late_parts[0]] + late_in)
    late_in = over_pairs([late_part] * pair_count)
    late_in, early_in = tie((late_in, early_in))
    late_block = stack(meta, [late_part] + late_in)
    late_in = over_cols([late_block] * col_count)
    early = widen(meta, [early_block] + early_in)
    early_twin = swap(early, "row", row_count, 1)
    late = widen(meta, [late_block] + late_in)
    late_twin = swap(late, "row", row_count, 1)
    return [early, late, early_twin, late_twin]


def chunk_body(momentum_shards, shard_starts):
    col_count = lax.axis_size("col")
    row_count = lax.axis_size("row")
    pair_count = row_count // 2
    slots = momentum_shards.shape[0]
    mean_rows = M // (row_count * col_count)
    jitter = 4 * (mean_rows // 8)
    even = col_count * mean_rows
    window = even + 2 * jitter
    row = lax.axis_index("row").astype(jnp.int32)
    col = lax.axis_index("col").astype(jnp.int32)
    shard_ends = jnp.concatenate([shard_starts[1:], jnp.full((1,), M, jnp.int32)])
    members = row * col_count + (col ^ jnp.arange(col_count, dtype=jnp.int32))
    begins = shard_starts[members]
    meta = jnp.concatenate(
        [row[None], col[None], begins - (row * even - jitter), shard_ends[members] - begins]
    )

    wide = row_count * col_count * CHUNK
    number = (N // (row_count * col_count)) // CHUNK
    distances = list(range(pair_count))

    def fetch(base, span, after):
        place, after = lax.optimization_barrier((col, after))
        received = [
            swap(
                lax.dynamic_slice_in_dim(
                    momentum_shards, base + (place ^ k) * span, span, axis=1
                ),
                "col",
                col_count,
                k,
            )
            for k in range(1, col_count)
        ]
        return received, after

    def across(pieces):
        return [pieces[0]] + [swap(pieces[q], "row", row_count, 2 * q) for q in distances[1:]]

    far_first = distances[pair_count // 2 :] + distances[: pair_count // 2]

    def tie(crossed, other):
        ordered, other = lax.optimization_barrier(([crossed[q] for q in far_first], other))
        return [ordered[far_first.index(q)] for q in distances], other

    def gather_chunk(c, received):
        keep, give = pack_pair(
            meta, momentum_shards, received, c * wide, CHUNK, row_count, window
        )
        return join(meta, keep, swap(give, "row", row_count, 1), even, window, pair_count)

    last, _ = fetch(number * wide, pair_count * LAST, shard_starts)
    received, last = fetch(0, row_count * CHUNK, last)
    pieces = pack(
        meta, momentum_shards, last, number * wide, LAST, 2, pair_count, window
    )
    crossed_last, received = tie(across(pieces), received)
    joined = gather_chunk(0, received)
    landed = []
    for c in range(1, number):
        received, joined = fetch(c * wide, row_count * CHUNK, joined)
        crossed, received = tie(across(joined), received)
        landed.append(crossed)
        joined = gather_chunk(c, received)
    landed.append(across(joined))
    matrices = [
        merge(meta, pieces, [[q] for q in distances], 2 * even, 2, jitter) for pieces in landed
    ]
    twin = [swap(piece, "row", row_count, 1) for piece in crossed_last]
    matrices.append(
        merge(
            meta,
            crossed_last + twin,
            [[2 * q] for q in distances] + [[2 * q + 1] for q in distances],
            even,
            1,
            jitter,
        )
    )

    tiles = sum_tiles(meta, collect(meta, matrices), row_count, col_count)

    sends = [(2 * even, 2, even + window, distances)] * number
    sends.append((even, 1, window, [2 * q for q in distances]))
    first, gram = first_apply(meta, tiles, matrices[0], sends[0], jitter)
    results = [first] + next_apply(meta, gram, matrices[1:], sends[1:], jitter)

    crossed = [across(results[0])]
    crossed[0], results[1:] = tie(crossed[0], results[1:])
    for pieces in results[1:]:
        crossed[-1], pieces = tie(crossed[-1], pieces)
        crossed.append(across(pieces))
    backs = []
    for c in range(number + 1):
        if c < number:
            got = swap(cut(meta, crossed[c], even, window), "row", row_count, 1)
            parts = list(
                unpack_pair(meta, crossed[c], got, col_count, slots, even, window)
            )
        else:
            parts = unpack(meta, crossed[c], col_count, slots, 2)
        if c + 1 == number:
            crossed[c + 1], parts[0] = tie(crossed[c + 1], parts[0])
        back = [parts[0]] + [swap(parts[k], "col", col_count, k) for k in range(1, col_count)]
        if c + 1 < number:
            crossed[c + 1], back = tie(crossed[c + 1], back)
        backs.append(back)
    out = jnp.zeros(momentum_shards.shape, jnp.bfloat16)
    for c, back in enumerate(backs):
        span = row_count * CHUNK if c < number else pair_count * LAST
        for k in range(col_count):
            out = lax.dynamic_update_slice_in_dim(
                out, back[k], c * wide + (col ^ k) * span, axis=1
            )
    return out


def body(momentum_shards, shard_starts):
    devices = lax.axis_size("col") * lax.axis_size("row")
    chunks = (N // devices) % CHUNK == LAST // 2 and N // devices > CHUNK
    powers = all(lax.axis_size(a) & (lax.axis_size(a) - 1) == 0 for a in ("row", "col"))
    jitter = 4 * (M // devices // 8)
    if chunks and powers and jitter % 8 == 0:
        return chunk_body(momentum_shards, shard_starts)
    return plain_body(momentum_shards, shard_starts)


def solution(mesh):
    in_specs = (P(("row", "col"), None), P())
    out_specs = P(("row", "col"), None)
    return jax.shard_map(body, mesh=mesh, in_specs=in_specs, out_specs=out_specs, check_vma=False)
```

```python
import math

import jax
import jax.numpy as jnp
import numpy as np
from jax import lax
from jax.experimental import pallas as pl
from jax.experimental.pallas import tpu as pltpu
from jax.sharding import PartitionSpec as P

M = 3584
N = 18432
TILE = 512
BLOCKS = M // TILE

coef_one = 3.4445
coef_two = -4.775
coef_three = 2.0315

PAIRS = [(i, j) for i in range(BLOCKS) for j in range(i, BLOCKS)]
PAIR_ROWS = np.array([i for i, _ in PAIRS], np.int32)
PAIR_COLS = np.array([j for _, j in PAIRS], np.int32)


def packing(shard_starts, row_block, col_count, shard_rows, window, first_row):
    shard_ends = jnp.concatenate([shard_starts[1:], jnp.full((1,), M, jnp.int32)])
    first_starts = lax.dynamic_slice_in_dim(shard_starts, row_block * col_count, col_count)
    last_ends = lax.dynamic_slice_in_dim(shard_ends, row_block * col_count, col_count)
    slot_index = jnp.arange(col_count * shard_rows, dtype=jnp.int32)
    member = slot_index // shard_rows
    offset = slot_index % shard_rows
    pick = member[:, None] == jnp.arange(col_count, dtype=jnp.int32)[None, :]
    shard_begin = jnp.sum(jnp.where(pick, first_starts[None, :], 0), axis=1)
    length = jnp.sum(jnp.where(pick, (last_ends - first_starts)[None, :], 0), axis=1)
    target = shard_begin - first_row + offset
    is_valid = offset < length
    window_rows = jnp.arange(window, dtype=jnp.int32)
    return ((window_rows[:, None] == target[None, :]) & is_valid[None, :]).astype(jnp.bfloat16)


def gram_kernel(rows_ref, cols_ref, left_ref, right_ref, out_ref):
    out_ref[...] = lax.dot_general(
        left_ref[...], right_ref[...], (((1,), (1,)), ((), ())), preferred_element_type=jnp.float32
    ).astype(jnp.bfloat16)


def gram_tiles(matrix):
    width = matrix.shape[1]
    count = len(PAIRS)
    return pl.pallas_call(
        gram_kernel,
        out_shape=jax.ShapeDtypeStruct((count * TILE, TILE), jnp.bfloat16),
        grid_spec=pltpu.PrefetchScalarGridSpec(
            num_scalar_prefetch=2,
            grid=(count,),
            in_specs=[
                pl.BlockSpec((TILE, width), lambda p, rows, cols: (rows[p], 0)),
                pl.BlockSpec((TILE, width), lambda p, rows, cols: (cols[p], 0)),
            ],
            out_specs=pl.BlockSpec((TILE, TILE), lambda p, rows, cols: (p, 0)),
        ),
        compiler_params=pltpu.CompilerParams(vmem_limit_bytes=32 * 1024 * 1024),
        cost_estimate=pl.CostEstimate(
            flops=2 * count * TILE * TILE * width,
            bytes_accessed=2 * count * TILE * (TILE + width),
            transcendentals=0,
        ),
    )(jnp.asarray(PAIR_ROWS), jnp.asarray(PAIR_COLS), matrix, matrix)


def apply_kernel(rows_ref, cols_ref, tile_ref, matrix_ref, out_ref, total, factor):
    turn = pl.program_id(0)
    pair = pl.program_id(1)
    i = rows_ref[pair]
    j = cols_ref[pair]
    here = pl.ds(pl.multiple_of(i * TILE, TILE), TILE)
    there = pl.ds(pl.multiple_of(j * TILE, TILE), TILE)

    @pl.when((turn == 0) & (pair == 0))
    def _():
        total[...] = jnp.zeros_like(total)
        factor[...] = matrix_ref[...]

    @pl.when((turn == 1) & (pair == 0))
    def _():
        @pl.loop(0, BLOCKS)
        def _(b):
            part = pl.ds(pl.multiple_of(b * TILE, TILE), TILE)
            product = total[part, :]
            factor[part, :] = (coef_three * product).astype(jnp.bfloat16)
            total[part, :] = coef_one * matrix_ref[part, :].astype(jnp.float32) + coef_two * product

    total[here, :] += jnp.dot(tile_ref[...], factor[there, :], preferred_element_type=jnp.float32)

    @pl.when(i != j)
    def _():
        total[there, :] += lax.dot_general(
            tile_ref[...], factor[here, :], (((0,), (0,)), ((), ())), preferred_element_type=jnp.float32
        )

    @pl.when((turn == 1) & (pair == pl.num_programs(1) - 1))
    def _():
        @pl.loop(0, BLOCKS)
        def _(b):
            part = pl.ds(pl.multiple_of(b * TILE, TILE), TILE)
            out_ref[part, :] = (math.sqrt(N) * total[part, :]).astype(jnp.bfloat16)


def apply_polynomial(tiles, matrix):
    rows, width = matrix.shape
    count = len(PAIRS)
    return pl.pallas_call(
        apply_kernel,
        out_shape=jax.ShapeDtypeStruct((rows, width), jnp.bfloat16),
        grid_spec=pltpu.PrefetchScalarGridSpec(
            num_scalar_prefetch=2,
            grid=(2, count),
            in_specs=[
                pl.BlockSpec((TILE, TILE), lambda t, p, rows, cols: (p, 0)),
                pl.BlockSpec((rows, width), lambda t, p, rows, cols: (0, 0)),
            ],
            out_specs=pl.BlockSpec((rows, width), lambda t, p, rows, cols: (0, 0)),
            scratch_shapes=[
                pltpu.VMEM((rows, width), jnp.float32),
                pltpu.VMEM((rows, width), jnp.bfloat16),
            ],
        ),
        compiler_params=pltpu.CompilerParams(vmem_limit_bytes=48 * 1024 * 1024),
        cost_estimate=pl.CostEstimate(
            flops=4 * rows * rows * width,
            bytes_accessed=4 * rows * width + 4 * count * TILE * TILE,
            transcendentals=0,
        ),
    )(jnp.asarray(PAIR_ROWS), jnp.asarray(PAIR_COLS), tiles, matrix)


def plain_body(momentum_shards, shard_starts):
    col_count = lax.axis_size("col")
    row_count = lax.axis_size("row")
    shard_rows = momentum_shards.shape[0]
    mean_rows = M // (row_count * col_count)
    jitter = 4 * (mean_rows // 8)
    even = col_count * mean_rows
    window = even + 2 * jitter
    row_block = lax.axis_index("row")
    packer = packing(
        shard_starts, row_block, col_count, shard_rows, window, row_block * even - jitter
    )
    columns = lax.all_to_all(momentum_shards, "col", split_axis=1, concat_axis=0, tiled=True)
    local_tile = jnp.dot(packer, columns, preferred_element_type=jnp.float32).astype(jnp.bfloat16)
    windows = lax.all_to_all(local_tile, "row", split_axis=1, concat_axis=0, tiled=True)
    width = windows.shape[1]
    windows = windows.reshape(row_count, window, width)
    nothing = jnp.zeros((1, jitter, width), jnp.bfloat16)
    head = jnp.concatenate([nothing, windows[:-1, jitter + even :]], axis=0)
    tail = jnp.concatenate([windows[1:, :jitter], nothing], axis=0)
    middle = windows[:, jitter : jitter + even]
    matrix = jnp.concatenate(
        [
            middle[:, :jitter] + head,
            middle[:, jitter : even - jitter],
            middle[:, even - jitter :] + tail,
        ],
        axis=1,
    ).reshape(M, width)

    tiles = lax.psum(gram_tiles(matrix), ("row", "col"))
    update = apply_polynomial(tiles, matrix).reshape(row_count, even, width)

    before = jnp.concatenate([nothing, update[:-1, even - jitter :]], axis=0)
    after = jnp.concatenate([update[1:, :jitter], nothing], axis=0)
    spread = jnp.concatenate([before, update, after], axis=1).reshape(row_count * window, width)
    own_rows = lax.all_to_all(spread, "row", split_axis=0, concat_axis=1, tiled=True)
    back_rows = lax.dot_general(
        packer, own_rows, (((0,), (0,)), ((), ())), preferred_element_type=jnp.float32
    ).astype(jnp.bfloat16)
    return lax.all_to_all(back_rows, "col", split_axis=0, concat_axis=1, tiled=True)


CHUNK = 256
LAST = 128
VMEM_LIMIT = 56 * 1024 * 1024


def swap(value, axis, size, distance):
    return lax.ppermute(value, axis, perm=[(i, i ^ distance) for i in range(size)])


def pack_kernel(step, col_count, meta_ref, *refs):
    pieces, outs, choose = refs[:col_count], refs[col_count:-1], refs[-1]
    turn = pl.program_id(0)
    _, window, slots = choose.shape

    @pl.when(turn == 0)
    def _():
        rows = lax.broadcasted_iota(jnp.int32, (window, slots), 0)
        columns = lax.broadcasted_iota(jnp.int32, (window, slots), 1)
        for k in range(col_count):
            hit = (rows == columns + meta_ref[2 + k]) & (columns < meta_ref[2 + col_count + k])
            choose[k] = jnp.where(hit, 1.0, 0.0).astype(jnp.bfloat16)

    total = jnp.dot(choose[0], pieces[0][...], preferred_element_type=jnp.float32)
    for k in range(1, col_count):
        total += jnp.dot(choose[k], pieces[k][...], preferred_element_type=jnp.float32)
    for q, out in enumerate(outs):

        @pl.when(turn == q)
        def _():
            out[...] = total.astype(jnp.bfloat16)


def pack(meta, momentum, received, base, width, step, count, window):
    slots = momentum.shape[0]
    col_count = len(received) + 1
    first = base // width
    return pl.pallas_call(
        lambda *refs: pack_kernel(step, col_count, *refs),
        out_shape=[jax.ShapeDtypeStruct((window, width), jnp.bfloat16)] * count,
        grid_spec=pltpu.PrefetchScalarGridSpec(
            num_scalar_prefetch=1,
            grid=(count,),
            in_specs=[
                pl.BlockSpec(
                    (slots, width),
                    lambda q, meta: (0, first + meta[1] * count + ((meta[0] // step) ^ q)),
                )
            ]
            + [pl.BlockSpec((slots, width), lambda q, meta: (0, (meta[0] // step) ^ q))]
            * (col_count - 1),
            out_specs=[pl.BlockSpec((window, width), lambda q, meta: (0, 0))] * count,
            scratch_shapes=[pltpu.VMEM((col_count, window, slots), jnp.bfloat16)],
        ),
        compiler_params=pltpu.CompilerParams(vmem_limit_bytes=VMEM_LIMIT),
        cost_estimate=pl.CostEstimate(
            flops=2 * window * slots * col_count * width * count,
            bytes_accessed=2 * count * width * (slots * col_count + window),
            transcendentals=0,
        ),
    )(meta, momentum, *received)


def pack_pair_kernel(col_count, meta_ref, *refs):
    pieces, keep, give, choose = refs[:col_count], refs[col_count], refs[col_count + 1], refs[-1]
    other = pl.program_id(0) == 0
    _, window, slots = choose.shape

    @pl.when(other & (pl.program_id(1) == 0))
    def _():
        fill_choose(meta_ref, choose, 0)

    total = jnp.dot(choose[0], pieces[0][...], preferred_element_type=jnp.float32)
    for k in range(1, col_count):
        total += jnp.dot(choose[k], pieces[k][...], preferred_element_type=jnp.float32)

    @pl.when(other)
    def _():
        give[...] = total.astype(jnp.bfloat16)

    @pl.when(jnp.logical_not(other))
    def _():
        keep[...] = total.astype(jnp.bfloat16)


def fill_choose(meta_ref, choose, slot_axis):
    col_count = choose.shape[0]
    shape = choose.shape[1:]
    rows = lax.broadcasted_iota(jnp.int32, shape, slot_axis)
    slots = lax.broadcasted_iota(jnp.int32, shape, 1 - slot_axis)
    for k in range(col_count):
        hit = (rows == slots + meta_ref[2 + k]) & (slots < meta_ref[2 + col_count + k])
        choose[k] = jnp.where(hit, 1.0, 0.0).astype(jnp.bfloat16)


def pack_pair(meta, momentum, received, base, width, row_count, window):
    slots = momentum.shape[0]
    col_count = len(received) + 1
    pairs = row_count // 2
    first = base // width
    block = lambda e, q, meta: meta[0] ^ (2 * q + 1 - e)
    shape = jax.ShapeDtypeStruct((pairs * window, width), jnp.bfloat16)
    return pl.pallas_call(
        lambda *refs: pack_pair_kernel(col_count, *refs),
        out_shape=[shape, shape],
        grid_spec=pltpu.PrefetchScalarGridSpec(
            num_scalar_prefetch=1,
            grid=(2, pairs),
            in_specs=[
                pl.BlockSpec(
                    (slots, width),
                    lambda e, q, meta: (0, first + meta[1] * row_count + block(e, q, meta)),
                )
            ]
            + [pl.BlockSpec((slots, width), lambda e, q, meta: (0, block(e, q, meta)))]
            * (col_count - 1),
            out_specs=[
                pl.BlockSpec((window, width), lambda e, q, meta: (jnp.where(e == 0, 0, q), 0)),
                pl.BlockSpec(
                    (window, width), lambda e, q, meta: (jnp.where(e == 0, q, pairs - 1), 0)
                ),
            ],
            scratch_shapes=[pltpu.VMEM((col_count, window, slots), jnp.bfloat16)],
        ),
        compiler_params=pltpu.CompilerParams(vmem_limit_bytes=VMEM_LIMIT),
        cost_estimate=pl.CostEstimate(
            flops=2 * window * slots * col_count * width * row_count,
            bytes_accessed=2 * row_count * width * (slots * col_count + window),
            transcendentals=0,
        ),
    )(meta, momentum, *received)


def join_kernel(even, window, meta_ref, keep, got, *outs):
    def write(low, high):
        for q, out in enumerate(outs):
            base = q * window
            lap = window - even
            out[:even, :] = low[base : base + even, :]
            out[even:window, :] = (
                low[base + even : base + window, :].astype(jnp.float32)
                + high[base : base + lap, :].astype(jnp.float32)
            ).astype(jnp.bfloat16)
            out[window:, :] = high[base + lap : base + window, :]

    @pl.when(meta_ref[0] % 2 == 0)
    def _():
        write(keep, got)

    @pl.when(meta_ref[0] % 2 == 1)
    def _():
        write(got, keep)


def local_call(kernel, out_shape, operands, moved, scratch=()):
    whole = pl.BlockSpec(memory_space=pltpu.VMEM)
    return pl.pallas_call(
        kernel,
        out_shape=out_shape,
        in_specs=[pl.BlockSpec(memory_space=pltpu.SMEM)] + [whole] * (len(operands) - 1),
        out_specs=jax.tree.map(lambda _: whole, out_shape),
        scratch_shapes=list(scratch),
        compiler_params=pltpu.CompilerParams(vmem_limit_bytes=VMEM_LIMIT),
        cost_estimate=pl.CostEstimate(flops=moved, bytes_accessed=moved, transcendentals=0),
    )(*operands)


def join(meta, keep, got, even, window, pairs):
    width = keep.shape[1]
    shape = jax.ShapeDtypeStruct((even + window, width), jnp.bfloat16)
    return local_call(
        lambda *refs: join_kernel(even, window, *refs),
        [shape] * pairs,
        (meta, keep, got),
        8 * pairs * window * width,
    )


def cut_kernel(even, window, meta_ref, *refs):
    pieces, out = refs[:-1], refs[-1]
    place = pl.ds(pl.multiple_of((1 - meta_ref[0] % 2) * even, 16), window)
    for q, piece in enumerate(pieces):
        out[q * window : (q + 1) * window, :] = piece[place, :]


def cut(meta, pieces, even, window):
    width = pieces[0].shape[1]
    return local_call(
        lambda *refs: cut_kernel(even, window, *refs),
        jax.ShapeDtypeStruct((len(pieces) * window, width), jnp.bfloat16),
        (meta, *pieces),
        4 * len(pieces) * window * width,
    )


def unpack_pair_kernel(col_count, even, window, meta_ref, *refs):
    got, outs, choose = refs[-2 - col_count], refs[-1 - col_count : -1], refs[-1]
    pieces = refs[: -2 - col_count]
    turn = pl.program_id(0)

    @pl.when(turn == 0)
    def _():
        fill_choose(meta_ref, choose, 1)

    def place(block):
        for k in range(col_count):
            outs[k][...] = jnp.dot(
                choose[k], block, preferred_element_type=jnp.float32
            ).astype(jnp.bfloat16)

    for q, piece in enumerate(pieces):

        @pl.when(turn == 2 * q)
        def _():
            own = pl.ds(pl.multiple_of(meta_ref[0] % 2 * even, 16), window)
            place(piece[own, :])

    @pl.when(turn % 2 == 1)
    def _():
        part = pl.ds(pl.multiple_of(turn // 2 * window, 16), window)
        place(got[part, :])


def unpack_pair(meta, pieces, got, col_count, slots, even, window):
    width = got.shape[1]
    count = 2 * len(pieces)
    return pl.pallas_call(
        lambda *refs: unpack_pair_kernel(col_count, even, window, *refs),
        out_shape=[jax.ShapeDtypeStruct((slots, count * width), jnp.bfloat16)] * col_count,
        grid_spec=pltpu.PrefetchScalarGridSpec(
            num_scalar_prefetch=1,
            grid=(count,),
            in_specs=[pl.BlockSpec(x.shape, lambda q, meta: (0, 0)) for x in (*pieces, got)],
            out_specs=[pl.BlockSpec((slots, width), lambda q, meta: (0, meta[0] ^ q))]
            * col_count,
            scratch_shapes=[pltpu.VMEM((col_count, slots, window), jnp.bfloat16)],
        ),
        compiler_params=pltpu.CompilerParams(vmem_limit_bytes=VMEM_LIMIT),
        cost_estimate=pl.CostEstimate(
            flops=2 * window * slots * col_count * width * count,
            bytes_accessed=2 * count * width * (slots * col_count + window),
            transcendentals=0,
        ),
    )(meta, *pieces, got)


def unpack_kernel(col_count, meta_ref, *refs):
    pieces, outs, choose = refs[: -1 - col_count], refs[-1 - col_count : -1], refs[-1]
    turn = pl.program_id(0)
    _, slots, window = choose.shape

    @pl.when(turn == 0)
    def _():
        rows = lax.broadcasted_iota(jnp.int32, (slots, window), 1)
        columns = lax.broadcasted_iota(jnp.int32, (slots, window), 0)
        for k in range(col_count):
            hit = (rows == columns + meta_ref[2 + k]) & (columns < meta_ref[2 + col_count + k])
            choose[k] = jnp.where(hit, 1.0, 0.0).astype(jnp.bfloat16)

    for q, piece in enumerate(pieces):

        @pl.when(turn == q)
        def _():
            for k in range(col_count):
                outs[k][...] = jnp.dot(
                    choose[k], piece[...], preferred_element_type=jnp.float32
                ).astype(jnp.bfloat16)


def unpack(meta, pieces, col_count, slots, step):
    window, width = pieces[0].shape
    count = len(pieces)
    return pl.pallas_call(
        lambda *refs: unpack_kernel(col_count, *refs),
        out_shape=[jax.ShapeDtypeStruct((slots, count * width), jnp.bfloat16)] * col_count,
        grid_spec=pltpu.PrefetchScalarGridSpec(
            num_scalar_prefetch=1,
            grid=(count,),
            in_specs=[pl.BlockSpec((window, width), lambda q, meta: (0, 0))] * count,
            out_specs=[pl.BlockSpec((slots, width), lambda q, meta: (0, (meta[0] // step) ^ q))]
            * col_count,
            scratch_shapes=[pltpu.VMEM((col_count, slots, window), jnp.bfloat16)],
        ),
        compiler_params=pltpu.CompilerParams(vmem_limit_bytes=VMEM_LIMIT),
        cost_estimate=pl.CostEstimate(
            flops=2 * window * slots * col_count * width * count,
            bytes_accessed=2 * count * width * (slots * col_count + window),
            transcendentals=0,
        ),
    )(meta, *pieces)


def merge_kernel(unit, share, distances, meta_ref, *refs):
    pieces, out_ref, total = refs[:-2], refs[-2], refs[-1]
    jitter = (total.shape[0] - M) // 2
    total[...] = jnp.zeros_like(total)
    for places, piece in zip(distances, pieces):
        rows = piece.shape[0] // len(places)
        for n, distance in enumerate(places):
            place = pl.ds(pl.multiple_of(((meta_ref[0] // share) ^ distance) * unit, 8), rows)
            total[place, :] += piece[n * rows : (n + 1) * rows, :].astype(jnp.float32)

    @pl.loop(0, BLOCKS)
    def _(b):
        source = pl.ds(pl.multiple_of(b * TILE + jitter, 8), TILE)
        out_ref[tile_rows(b), :] = total[source, :].astype(jnp.bfloat16)


def merge(meta, pieces, distances, unit, share, jitter):
    width = pieces[0].shape[1]
    return local_call(
        lambda *refs: merge_kernel(unit, share, distances, *refs),
        jax.ShapeDtypeStruct((M, width), jnp.bfloat16),
        (meta, *pieces),
        5 * M * width,
        [pltpu.VMEM((M + 2 * jitter, width), jnp.float32)],
    )


def collect_kernel(meta_ref, *refs):
    matrices, joined = refs[:-1], refs[-1]
    place = 0
    for matrix in matrices[:-1]:
        joined[:, place : place + matrix.shape[1]] = matrix[...]
        place += matrix.shape[1]
    lane = lax.broadcasted_iota(jnp.int32, (TILE, LAST), 1)
    own = lane // (LAST // 2) == meta_ref[0] % 2

    @pl.loop(0, BLOCKS)
    def _(b):
        block = matrices[-1][tile_rows(b), :].astype(jnp.float32)
        joined[tile_rows(b), place:] = jnp.where(own, block, 0.0).astype(jnp.bfloat16)


def collect(meta, chunks):
    width = sum(x.shape[1] for x in chunks)
    return local_call(
        collect_kernel,
        jax.ShapeDtypeStruct((M, width), jnp.bfloat16),
        (meta, *chunks),
        4 * M * width,
    )


PIECES = 2
HALF = len(PAIRS) // 2
PART = HALF // PIECES


def half_gram_kernel(flip, rows_ref, cols_ref, meta_ref, joined, *outs):
    turn = pl.program_id(0)
    pair = (meta_ref[0] % 2 ^ flip) * HALF + turn
    here = pl.ds(pl.multiple_of(rows_ref[pair] * TILE, TILE), TILE)
    there = pl.ds(pl.multiple_of(cols_ref[pair] * TILE, TILE), TILE)
    tile = lax.dot_general(
        joined[here, :],
        joined[there, :],
        (((1,), (1,)), ((), ())),
        preferred_element_type=jnp.float32,
    ).astype(jnp.bfloat16)
    for n, out in enumerate(outs):

        @pl.when(turn // PART == n)
        def _():
            out[...] = tile


def half_gram(meta, joined, flip):
    width = joined.shape[1]
    place = lambda n: lambda p, rows, cols, meta: (jnp.clip(p - n * PART, 0, PART - 1), 0)
    return pl.pallas_call(
        lambda *refs: half_gram_kernel(flip, *refs),
        out_shape=[jax.ShapeDtypeStruct((PART * TILE, TILE), jnp.bfloat16)] * PIECES,
        grid_spec=pltpu.PrefetchScalarGridSpec(
            num_scalar_prefetch=3,
            grid=(HALF,),
            in_specs=[pl.BlockSpec((M, width), lambda p, rows, cols, meta: (0, 0))],
            out_specs=[pl.BlockSpec((TILE, TILE), place(n)) for n in range(PIECES)],
        ),
        compiler_params=pltpu.CompilerParams(vmem_limit_bytes=VMEM_LIMIT),
        cost_estimate=pl.CostEstimate(
            flops=2 * HALF * TILE * TILE * width,
            bytes_accessed=2 * HALF * TILE * TILE + 2 * M * width,
            transcendentals=0,
        ),
    )(jnp.asarray(PAIR_ROWS), jnp.asarray(PAIR_COLS), meta, joined)


def lane_block(block, lanes):
    return pl.ds(pl.multiple_of(block * lanes, lanes), lanes)


def add_halves_kernel(meta_ref, *refs):
    count = len(refs) // 3
    for keep, got, out in zip(refs[:count], refs[count : 2 * count], refs[2 * count :]):
        out[...] = keep[...] + got[...]


def add_halves(meta, keep, got, col_count):
    rows, lanes = keep.shape
    lanes //= col_count
    tall = rows // 4
    place = lambda k: lambda t, meta: (t, meta[1] ^ k)
    return pl.pallas_call(
        add_halves_kernel,
        out_shape=[jax.ShapeDtypeStruct((rows, lanes), jnp.bfloat16)] * col_count,
        grid_spec=pltpu.PrefetchScalarGridSpec(
            num_scalar_prefetch=1,
            grid=(rows // tall,),
            in_specs=[pl.BlockSpec((tall, lanes), place(k)) for k in range(col_count)] * 2,
            out_specs=[pl.BlockSpec((tall, lanes), lambda t, meta: (t, 0))] * col_count,
        ),
        compiler_params=pltpu.CompilerParams(vmem_limit_bytes=VMEM_LIMIT),
        cost_estimate=pl.CostEstimate(
            flops=keep.size, bytes_accessed=6 * keep.size, transcendentals=0
        ),
    )(meta, *[keep] * col_count, *[got] * col_count)


def total_of(refs, part):
    total = refs[0][part, :].astype(jnp.float32)
    for ref in refs[1:]:
        total += ref[part, :].astype(jnp.float32)
    return total.astype(jnp.bfloat16)


def add_quarters_kernel(col_count, meta_ref, *refs):
    blocks, outs = refs[:col_count], refs[col_count:]
    rows = outs[0].shape[0]
    for q, out in enumerate(outs):
        place = (meta_ref[0] // 2 ^ q) * rows
        out[...] = total_of(blocks, pl.ds(pl.multiple_of(place, rows), rows))


def add_quarters(meta, blocks, pair_count):
    rows, lanes = blocks[0].shape
    shape = jax.ShapeDtypeStruct((rows // pair_count, lanes), jnp.bfloat16)
    return local_call(
        lambda *refs: add_quarters_kernel(len(blocks), *refs),
        [shape] * pair_count,
        (meta, *blocks),
        10 * rows * lanes,
    )


def add_parts_kernel(meta_ref, *refs):
    rows = refs[-1].shape[0]
    refs[-1][...] = total_of(refs[:-1], pl.ds(0, rows))


def add_parts(meta, parts):
    return local_call(
        add_parts_kernel,
        jax.ShapeDtypeStruct(parts[0].shape, jnp.bfloat16),
        (meta, *parts),
        10 * parts[0].size,
    )


def stack_kernel(meta_ref, *refs):
    parts, out = refs[:-1], refs[-1]
    rows = parts[0].shape[0]
    for q, part in enumerate(parts):
        out[pl.ds(pl.multiple_of((meta_ref[0] // 2 ^ q) * rows, rows), rows), :] = part[...]


def stack(meta, parts):
    rows, lanes = parts[0].shape
    return local_call(
        stack_kernel,
        jax.ShapeDtypeStruct((rows * len(parts), lanes), jnp.bfloat16),
        (meta, *parts),
        4 * rows * lanes * len(parts),
    )


def tile_rows(b):
    return pl.ds(pl.multiple_of(b * TILE, TILE), TILE)


def first_product(panel, b, jitter, matrix, total, factor):
    product = jnp.dot(panel, matrix[...], preferred_element_type=jnp.float32)
    factor[tile_rows(b), :] = (coef_three * product).astype(jnp.bfloat16)
    total[pl.ds(pl.multiple_of(b * TILE + jitter, 8), TILE), :] = (
        coef_one * matrix[tile_rows(b), :].astype(jnp.float32) + coef_two * product
    )


def second_product(panel, b, jitter, total, factor):
    place = pl.ds(pl.multiple_of(b * TILE + jitter, 8), TILE)
    total[place, :] = math.sqrt(N) * (
        total[place, :] + jnp.dot(panel, factor[...], preferred_element_type=jnp.float32)
    )


def clear_edges(total, jitter):
    edge = jnp.zeros((jitter, total.shape[1]), jnp.float32)
    total[pl.ds(0, jitter), :] = edge
    total[pl.ds(M + jitter, jitter), :] = edge


def store_windows(row, send, total, outs):
    unit, share, rows, distances = send
    for distance, out in zip(distances, outs):
        place = pl.ds(pl.multiple_of(((row // share) ^ distance) * unit, 8), rows)
        out[...] = total[place, :].astype(jnp.bfloat16)


def first_apply_kernel(jitter, send, col_count, rows_ref, cols_ref, meta_ref, *refs):
    count = 2 * PIECES * col_count
    blocks, matrix, outs, gram_out = refs[:count], refs[count], refs[count + 1 : -6], refs[-6]
    gram, total, factor, tile_sems, out_sem = refs[-5:]
    lanes = TILE // col_count
    tiles = []
    for n in range(2 * HALF):
        half, part = divmod(n, HALF)
        pair = (meta_ref[0] % 2 ^ half) * HALF + part
        i, j = rows_ref[pair], cols_ref[pair]
        rows = pl.ds(part % PART * TILE, TILE)
        first = (half * PIECES + part // PART) * col_count
        moves = [
            (
                blocks[first + k].at[rows, :],
                gram.at[i, :, lane_block(j * col_count + (meta_ref[1] ^ k), lanes)],
            )
            for k in range(col_count)
        ]
        copies = [
            pltpu.make_async_copy(source, target, tile_sems.at[n, k])
            for k, (source, target) in enumerate(moves)
        ]
        for copy in copies:
            copy.start()
        tiles.append((copies, i, j))
    clear_edges(total, jitter)
    for copies, i, j in tiles:
        for copy in copies:
            copy.wait()

        @pl.when(i != j)
        def _():
            gram[j, :, lane_block(i, TILE)] = gram[i, :, lane_block(j, TILE)].T

    back = pltpu.make_async_copy(gram, gram_out, out_sem)
    back.start()

    @pl.loop(0, BLOCKS)
    def _(b):
        first_product(gram[b], b, jitter, matrix, total, factor)

    @pl.loop(0, BLOCKS)
    def _(b):
        second_product(gram[b], b, jitter, total, factor)

    store_windows(meta_ref[0], send, total, outs)
    back.wait()


def first_apply(meta, own, twin, matrix, send, jitter):
    pieces = [*own, *twin]
    col_count = len(own) // PIECES
    width = matrix.shape[1]
    whole = pl.BlockSpec(memory_space=pltpu.VMEM)
    outs = pl.pallas_call(
        lambda *refs: first_apply_kernel(jitter, send, col_count, *refs),
        out_shape=[jax.ShapeDtypeStruct((send[2], width), jnp.bfloat16)] * len(send[3])
        + [jax.ShapeDtypeStruct((BLOCKS, TILE, M), jnp.bfloat16)],
        in_specs=[pl.BlockSpec(memory_space=pltpu.SMEM)] * 3
        + [pl.BlockSpec(memory_space=pl.ANY)] * len(pieces)
        + [whole],
        out_specs=[whole] * len(send[3]) + [pl.BlockSpec(memory_space=pl.ANY)],
        scratch_shapes=[
            pltpu.VMEM((BLOCKS, TILE, M), jnp.bfloat16),
            pltpu.VMEM((M + 2 * jitter, width), jnp.float32),
            pltpu.VMEM((M, width), jnp.bfloat16),
            pltpu.SemaphoreType.DMA((len(PAIRS), col_count)),
            pltpu.SemaphoreType.DMA,
        ],
        compiler_params=pltpu.CompilerParams(vmem_limit_bytes=VMEM_LIMIT),
        cost_estimate=pl.CostEstimate(
            flops=4 * M * M * width, bytes_accessed=4 * M * width + 4 * M * M, transcendentals=0
        ),
    )(jnp.asarray(PAIR_ROWS), jnp.asarray(PAIR_COLS), meta, *pieces, matrix)
    return outs[:-1], outs[-1]


def next_apply_kernel(jitter, sends, meta_ref, panel_ref, *refs):
    chunks = len(sends)
    outs_count = sum(len(s[3]) for s in sends)
    matrices = refs[:chunks]
    outs = refs[chunks : chunks + outs_count]
    totals = refs[chunks + outs_count : 2 * chunks + outs_count]
    factors = refs[2 * chunks + outs_count :]
    turn = pl.program_id(0)

    @pl.when(turn < BLOCKS)
    def _():
        for matrix, total, factor in zip(matrices, totals, factors):
            first_product(panel_ref[0], turn, jitter, matrix, total, factor)

    @pl.when(turn >= BLOCKS)
    def _():
        for total, factor in zip(totals, factors):
            second_product(panel_ref[0], turn - BLOCKS, jitter, total, factor)

    @pl.when(turn == 2 * BLOCKS - 1)
    def _():
        place = 0
        for total, send in zip(totals, sends):
            clear_edges(total, jitter)
            store_windows(meta_ref[0], send, total, outs[place : place + len(send[3])])
            place += len(send[3])


def next_apply(meta, gram, matrices, sends, jitter):
    widths = [x.shape[1] for x in matrices]
    shapes = [(send[2], width) for width, send in zip(widths, sends) for _ in send[3]]
    whole = lambda t, meta: (0, 0)
    outs = pl.pallas_call(
        lambda *refs: next_apply_kernel(jitter, sends, *refs),
        out_shape=[jax.ShapeDtypeStruct(shape, jnp.bfloat16) for shape in shapes],
        grid_spec=pltpu.PrefetchScalarGridSpec(
            num_scalar_prefetch=1,
            grid=(2 * BLOCKS,),
            in_specs=[pl.BlockSpec((1, TILE, M), lambda t, meta: (t % BLOCKS, 0, 0))]
            + [pl.BlockSpec((M, width), whole) for width in widths],
            out_specs=[pl.BlockSpec(shape, whole) for shape in shapes],
            scratch_shapes=[pltpu.VMEM((M + 2 * jitter, width), jnp.float32) for width in widths]
            + [pltpu.VMEM((M, width), jnp.bfloat16) for width in widths],
        ),
        compiler_params=pltpu.CompilerParams(vmem_limit_bytes=VMEM_LIMIT),
        cost_estimate=pl.CostEstimate(
            flops=4 * M * M * sum(widths),
            bytes_accessed=4 * M * sum(widths) + 4 * M * M,
            transcendentals=0,
        ),
    )(meta, gram, *matrices)
    result = []
    for send in sends:
        result.append(outs[: len(send[3])])
        outs = outs[len(send[3]) :]
    return result


def sum_tiles(meta, joined, row_count, col_count):
    pair_count = row_count // 2
    tie = lax.optimization_barrier

    def over_cols(blocks):
        return [swap(blocks[k], "col", col_count, k) for k in range(1, col_count)]

    def over_pairs(blocks):
        return [swap(blocks[q], "row", row_count, 2 * q) for q in range(1, pair_count)]

    give = half_gram(meta, joined, 1)
    got = [swap(piece, "row", row_count, 1) for piece in give]
    keep = half_gram(meta, joined, 0)

    early = add_halves(meta, keep[0], got[0], col_count)
    early_in = over_cols(early)
    late = add_halves(meta, keep[1], got[1], col_count)
    late, early_in = tie((late, early_in))
    late_in = over_cols(late)
    early_parts = add_quarters(meta, [early[0]] + early_in, pair_count)
    early_in = over_pairs(early_parts)
    early_part = add_parts(meta, [early_parts[0]] + early_in)
    early_in = over_pairs([early_part] * pair_count)
    late_in, early_in = tie((late_in, early_in))
    late_parts = add_quarters(meta, [late[0]] + late_in, pair_count)
    early_block = stack(meta, [early_part] + early_in)
    early_in = over_cols([early_block] * col_count)
    late_in = over_pairs(late_parts)
    late_part = add_parts(meta, [late_parts[0]] + late_in)
    late_in = over_pairs([late_part] * pair_count)
    late_in, early_in = tie((late_in, early_in))
    late_block = stack(meta, [late_part] + late_in)
    late_in = over_cols([late_block] * col_count)
    early = [early_block] + early_in
    early_twin = [swap(block, "row", row_count, 1) for block in early]
    late = [late_block] + late_in
    late_twin = [swap(block, "row", row_count, 1) for block in late]
    return early + late, early_twin + late_twin


def chunk_body(momentum_shards, shard_starts):
    col_count = lax.axis_size("col")
    row_count = lax.axis_size("row")
    pair_count = row_count // 2
    slots = momentum_shards.shape[0]
    mean_rows = M // (row_count * col_count)
    jitter = 4 * (mean_rows // 8)
    even = col_count * mean_rows
    window = even + 2 * jitter
    row = lax.axis_index("row").astype(jnp.int32)
    col = lax.axis_index("col").astype(jnp.int32)
    shard_ends = jnp.concatenate([shard_starts[1:], jnp.full((1,), M, jnp.int32)])
    members = row * col_count + (col ^ jnp.arange(col_count, dtype=jnp.int32))
    begins = shard_starts[members]
    meta = jnp.concatenate(
        [row[None], col[None], begins - (row * even - jitter), shard_ends[members] - begins]
    )

    wide = row_count * col_count * CHUNK
    number = (N // (row_count * col_count)) // CHUNK
    distances = list(range(pair_count))

    def fetch(base, span, after):
        place, after = lax.optimization_barrier((col, after))
        received = [
            swap(
                lax.dynamic_slice_in_dim(
                    momentum_shards, base + (place ^ k) * span, span, axis=1
                ),
                "col",
                col_count,
                k,
            )
            for k in range(1, col_count)
        ]
        return received, after

    def across(pieces):
        return [pieces[0]] + [swap(pieces[q], "row", row_count, 2 * q) for q in distances[1:]]

    far_first = distances[pair_count // 2 :] + distances[: pair_count // 2]

    def tie(crossed, other):
        ordered, other = lax.optimization_barrier(([crossed[q] for q in far_first], other))
        return [ordered[far_first.index(q)] for q in distances], other

    def gather_chunk(c, received):
        keep, give = pack_pair(
            meta, momentum_shards, received, c * wide, CHUNK, row_count, window
        )
        return join(meta, keep, swap(give, "row", row_count, 1), even, window, pair_count)

    last, _ = fetch(number * wide, pair_count * LAST, shard_starts)
    received, last = fetch(0, row_count * CHUNK, last)
    pieces = pack(
        meta, momentum_shards, last, number * wide, LAST, 2, pair_count, window
    )
    crossed_last, received = tie(across(pieces), received)
    joined = gather_chunk(0, received)
    landed = []
    for c in range(1, number):
        received, joined = fetch(c * wide, row_count * CHUNK, joined)
        crossed, received = tie(across(joined), received)
        landed.append(crossed)
        joined = gather_chunk(c, received)
    landed.append(across(joined))
    matrices = [
        merge(meta, pieces, [[q] for q in distances], 2 * even, 2, jitter) for pieces in landed
    ]
    twin = [swap(piece, "row", row_count, 1) for piece in crossed_last]
    matrices.append(
        merge(
            meta,
            crossed_last + twin,
            [[2 * q] for q in distances] + [[2 * q + 1] for q in distances],
            even,
            1,
            jitter,
        )
    )

    tiles = sum_tiles(meta, collect(meta, matrices), row_count, col_count)

    sends = [(2 * even, 2, even + window, distances)] * number
    sends.append((even, 1, window, [2 * q for q in distances]))
    first, gram = first_apply(meta, *tiles, matrices[0], sends[0], jitter)
    results = [first] + next_apply(meta, gram, matrices[1:], sends[1:], jitter)

    crossed = [across(results[0])]
    crossed[0], results[1:] = tie(crossed[0], results[1:])
    for pieces in results[1:]:
        crossed[-1], pieces = tie(crossed[-1], pieces)
        crossed.append(across(pieces))
    backs = []
    for c in range(number + 1):
        if c < number:
            got = swap(cut(meta, crossed[c], even, window), "row", row_count, 1)
            parts = list(
                unpack_pair(meta, crossed[c], got, col_count, slots, even, window)
            )
        else:
            parts = unpack(meta, crossed[c], col_count, slots, 2)
        if c + 1 == number:
            crossed[c + 1], parts[0] = tie(crossed[c + 1], parts[0])
        back = [parts[0]] + [swap(parts[k], "col", col_count, k) for k in range(1, col_count)]
        if c + 1 < number:
            crossed[c + 1], back = tie(crossed[c + 1], back)
        backs.append(back)
    out = jnp.zeros(momentum_shards.shape, jnp.bfloat16)
    for c, back in enumerate(backs):
        span = row_count * CHUNK if c < number else pair_count * LAST
        for k in range(col_count):
            out = lax.dynamic_update_slice_in_dim(
                out, back[k], c * wide + (col ^ k) * span, axis=1
            )
    return out


def body(momentum_shards, shard_starts):
    devices = lax.axis_size("col") * lax.axis_size("row")
    chunks = (N // devices) % CHUNK == LAST // 2 and N // devices > CHUNK
    powers = all(lax.axis_size(a) & (lax.axis_size(a) - 1) == 0 for a in ("row", "col"))
    jitter = 4 * (M // devices // 8)
    if chunks and powers and jitter % 8 == 0:
        return chunk_body(momentum_shards, shard_starts)
    return plain_body(momentum_shards, shard_starts)


def solution(mesh):
    in_specs = (P(("row", "col"), None), P())
    out_specs = P(("row", "col"), None)
    return jax.shard_map(body, mesh=mesh, in_specs=in_specs, out_specs=out_specs, check_vma=False)
```

```python
import math

import jax
import jax.numpy as jnp
import numpy as np
from jax import lax
from jax.experimental import pallas as pl
from jax.experimental.pallas import tpu as pltpu
from jax.sharding import PartitionSpec as P

M = 3584
N = 18432
TILE = 512
BLOCKS = M // TILE

coef_one = 3.4445
coef_two = -4.775
coef_three = 2.0315

PAIRS = [(i, j) for i in range(BLOCKS) for j in range(i, BLOCKS)]
PAIR_ROWS = np.array([i for i, _ in PAIRS], np.int32)
PAIR_COLS = np.array([j for _, j in PAIRS], np.int32)


def packing(shard_starts, row_block, col_count, shard_rows, window, first_row):
    shard_ends = jnp.concatenate([shard_starts[1:], jnp.full((1,), M, jnp.int32)])
    first_starts = lax.dynamic_slice_in_dim(shard_starts, row_block * col_count, col_count)
    last_ends = lax.dynamic_slice_in_dim(shard_ends, row_block * col_count, col_count)
    slot_index = jnp.arange(col_count * shard_rows, dtype=jnp.int32)
    member = slot_index // shard_rows
    offset = slot_index % shard_rows
    pick = member[:, None] == jnp.arange(col_count, dtype=jnp.int32)[None, :]
    shard_begin = jnp.sum(jnp.where(pick, first_starts[None, :], 0), axis=1)
    length = jnp.sum(jnp.where(pick, (last_ends - first_starts)[None, :], 0), axis=1)
    target = shard_begin - first_row + offset
    is_valid = offset < length
    window_rows = jnp.arange(window, dtype=jnp.int32)
    return ((window_rows[:, None] == target[None, :]) & is_valid[None, :]).astype(jnp.bfloat16)


def gram_kernel(rows_ref, cols_ref, left_ref, right_ref, out_ref):
    out_ref[...] = lax.dot_general(
        left_ref[...], right_ref[...], (((1,), (1,)), ((), ())), preferred_element_type=jnp.float32
    ).astype(jnp.bfloat16)


def gram_tiles(matrix):
    width = matrix.shape[1]
    count = len(PAIRS)
    return pl.pallas_call(
        gram_kernel,
        out_shape=jax.ShapeDtypeStruct((count * TILE, TILE), jnp.bfloat16),
        grid_spec=pltpu.PrefetchScalarGridSpec(
            num_scalar_prefetch=2,
            grid=(count,),
            in_specs=[
                pl.BlockSpec((TILE, width), lambda p, rows, cols: (rows[p], 0)),
                pl.BlockSpec((TILE, width), lambda p, rows, cols: (cols[p], 0)),
            ],
            out_specs=pl.BlockSpec((TILE, TILE), lambda p, rows, cols: (p, 0)),
        ),
        compiler_params=pltpu.CompilerParams(vmem_limit_bytes=32 * 1024 * 1024),
        cost_estimate=pl.CostEstimate(
            flops=2 * count * TILE * TILE * width,
            bytes_accessed=2 * count * TILE * (TILE + width),
            transcendentals=0,
        ),
    )(jnp.asarray(PAIR_ROWS), jnp.asarray(PAIR_COLS), matrix, matrix)


def apply_kernel(rows_ref, cols_ref, tile_ref, matrix_ref, out_ref, total, factor):
    turn = pl.program_id(0)
    pair = pl.program_id(1)
    i = rows_ref[pair]
    j = cols_ref[pair]
    here = pl.ds(pl.multiple_of(i * TILE, TILE), TILE)
    there = pl.ds(pl.multiple_of(j * TILE, TILE), TILE)

    @pl.when((turn == 0) & (pair == 0))
    def _():
        total[...] = jnp.zeros_like(total)
        factor[...] = matrix_ref[...]

    @pl.when((turn == 1) & (pair == 0))
    def _():
        @pl.loop(0, BLOCKS)
        def _(b):
            part = pl.ds(pl.multiple_of(b * TILE, TILE), TILE)
            product = total[part, :]
            factor[part, :] = (coef_three * product).astype(jnp.bfloat16)
            total[part, :] = coef_one * matrix_ref[part, :].astype(jnp.float32) + coef_two * product

    total[here, :] += jnp.dot(tile_ref[...], factor[there, :], preferred_element_type=jnp.float32)

    @pl.when(i != j)
    def _():
        total[there, :] += lax.dot_general(
            tile_ref[...], factor[here, :], (((0,), (0,)), ((), ())), preferred_element_type=jnp.float32
        )

    @pl.when((turn == 1) & (pair == pl.num_programs(1) - 1))
    def _():
        @pl.loop(0, BLOCKS)
        def _(b):
            part = pl.ds(pl.multiple_of(b * TILE, TILE), TILE)
            out_ref[part, :] = (math.sqrt(N) * total[part, :]).astype(jnp.bfloat16)


def apply_polynomial(tiles, matrix):
    rows, width = matrix.shape
    count = len(PAIRS)
    return pl.pallas_call(
        apply_kernel,
        out_shape=jax.ShapeDtypeStruct((rows, width), jnp.bfloat16),
        grid_spec=pltpu.PrefetchScalarGridSpec(
            num_scalar_prefetch=2,
            grid=(2, count),
            in_specs=[
                pl.BlockSpec((TILE, TILE), lambda t, p, rows, cols: (p, 0)),
                pl.BlockSpec((rows, width), lambda t, p, rows, cols: (0, 0)),
            ],
            out_specs=pl.BlockSpec((rows, width), lambda t, p, rows, cols: (0, 0)),
            scratch_shapes=[
                pltpu.VMEM((rows, width), jnp.float32),
                pltpu.VMEM((rows, width), jnp.bfloat16),
            ],
        ),
        compiler_params=pltpu.CompilerParams(vmem_limit_bytes=48 * 1024 * 1024),
        cost_estimate=pl.CostEstimate(
            flops=4 * rows * rows * width,
            bytes_accessed=4 * rows * width + 4 * count * TILE * TILE,
            transcendentals=0,
        ),
    )(jnp.asarray(PAIR_ROWS), jnp.asarray(PAIR_COLS), tiles, matrix)


def plain_body(momentum_shards, shard_starts):
    col_count = lax.axis_size("col")
    row_count = lax.axis_size("row")
    shard_rows = momentum_shards.shape[0]
    mean_rows = M // (row_count * col_count)
    jitter = 4 * (mean_rows // 8)
    even = col_count * mean_rows
    window = even + 2 * jitter
    row_block = lax.axis_index("row")
    packer = packing(
        shard_starts, row_block, col_count, shard_rows, window, row_block * even - jitter
    )
    columns = lax.all_to_all(momentum_shards, "col", split_axis=1, concat_axis=0, tiled=True)
    local_tile = jnp.dot(packer, columns, preferred_element_type=jnp.float32).astype(jnp.bfloat16)
    windows = lax.all_to_all(local_tile, "row", split_axis=1, concat_axis=0, tiled=True)
    width = windows.shape[1]
    windows = windows.reshape(row_count, window, width)
    nothing = jnp.zeros((1, jitter, width), jnp.bfloat16)
    head = jnp.concatenate([nothing, windows[:-1, jitter + even :]], axis=0)
    tail = jnp.concatenate([windows[1:, :jitter], nothing], axis=0)
    middle = windows[:, jitter : jitter + even]
    matrix = jnp.concatenate(
        [
            middle[:, :jitter] + head,
            middle[:, jitter : even - jitter],
            middle[:, even - jitter :] + tail,
        ],
        axis=1,
    ).reshape(M, width)

    tiles = lax.psum(gram_tiles(matrix), ("row", "col"))
    update = apply_polynomial(tiles, matrix).reshape(row_count, even, width)

    before = jnp.concatenate([nothing, update[:-1, even - jitter :]], axis=0)
    after = jnp.concatenate([update[1:, :jitter], nothing], axis=0)
    spread = jnp.concatenate([before, update, after], axis=1).reshape(row_count * window, width)
    own_rows = lax.all_to_all(spread, "row", split_axis=0, concat_axis=1, tiled=True)
    back_rows = lax.dot_general(
        packer, own_rows, (((0,), (0,)), ((), ())), preferred_element_type=jnp.float32
    ).astype(jnp.bfloat16)
    return lax.all_to_all(back_rows, "col", split_axis=0, concat_axis=1, tiled=True)


CHUNK = 256
LAST = 128
VMEM_LIMIT = 56 * 1024 * 1024


def swap(value, axis, size, distance):
    return lax.ppermute(value, axis, perm=[(i, i ^ distance) for i in range(size)])


def pack_kernel(step, col_count, meta_ref, *refs):
    pieces, outs, choose = refs[:col_count], refs[col_count:-1], refs[-1]
    turn = pl.program_id(0)
    _, window, slots = choose.shape

    @pl.when(turn == 0)
    def _():
        rows = lax.broadcasted_iota(jnp.int32, (window, slots), 0)
        columns = lax.broadcasted_iota(jnp.int32, (window, slots), 1)
        for k in range(col_count):
            hit = (rows == columns + meta_ref[2 + k]) & (columns < meta_ref[2 + col_count + k])
            choose[k] = jnp.where(hit, 1.0, 0.0).astype(jnp.bfloat16)

    total = jnp.dot(choose[0], pieces[0][...], preferred_element_type=jnp.float32)
    for k in range(1, col_count):
        total += jnp.dot(choose[k], pieces[k][...], preferred_element_type=jnp.float32)
    for q, out in enumerate(outs):

        @pl.when(turn == q)
        def _():
            out[...] = total.astype(jnp.bfloat16)


def pack(meta, momentum, received, base, width, step, count, window):
    slots = momentum.shape[0]
    col_count = len(received) + 1
    first = base // width
    return pl.pallas_call(
        lambda *refs: pack_kernel(step, col_count, *refs),
        out_shape=[jax.ShapeDtypeStruct((window, width), jnp.bfloat16)] * count,
        grid_spec=pltpu.PrefetchScalarGridSpec(
            num_scalar_prefetch=1,
            grid=(count,),
            in_specs=[
                pl.BlockSpec(
                    (slots, width),
                    lambda q, meta: (0, first + meta[1] * count + ((meta[0] // step) ^ q)),
                )
            ]
            + [pl.BlockSpec((slots, width), lambda q, meta: (0, (meta[0] // step) ^ q))]
            * (col_count - 1),
            out_specs=[pl.BlockSpec((window, width), lambda q, meta: (0, 0))] * count,
            scratch_shapes=[pltpu.VMEM((col_count, window, slots), jnp.bfloat16)],
        ),
        compiler_params=pltpu.CompilerParams(vmem_limit_bytes=VMEM_LIMIT),
        cost_estimate=pl.CostEstimate(
            flops=2 * window * slots * col_count * width * count,
            bytes_accessed=2 * count * width * (slots * col_count + window),
            transcendentals=0,
        ),
    )(meta, momentum, *received)


def pack_pair_kernel(col_count, meta_ref, *refs):
    pieces, keep, give, choose = refs[:col_count], refs[col_count], refs[col_count + 1], refs[-1]
    other = pl.program_id(0) == 0
    _, window, slots = choose.shape

    @pl.when(other & (pl.program_id(1) == 0))
    def _():
        fill_choose(meta_ref, choose, 0)

    total = jnp.dot(choose[0], pieces[0][...], preferred_element_type=jnp.float32)
    for k in range(1, col_count):
        total += jnp.dot(choose[k], pieces[k][...], preferred_element_type=jnp.float32)

    @pl.when(other)
    def _():
        give[...] = total.astype(jnp.bfloat16)

    @pl.when(jnp.logical_not(other))
    def _():
        keep[...] = total.astype(jnp.bfloat16)


def fill_choose(meta_ref, choose, slot_axis):
    col_count = choose.shape[0]
    shape = choose.shape[1:]
    rows = lax.broadcasted_iota(jnp.int32, shape, slot_axis)
    slots = lax.broadcasted_iota(jnp.int32, shape, 1 - slot_axis)
    for k in range(col_count):
        hit = (rows == slots + meta_ref[2 + k]) & (slots < meta_ref[2 + col_count + k])
        choose[k] = jnp.where(hit, 1.0, 0.0).astype(jnp.bfloat16)


def pack_pair(meta, momentum, received, base, width, row_count, window):
    slots = momentum.shape[0]
    col_count = len(received) + 1
    pairs = row_count // 2
    first = base // width
    block = lambda e, q, meta: meta[0] ^ (2 * q + 1 - e)
    shape = jax.ShapeDtypeStruct((pairs * window, width), jnp.bfloat16)
    return pl.pallas_call(
        lambda *refs: pack_pair_kernel(col_count, *refs),
        out_shape=[shape, shape],
        grid_spec=pltpu.PrefetchScalarGridSpec(
            num_scalar_prefetch=1,
            grid=(2, pairs),
            in_specs=[
                pl.BlockSpec(
                    (slots, width),
                    lambda e, q, meta: (0, first + meta[1] * row_count + block(e, q, meta)),
                )
            ]
            + [pl.BlockSpec((slots, width), lambda e, q, meta: (0, block(e, q, meta)))]
            * (col_count - 1),
            out_specs=[
                pl.BlockSpec((window, width), lambda e, q, meta: (jnp.where(e == 0, 0, q), 0)),
                pl.BlockSpec(
                    (window, width), lambda e, q, meta: (jnp.where(e == 0, q, pairs - 1), 0)
                ),
            ],
            scratch_shapes=[pltpu.VMEM((col_count, window, slots), jnp.bfloat16)],
        ),
        compiler_params=pltpu.CompilerParams(vmem_limit_bytes=VMEM_LIMIT),
        cost_estimate=pl.CostEstimate(
            flops=2 * window * slots * col_count * width * row_count,
            bytes_accessed=10 * row_count * width * (slots * col_count + window),
            transcendentals=0,
        ),
    )(meta, momentum, *received)


def join_kernel(even, window, meta_ref, keep, got, *outs):
    def write(low, high):
        for q, out in enumerate(outs):
            base = q * window
            lap = window - even
            out[:even, :] = low[base : base + even, :]
            out[even:window, :] = (
                low[base + even : base + window, :].astype(jnp.float32)
                + high[base : base + lap, :].astype(jnp.float32)
            ).astype(jnp.bfloat16)
            out[window:, :] = high[base + lap : base + window, :]

    @pl.when(meta_ref[0] % 2 == 0)
    def _():
        write(keep, got)

    @pl.when(meta_ref[0] % 2 == 1)
    def _():
        write(got, keep)


def local_call(kernel, out_shape, operands, moved, scratch=()):
    whole = pl.BlockSpec(memory_space=pltpu.VMEM)
    return pl.pallas_call(
        kernel,
        out_shape=out_shape,
        in_specs=[pl.BlockSpec(memory_space=pltpu.SMEM)] + [whole] * (len(operands) - 1),
        out_specs=jax.tree.map(lambda _: whole, out_shape),
        scratch_shapes=list(scratch),
        compiler_params=pltpu.CompilerParams(vmem_limit_bytes=VMEM_LIMIT),
        cost_estimate=pl.CostEstimate(flops=moved, bytes_accessed=moved, transcendentals=0),
    )(*operands)


def join(meta, keep, got, even, window, pairs):
    width = keep.shape[1]
    shape = jax.ShapeDtypeStruct((even + window, width), jnp.bfloat16)
    return local_call(
        lambda *refs: join_kernel(even, window, *refs),
        [shape] * pairs,
        (meta, keep, got),
        8 * pairs * window * width,
    )


def cut_kernel(even, window, meta_ref, *refs):
    pieces, out = refs[:-1], refs[-1]
    place = pl.ds(pl.multiple_of((1 - meta_ref[0] % 2) * even, 16), window)
    for q, piece in enumerate(pieces):
        out[q * window : (q + 1) * window, :] = piece[place, :]


def cut(meta, pieces, even, window):
    width = pieces[0].shape[1]
    return local_call(
        lambda *refs: cut_kernel(even, window, *refs),
        jax.ShapeDtypeStruct((len(pieces) * window, width), jnp.bfloat16),
        (meta, *pieces),
        4 * len(pieces) * window * width,
    )


def unpack_pair_kernel(col_count, even, window, meta_ref, *refs):
    got, outs, choose = refs[-2 - col_count], refs[-1 - col_count : -1], refs[-1]
    pieces = refs[: -2 - col_count]
    turn = pl.program_id(0)

    @pl.when(turn == 0)
    def _():
        fill_choose(meta_ref, choose, 1)

    def place(block):
        for k in range(col_count):
            outs[k][...] = jnp.dot(
                choose[k], block, preferred_element_type=jnp.float32
            ).astype(jnp.bfloat16)

    for q, piece in enumerate(pieces):

        @pl.when(turn == 2 * q)
        def _():
            own = pl.ds(pl.multiple_of(meta_ref[0] % 2 * even, 16), window)
            place(piece[own, :])

    @pl.when(turn % 2 == 1)
    def _():
        part = pl.ds(pl.multiple_of(turn // 2 * window, 16), window)
        place(got[part, :])


def unpack_pair(meta, pieces, got, col_count, slots, even, window):
    width = got.shape[1]
    count = 2 * len(pieces)
    return pl.pallas_call(
        lambda *refs: unpack_pair_kernel(col_count, even, window, *refs),
        out_shape=[jax.ShapeDtypeStruct((slots, count * width), jnp.bfloat16)] * col_count,
        grid_spec=pltpu.PrefetchScalarGridSpec(
            num_scalar_prefetch=1,
            grid=(count,),
            in_specs=[pl.BlockSpec(x.shape, lambda q, meta: (0, 0)) for x in (*pieces, got)],
            out_specs=[pl.BlockSpec((slots, width), lambda q, meta: (0, meta[0] ^ q))]
            * col_count,
            scratch_shapes=[pltpu.VMEM((col_count, slots, window), jnp.bfloat16)],
        ),
        compiler_params=pltpu.CompilerParams(vmem_limit_bytes=VMEM_LIMIT),
        cost_estimate=pl.CostEstimate(
            flops=2 * window * slots * col_count * width * count,
            bytes_accessed=10 * count * width * (slots * col_count + window),
            transcendentals=0,
        ),
    )(meta, *pieces, got)


def unpack_kernel(col_count, meta_ref, *refs):
    pieces, outs, choose = refs[: -1 - col_count], refs[-1 - col_count : -1], refs[-1]
    turn = pl.program_id(0)
    _, slots, window = choose.shape

    @pl.when(turn == 0)
    def _():
        rows = lax.broadcasted_iota(jnp.int32, (slots, window), 1)
        columns = lax.broadcasted_iota(jnp.int32, (slots, window), 0)
        for k in range(col_count):
            hit = (rows == columns + meta_ref[2 + k]) & (columns < meta_ref[2 + col_count + k])
            choose[k] = jnp.where(hit, 1.0, 0.0).astype(jnp.bfloat16)

    for q, piece in enumerate(pieces):

        @pl.when(turn == q)
        def _():
            for k in range(col_count):
                outs[k][...] = jnp.dot(
                    choose[k], piece[...], preferred_element_type=jnp.float32
                ).astype(jnp.bfloat16)


def unpack(meta, pieces, col_count, slots, step):
    window, width = pieces[0].shape
    count = len(pieces)
    return pl.pallas_call(
        lambda *refs: unpack_kernel(col_count, *refs),
        out_shape=[jax.ShapeDtypeStruct((slots, count * width), jnp.bfloat16)] * col_count,
        grid_spec=pltpu.PrefetchScalarGridSpec(
            num_scalar_prefetch=1,
            grid=(count,),
            in_specs=[pl.BlockSpec((window, width), lambda q, meta: (0, 0))] * count,
            out_specs=[pl.BlockSpec((slots, width), lambda q, meta: (0, (meta[0] // step) ^ q))]
            * col_count,
            scratch_shapes=[pltpu.VMEM((col_count, slots, window), jnp.bfloat16)],
        ),
        compiler_params=pltpu.CompilerParams(vmem_limit_bytes=VMEM_LIMIT),
        cost_estimate=pl.CostEstimate(
            flops=2 * window * slots * col_count * width * count,
            bytes_accessed=10 * count * width * (slots * col_count + window),
            transcendentals=0,
        ),
    )(meta, *pieces)


def merge_kernel(unit, share, distances, meta_ref, *refs):
    pieces, out_ref, total = refs[:-2], refs[-2], refs[-1]
    jitter = (total.shape[0] - M) // 2
    total[...] = jnp.zeros_like(total)
    for places, piece in zip(distances, pieces):
        rows = piece.shape[0] // len(places)
        for n, distance in enumerate(places):
            place = pl.ds(pl.multiple_of(((meta_ref[0] // share) ^ distance) * unit, 8), rows)
            total[place, :] += piece[n * rows : (n + 1) * rows, :].astype(jnp.float32)

    @pl.loop(0, BLOCKS)
    def _(b):
        source = pl.ds(pl.multiple_of(b * TILE + jitter, 8), TILE)
        out_ref[tile_rows(b), :] = total[source, :].astype(jnp.bfloat16)


def merge(meta, pieces, distances, unit, share, jitter):
    width = pieces[0].shape[1]
    return local_call(
        lambda *refs: merge_kernel(unit, share, distances, *refs),
        jax.ShapeDtypeStruct((M, width), jnp.bfloat16),
        (meta, *pieces),
        5 * M * width,
        [pltpu.VMEM((M + 2 * jitter, width), jnp.float32)],
    )


def collect_kernel(meta_ref, *refs):
    matrices, joined = refs[:-1], refs[-1]
    place = 0
    for matrix in matrices[:-1]:
        joined[:, place : place + matrix.shape[1]] = matrix[...]
        place += matrix.shape[1]
    lane = lax.broadcasted_iota(jnp.int32, (TILE, LAST), 1)
    own = lane // (LAST // 2) == meta_ref[0] % 2

    @pl.loop(0, BLOCKS)
    def _(b):
        block = matrices[-1][tile_rows(b), :].astype(jnp.float32)
        joined[tile_rows(b), place:] = jnp.where(own, block, 0.0).astype(jnp.bfloat16)


def collect(meta, chunks):
    width = sum(x.shape[1] for x in chunks)
    return local_call(
        collect_kernel,
        jax.ShapeDtypeStruct((M, width), jnp.bfloat16),
        (meta, *chunks),
        4 * M * width,
    )


PIECES = 2
HALF = len(PAIRS) // 2
PART = HALF // PIECES


def half_gram_kernel(flip, rows_ref, cols_ref, meta_ref, joined, *outs):
    turn = pl.program_id(0)
    pair = (meta_ref[0] % 2 ^ flip) * HALF + turn
    here = pl.ds(pl.multiple_of(rows_ref[pair] * TILE, TILE), TILE)
    there = pl.ds(pl.multiple_of(cols_ref[pair] * TILE, TILE), TILE)
    tile = lax.dot_general(
        joined[here, :],
        joined[there, :],
        (((1,), (1,)), ((), ())),
        preferred_element_type=jnp.float32,
    ).astype(jnp.bfloat16)
    for n, out in enumerate(outs):

        @pl.when(turn // PART == n)
        def _():
            out[...] = tile


def half_gram(meta, joined, flip):
    width = joined.shape[1]
    place = lambda n: lambda p, rows, cols, meta: (jnp.clip(p - n * PART, 0, PART - 1), 0)
    return pl.pallas_call(
        lambda *refs: half_gram_kernel(flip, *refs),
        out_shape=[jax.ShapeDtypeStruct((PART * TILE, TILE), jnp.bfloat16)] * PIECES,
        grid_spec=pltpu.PrefetchScalarGridSpec(
            num_scalar_prefetch=3,
            grid=(HALF,),
            in_specs=[pl.BlockSpec((M, width), lambda p, rows, cols, meta: (0, 0))],
            out_specs=[pl.BlockSpec((TILE, TILE), place(n)) for n in range(PIECES)],
        ),
        compiler_params=pltpu.CompilerParams(vmem_limit_bytes=VMEM_LIMIT),
        cost_estimate=pl.CostEstimate(
            flops=2 * HALF * TILE * TILE * width,
            bytes_accessed=2 * HALF * TILE * TILE + 2 * M * width,
            transcendentals=0,
        ),
    )(jnp.asarray(PAIR_ROWS), jnp.asarray(PAIR_COLS), meta, joined)


def lane_block(block, lanes):
    return pl.ds(pl.multiple_of(block * lanes, lanes), lanes)


def add_halves_kernel(meta_ref, *refs):
    count = len(refs) // 3
    for keep, got, out in zip(refs[:count], refs[count : 2 * count], refs[2 * count :]):
        out[...] = keep[...] + got[...]


def add_halves(meta, keep, got, col_count):
    rows, lanes = keep.shape
    lanes //= col_count
    tall = rows // 4
    place = lambda k: lambda t, meta: (t, meta[1] ^ k)
    return pl.pallas_call(
        add_halves_kernel,
        out_shape=[jax.ShapeDtypeStruct((rows, lanes), jnp.bfloat16)] * col_count,
        grid_spec=pltpu.PrefetchScalarGridSpec(
            num_scalar_prefetch=1,
            grid=(rows // tall,),
            in_specs=[pl.BlockSpec((tall, lanes), place(k)) for k in range(col_count)] * 2,
            out_specs=[pl.BlockSpec((tall, lanes), lambda t, meta: (t, 0))] * col_count,
        ),
        compiler_params=pltpu.CompilerParams(vmem_limit_bytes=VMEM_LIMIT),
        cost_estimate=pl.CostEstimate(
            flops=keep.size, bytes_accessed=6 * keep.size, transcendentals=0
        ),
    )(meta, *[keep] * col_count, *[got] * col_count)


def total_of(refs, part):
    total = refs[0][part, :].astype(jnp.float32)
    for ref in refs[1:]:
        total += ref[part, :].astype(jnp.float32)
    return total.astype(jnp.bfloat16)


def add_quarters_kernel(col_count, meta_ref, *refs):
    blocks, outs = refs[:col_count], refs[col_count:]
    rows = outs[0].shape[0]
    for q, out in enumerate(outs):
        place = (meta_ref[0] // 2 ^ q) * rows
        out[...] = total_of(blocks, pl.ds(pl.multiple_of(place, rows), rows))


def add_quarters(meta, blocks, pair_count):
    rows, lanes = blocks[0].shape
    shape = jax.ShapeDtypeStruct((rows // pair_count, lanes), jnp.bfloat16)
    return local_call(
        lambda *refs: add_quarters_kernel(len(blocks), *refs),
        [shape] * pair_count,
        (meta, *blocks),
        10 * rows * lanes,
    )


def add_parts_kernel(meta_ref, *refs):
    rows = refs[-1].shape[0]
    refs[-1][...] = total_of(refs[:-1], pl.ds(0, rows))


def add_parts(meta, parts):
    return local_call(
        add_parts_kernel,
        jax.ShapeDtypeStruct(parts[0].shape, jnp.bfloat16),
        (meta, *parts),
        10 * parts[0].size,
    )


def stack_kernel(order, meta_ref, *refs):
    parts, out = refs[:-1], refs[-1]
    rows = parts[0].shape[0]
    for q, part in zip(order, parts):
        out[pl.ds(pl.multiple_of((meta_ref[0] // 2 ^ q) * rows, rows), rows), :] = part[...]


def stack(meta, parts, order):
    rows, lanes = parts[0].shape
    return local_call(
        lambda *refs: stack_kernel(order, *refs),
        jax.ShapeDtypeStruct((rows * len(parts), lanes), jnp.bfloat16),
        (meta, *parts),
        4 * rows * lanes * len(parts),
    )


def tile_rows(b):
    return pl.ds(pl.multiple_of(b * TILE, TILE), TILE)


def first_product(panel, b, jitter, matrix, total, factor):
    product = jnp.dot(panel, matrix[...], preferred_element_type=jnp.float32)
    factor[tile_rows(b), :] = (coef_three * product).astype(jnp.bfloat16)
    total[pl.ds(pl.multiple_of(b * TILE + jitter, 8), TILE), :] = (
        coef_one * matrix[tile_rows(b), :].astype(jnp.float32) + coef_two * product
    )


def second_product(panel, b, jitter, total, factor):
    place = pl.ds(pl.multiple_of(b * TILE + jitter, 8), TILE)
    total[place, :] = math.sqrt(N) * (
        total[place, :] + jnp.dot(panel, factor[...], preferred_element_type=jnp.float32)
    )


def clear_edges(total, jitter):
    edge = jnp.zeros((jitter, total.shape[1]), jnp.float32)
    total[pl.ds(0, jitter), :] = edge
    total[pl.ds(M + jitter, jitter), :] = edge


def store_windows(row, send, total, outs):
    unit, share, rows, distances = send
    for distance, out in zip(distances, outs):
        place = pl.ds(pl.multiple_of(((row // share) ^ distance) * unit, 8), rows)
        out[...] = total[place, :].astype(jnp.bfloat16)


def first_apply_kernel(jitter, send, col_count, rows_ref, cols_ref, meta_ref, *refs):
    count = 2 * PIECES * col_count
    blocks, matrix, outs, gram_out = refs[:count], refs[count], refs[count + 1 : -6], refs[-6]
    gram, total, factor, tile_sems, out_sem = refs[-5:]
    lanes = TILE // col_count
    tiles = []
    for n in range(2 * HALF):
        half, part = divmod(n, HALF)
        pair = (meta_ref[0] % 2 ^ half) * HALF + part
        i, j = rows_ref[pair], cols_ref[pair]
        rows = pl.ds(part % PART * TILE, TILE)
        first = (half * PIECES + part // PART) * col_count
        moves = [
            (
                blocks[first + k].at[rows, :],
                gram.at[i, :, lane_block(j * col_count + (meta_ref[1] ^ k), lanes)],
            )
            for k in range(col_count)
        ]
        copies = [
            pltpu.make_async_copy(source, target, tile_sems.at[n, k])
            for k, (source, target) in enumerate(moves)
        ]
        for copy in copies:
            copy.start()
        tiles.append((copies, i, j))
    clear_edges(total, jitter)
    for copies, i, j in tiles:
        for copy in copies:
            copy.wait()

        @pl.when(i != j)
        def _():
            gram[j, :, lane_block(i, TILE)] = gram[i, :, lane_block(j, TILE)].T

    back = pltpu.make_async_copy(gram, gram_out, out_sem)
    back.start()

    @pl.loop(0, BLOCKS)
    def _(b):
        first_product(gram[b], b, jitter, matrix, total, factor)

    @pl.loop(0, BLOCKS)
    def _(b):
        second_product(gram[b], b, jitter, total, factor)

    store_windows(meta_ref[0], send, total, outs)
    back.wait()


def first_apply(meta, own, twin, matrix, send, jitter):
    pieces = [*own, *twin]
    col_count = len(own) // PIECES
    width = matrix.shape[1]
    whole = pl.BlockSpec(memory_space=pltpu.VMEM)
    outs = pl.pallas_call(
        lambda *refs: first_apply_kernel(jitter, send, col_count, *refs),
        out_shape=[jax.ShapeDtypeStruct((send[2], width), jnp.bfloat16)] * len(send[3])
        + [jax.ShapeDtypeStruct((BLOCKS, TILE, M), jnp.bfloat16)],
        in_specs=[pl.BlockSpec(memory_space=pltpu.SMEM)] * 3
        + [pl.BlockSpec(memory_space=pl.ANY)] * len(pieces)
        + [whole],
        out_specs=[whole] * len(send[3]) + [pl.BlockSpec(memory_space=pl.ANY)],
        scratch_shapes=[
            pltpu.VMEM((BLOCKS, TILE, M), jnp.bfloat16),
            pltpu.VMEM((M + 2 * jitter, width), jnp.float32),
            pltpu.VMEM((M, width), jnp.bfloat16),
            pltpu.SemaphoreType.DMA((len(PAIRS), col_count)),
            pltpu.SemaphoreType.DMA,
        ],
        compiler_params=pltpu.CompilerParams(vmem_limit_bytes=VMEM_LIMIT),
        cost_estimate=pl.CostEstimate(
            flops=4 * M * M * width, bytes_accessed=4 * M * width + 4 * M * M, transcendentals=0
        ),
    )(jnp.asarray(PAIR_ROWS), jnp.asarray(PAIR_COLS), meta, *pieces, matrix)
    return outs[:-1], outs[-1]


def next_apply_kernel(jitter, sends, meta_ref, panel_ref, *refs):
    chunks = len(sends)
    outs_count = sum(len(s[3]) for s in sends)
    matrices = refs[:chunks]
    outs = refs[chunks : chunks + outs_count]
    totals = refs[chunks + outs_count : 2 * chunks + outs_count]
    factors = refs[2 * chunks + outs_count :]
    turn = pl.program_id(0)

    @pl.when(turn < BLOCKS)
    def _():
        for matrix, total, factor in zip(matrices, totals, factors):
            first_product(panel_ref[0], turn, jitter, matrix, total, factor)

    @pl.when(turn >= BLOCKS)
    def _():
        for total, factor in zip(totals, factors):
            second_product(panel_ref[0], turn - BLOCKS, jitter, total, factor)

    @pl.when(turn == 2 * BLOCKS - 1)
    def _():
        place = 0
        for total, send in zip(totals, sends):
            clear_edges(total, jitter)
            store_windows(meta_ref[0], send, total, outs[place : place + len(send[3])])
            place += len(send[3])


def next_apply(meta, gram, matrices, sends, jitter):
    widths = [x.shape[1] for x in matrices]
    shapes = [(send[2], width) for width, send in zip(widths, sends) for _ in send[3]]
    whole = lambda t, meta: (0, 0)
    outs = pl.pallas_call(
        lambda *refs: next_apply_kernel(jitter, sends, *refs),
        out_shape=[jax.ShapeDtypeStruct(shape, jnp.bfloat16) for shape in shapes],
        grid_spec=pltpu.PrefetchScalarGridSpec(
            num_scalar_prefetch=1,
            grid=(2 * BLOCKS,),
            in_specs=[pl.BlockSpec((1, TILE, M), lambda t, meta: (t % BLOCKS, 0, 0))]
            + [pl.BlockSpec((M, width), whole) for width in widths],
            out_specs=[pl.BlockSpec(shape, whole) for shape in shapes],
            scratch_shapes=[pltpu.VMEM((M + 2 * jitter, width), jnp.float32) for width in widths]
            + [pltpu.VMEM((M, width), jnp.bfloat16) for width in widths],
        ),
        compiler_params=pltpu.CompilerParams(vmem_limit_bytes=VMEM_LIMIT),
        cost_estimate=pl.CostEstimate(
            flops=8 * M * M * sum(widths),
            bytes_accessed=4 * M * sum(widths) + 4 * M * M,
            transcendentals=0,
        ),
    )(meta, gram, *matrices)
    result = []
    for send in sends:
        result.append(outs[: len(send[3])])
        outs = outs[len(send[3]) :]
    return result


def sum_tiles(meta, joined, row_count, col_count):
    pair_count = row_count // 2
    tie = lax.optimization_barrier

    def over_cols(blocks):
        return [swap(blocks[k], "col", col_count, k) for k in range(1, col_count)]

    order = list(range(pair_count // 2, pair_count)) + list(range(1, pair_count // 2))

    def over_pairs(blocks):
        return [swap(blocks[q], "row", row_count, 2 * q) for q in order]

    give = half_gram(meta, joined, 1)
    got = [swap(piece, "row", row_count, 1) for piece in give]
    keep = half_gram(meta, joined, 0)

    early = add_halves(meta, keep[0], got[0], col_count)
    early_in = over_cols(early)
    late = add_halves(meta, keep[1], got[1], col_count)
    late, early_in = tie((late, early_in))
    late_in = over_cols(late)
    early_parts = add_quarters(meta, [early[0]] + early_in, pair_count)
    early_in = over_pairs(early_parts)
    early_part = add_parts(meta, [early_parts[0]] + early_in)
    early_in = over_pairs([early_part] * pair_count)
    late_in, early_in = tie((late_in, early_in))
    late_parts = add_quarters(meta, [late[0]] + late_in, pair_count)
    early_block = stack(meta, [early_part] + early_in, [0] + order)
    early_in = over_cols([early_block] * col_count)
    late_in = over_pairs(late_parts)
    late_part = add_parts(meta, [late_parts[0]] + late_in)
    late_in = over_pairs([late_part] * pair_count)
    late_in, early_in = tie((late_in, early_in))
    late_block = stack(meta, [late_part] + late_in, [0] + order)
    late_in = over_cols([late_block] * col_count)
    early = [early_block] + early_in
    early_twin = [swap(block, "row", row_count, 1) for block in early]
    late = [late_block] + late_in
    late_twin = [swap(block, "row", row_count, 1) for block in late]
    return early + late, early_twin + late_twin


def chunk_body(momentum_shards, shard_starts):
    col_count = lax.axis_size("col")
    row_count = lax.axis_size("row")
    pair_count = row_count // 2
    slots = momentum_shards.shape[0]
    mean_rows = M // (row_count * col_count)
    jitter = 4 * (mean_rows // 8)
    even = col_count * mean_rows
    window = even + 2 * jitter
    row = lax.axis_index("row").astype(jnp.int32)
    col = lax.axis_index("col").astype(jnp.int32)
    shard_ends = jnp.concatenate([shard_starts[1:], jnp.full((1,), M, jnp.int32)])
    members = row * col_count + (col ^ jnp.arange(col_count, dtype=jnp.int32))
    begins = shard_starts[members]
    meta = jnp.concatenate(
        [row[None], col[None], begins - (row * even - jitter), shard_ends[members] - begins]
    )

    wide = row_count * col_count * CHUNK
    number = (N // (row_count * col_count)) // CHUNK
    distances = list(range(pair_count))

    def fetch(base, span, after):
        place, after = lax.optimization_barrier((col, after))
        received = [
            swap(
                lax.dynamic_slice_in_dim(
                    momentum_shards, base + (place ^ k) * span, span, axis=1
                ),
                "col",
                col_count,
                k,
            )
            for k in range(1, col_count)
        ]
        return received, after

    def across(pieces):
        return [pieces[0]] + [swap(pieces[q], "row", row_count, 2 * q) for q in distances[1:]]

    far_first = distances[pair_count // 2 :] + distances[: pair_count // 2]

    def tie(crossed, other):
        ordered, other = lax.optimization_barrier(([crossed[q] for q in far_first], other))
        return [ordered[far_first.index(q)] for q in distances], other

    def gather_chunk(c, received):
        keep, give = pack_pair(
            meta, momentum_shards, received, c * wide, CHUNK, row_count, window
        )
        return join(meta, keep, swap(give, "row", row_count, 1), even, window, pair_count)

    last, _ = fetch(number * wide, pair_count * LAST, shard_starts)
    received, last = fetch(0, row_count * CHUNK, last)
    pieces = pack(
        meta, momentum_shards, last, number * wide, LAST, 2, pair_count, window
    )
    crossed_last, received = tie(across(pieces), received)
    joined = gather_chunk(0, received)
    landed = []
    for c in range(1, number):
        received, joined = fetch(c * wide, row_count * CHUNK, joined)
        crossed, received = tie(across(joined), received)
        landed.append(crossed)
        joined = gather_chunk(c, received)
    landed.append(across(joined))
    matrices = [
        merge(meta, pieces, [[q] for q in distances], 2 * even, 2, jitter) for pieces in landed
    ]
    twin = [swap(piece, "row", row_count, 1) for piece in crossed_last]
    matrices.append(
        merge(
            meta,
            crossed_last + twin,
            [[2 * q] for q in distances] + [[2 * q + 1] for q in distances],
            even,
            1,
            jitter,
        )
    )

    tiles = sum_tiles(meta, collect(meta, matrices), row_count, col_count)

    sends = [(2 * even, 2, even + window, distances)] * number
    sends.append((even, 1, window, [2 * q for q in distances]))
    first, gram = first_apply(meta, *tiles, matrices[0], sends[0], jitter)
    results = [first] + next_apply(meta, gram, matrices[1:], sends[1:], jitter)

    crossed = [across(results[0])]
    crossed[0], results[1:] = tie(crossed[0], results[1:])
    for pieces in results[1:]:
        crossed[-1], pieces = tie(crossed[-1], pieces)
        crossed.append(across(pieces))
    backs = []
    for c in range(number + 1):
        if c < number:
            got = swap(cut(meta, crossed[c], even, window), "row", row_count, 1)
            parts = list(
                unpack_pair(meta, crossed[c], got, col_count, slots, even, window)
            )
        else:
            parts = unpack(meta, crossed[c], col_count, slots, 2)
        if c + 1 == number:
            crossed[c + 1], parts[0] = tie(crossed[c + 1], parts[0])
        back = [parts[0]] + [swap(parts[k], "col", col_count, k) for k in range(1, col_count)]
        if c + 1 < number:
            crossed[c + 1], back = tie(crossed[c + 1], back)
        backs.append(back)
    out = jnp.zeros(momentum_shards.shape, jnp.bfloat16)
    for c, back in enumerate(backs):
        span = row_count * CHUNK if c < number else pair_count * LAST
        for k in range(col_count):
            out = lax.dynamic_update_slice_in_dim(
                out, back[k], c * wide + (col ^ k) * span, axis=1
            )
    return out


def body(momentum_shards, shard_starts):
    devices = lax.axis_size("col") * lax.axis_size("row")
    chunks = (N // devices) % CHUNK == LAST // 2 and N // devices > CHUNK
    powers = all(lax.axis_size(a) & (lax.axis_size(a) - 1) == 0 for a in ("row", "col"))
    jitter = 4 * (M // devices // 8)
    if chunks and powers and jitter % 8 == 0:
        return chunk_body(momentum_shards, shard_starts)
    return plain_body(momentum_shards, shard_starts)


def solution(mesh):
    in_specs = (P(("row", "col"), None), P())
    out_specs = P(("row", "col"), None)
    return jax.shard_map(body, mesh=mesh, in_specs=in_specs, out_specs=out_specs, check_vma=False)
```

```python
import math

import jax
import jax.numpy as jnp
import numpy as np
from jax import lax
from jax.experimental import pallas as pl
from jax.experimental.pallas import tpu as pltpu
from jax.sharding import PartitionSpec as P

M = 3584
N = 18432
TILE = 512
BLOCKS = M // TILE

coef_one = 3.4445
coef_two = -4.775
coef_three = 2.0315

PAIRS = [(i, j) for i in range(BLOCKS) for j in range(i, BLOCKS)]
PAIR_ROWS = np.array([i for i, _ in PAIRS], np.int32)
PAIR_COLS = np.array([j for _, j in PAIRS], np.int32)


def packing(shard_starts, row_block, col_count, shard_rows, window, first_row):
    shard_ends = jnp.concatenate([shard_starts[1:], jnp.full((1,), M, jnp.int32)])
    first_starts = lax.dynamic_slice_in_dim(shard_starts, row_block * col_count, col_count)
    last_ends = lax.dynamic_slice_in_dim(shard_ends, row_block * col_count, col_count)
    slot_index = jnp.arange(col_count * shard_rows, dtype=jnp.int32)
    member = slot_index // shard_rows
    offset = slot_index % shard_rows
    pick = member[:, None] == jnp.arange(col_count, dtype=jnp.int32)[None, :]
    shard_begin = jnp.sum(jnp.where(pick, first_starts[None, :], 0), axis=1)
    length = jnp.sum(jnp.where(pick, (last_ends - first_starts)[None, :], 0), axis=1)
    target = shard_begin - first_row + offset
    is_valid = offset < length
    window_rows = jnp.arange(window, dtype=jnp.int32)
    return ((window_rows[:, None] == target[None, :]) & is_valid[None, :]).astype(jnp.bfloat16)


def gram_kernel(rows_ref, cols_ref, left_ref, right_ref, out_ref):
    out_ref[...] = lax.dot_general(
        left_ref[...], right_ref[...], (((1,), (1,)), ((), ())), preferred_element_type=jnp.float32
    ).astype(jnp.bfloat16)


def gram_tiles(matrix):
    width = matrix.shape[1]
    count = len(PAIRS)
    return pl.pallas_call(
        gram_kernel,
        out_shape=jax.ShapeDtypeStruct((count * TILE, TILE), jnp.bfloat16),
        grid_spec=pltpu.PrefetchScalarGridSpec(
            num_scalar_prefetch=2,
            grid=(count,),
            in_specs=[
                pl.BlockSpec((TILE, width), lambda p, rows, cols: (rows[p], 0)),
                pl.BlockSpec((TILE, width), lambda p, rows, cols: (cols[p], 0)),
            ],
            out_specs=pl.BlockSpec((TILE, TILE), lambda p, rows, cols: (p, 0)),
        ),
        compiler_params=pltpu.CompilerParams(vmem_limit_bytes=32 * 1024 * 1024),
        cost_estimate=pl.CostEstimate(
            flops=2 * count * TILE * TILE * width,
            bytes_accessed=2 * count * TILE * (TILE + width),
            transcendentals=0,
        ),
    )(jnp.asarray(PAIR_ROWS), jnp.asarray(PAIR_COLS), matrix, matrix)


def apply_kernel(rows_ref, cols_ref, tile_ref, matrix_ref, out_ref, total, factor):
    turn = pl.program_id(0)
    pair = pl.program_id(1)
    i = rows_ref[pair]
    j = cols_ref[pair]
    here = pl.ds(pl.multiple_of(i * TILE, TILE), TILE)
    there = pl.ds(pl.multiple_of(j * TILE, TILE), TILE)

    @pl.when((turn == 0) & (pair == 0))
    def _():
        total[...] = jnp.zeros_like(total)
        factor[...] = matrix_ref[...]

    @pl.when((turn == 1) & (pair == 0))
    def _():
        @pl.loop(0, BLOCKS)
        def _(b):
            part = pl.ds(pl.multiple_of(b * TILE, TILE), TILE)
            product = total[part, :]
            factor[part, :] = (coef_three * product).astype(jnp.bfloat16)
            total[part, :] = coef_one * matrix_ref[part, :].astype(jnp.float32) + coef_two * product

    total[here, :] += jnp.dot(tile_ref[...], factor[there, :], preferred_element_type=jnp.float32)

    @pl.when(i != j)
    def _():
        total[there, :] += lax.dot_general(
            tile_ref[...], factor[here, :], (((0,), (0,)), ((), ())), preferred_element_type=jnp.float32
        )

    @pl.when((turn == 1) & (pair == pl.num_programs(1) - 1))
    def _():
        @pl.loop(0, BLOCKS)
        def _(b):
            part = pl.ds(pl.multiple_of(b * TILE, TILE), TILE)
            out_ref[part, :] = (math.sqrt(N) * total[part, :]).astype(jnp.bfloat16)


def apply_polynomial(tiles, matrix):
    rows, width = matrix.shape
    count = len(PAIRS)
    return pl.pallas_call(
        apply_kernel,
        out_shape=jax.ShapeDtypeStruct((rows, width), jnp.bfloat16),
        grid_spec=pltpu.PrefetchScalarGridSpec(
            num_scalar_prefetch=2,
            grid=(2, count),
            in_specs=[
                pl.BlockSpec((TILE, TILE), lambda t, p, rows, cols: (p, 0)),
                pl.BlockSpec((rows, width), lambda t, p, rows, cols: (0, 0)),
            ],
            out_specs=pl.BlockSpec((rows, width), lambda t, p, rows, cols: (0, 0)),
            scratch_shapes=[
                pltpu.VMEM((rows, width), jnp.float32),
                pltpu.VMEM((rows, width), jnp.bfloat16),
            ],
        ),
        compiler_params=pltpu.CompilerParams(vmem_limit_bytes=48 * 1024 * 1024),
        cost_estimate=pl.CostEstimate(
            flops=4 * rows * rows * width,
            bytes_accessed=4 * rows * width + 4 * count * TILE * TILE,
            transcendentals=0,
        ),
    )(jnp.asarray(PAIR_ROWS), jnp.asarray(PAIR_COLS), tiles, matrix)


def plain_body(momentum_shards, shard_starts):
    col_count = lax.axis_size("col")
    row_count = lax.axis_size("row")
    shard_rows = momentum_shards.shape[0]
    mean_rows = M // (row_count * col_count)
    jitter = 4 * (mean_rows // 8)
    even = col_count * mean_rows
    window = even + 2 * jitter
    row_block = lax.axis_index("row")
    packer = packing(
        shard_starts, row_block, col_count, shard_rows, window, row_block * even - jitter
    )
    columns = lax.all_to_all(momentum_shards, "col", split_axis=1, concat_axis=0, tiled=True)
    local_tile = jnp.dot(packer, columns, preferred_element_type=jnp.float32).astype(jnp.bfloat16)
    windows = lax.all_to_all(local_tile, "row", split_axis=1, concat_axis=0, tiled=True)
    width = windows.shape[1]
    windows = windows.reshape(row_count, window, width)
    nothing = jnp.zeros((1, jitter, width), jnp.bfloat16)
    head = jnp.concatenate([nothing, windows[:-1, jitter + even :]], axis=0)
    tail = jnp.concatenate([windows[1:, :jitter], nothing], axis=0)
    middle = windows[:, jitter : jitter + even]
    matrix = jnp.concatenate(
        [
            middle[:, :jitter] + head,
            middle[:, jitter : even - jitter],
            middle[:, even - jitter :] + tail,
        ],
        axis=1,
    ).reshape(M, width)

    tiles = lax.psum(gram_tiles(matrix), ("row", "col"))
    update = apply_polynomial(tiles, matrix).reshape(row_count, even, width)

    before = jnp.concatenate([nothing, update[:-1, even - jitter :]], axis=0)
    after = jnp.concatenate([update[1:, :jitter], nothing], axis=0)
    spread = jnp.concatenate([before, update, after], axis=1).reshape(row_count * window, width)
    own_rows = lax.all_to_all(spread, "row", split_axis=0, concat_axis=1, tiled=True)
    back_rows = lax.dot_general(
        packer, own_rows, (((0,), (0,)), ((), ())), preferred_element_type=jnp.float32
    ).astype(jnp.bfloat16)
    return lax.all_to_all(back_rows, "col", split_axis=0, concat_axis=1, tiled=True)


CHUNK = 256
LAST = 128
VMEM_LIMIT = 56 * 1024 * 1024


def swap(value, axis, size, distance):
    return lax.ppermute(value, axis, perm=[(i, i ^ distance) for i in range(size)])


def pack_kernel(step, col_count, meta_ref, *refs):
    pieces, choose, outs = refs[:col_count], refs[col_count], refs[col_count + 1 :]
    turn = pl.program_id(0)

    total = jnp.dot(choose[0], pieces[0][...], preferred_element_type=jnp.float32)
    for k in range(1, col_count):
        total += jnp.dot(choose[k], pieces[k][...], preferred_element_type=jnp.float32)
    for q, out in enumerate(outs):

        @pl.when(turn == q)
        def _():
            out[...] = total.astype(jnp.bfloat16)


def pack(meta, choose, momentum, received, base, width, step, count, window):
    slots = momentum.shape[0]
    col_count = len(received) + 1
    first = base // width
    return pl.pallas_call(
        lambda *refs: pack_kernel(step, col_count, *refs),
        out_shape=[jax.ShapeDtypeStruct((window, width), jnp.bfloat16)] * count,
        grid_spec=pltpu.PrefetchScalarGridSpec(
            num_scalar_prefetch=1,
            grid=(count,),
            in_specs=[
                pl.BlockSpec(
                    (slots, width),
                    lambda q, meta: (0, first + meta[1] * count + ((meta[0] // step) ^ q)),
                )
            ]
            + [pl.BlockSpec((slots, width), lambda q, meta: (0, (meta[0] // step) ^ q))]
            * (col_count - 1)
            + [pl.BlockSpec(choose.shape, lambda q, meta: (0, 0, 0))],
            out_specs=[pl.BlockSpec((window, width), lambda q, meta: (0, 0))] * count,
        ),
        compiler_params=pltpu.CompilerParams(vmem_limit_bytes=VMEM_LIMIT),
        cost_estimate=pl.CostEstimate(
            flops=2 * window * slots * col_count * width * count,
            bytes_accessed=2 * count * width * (slots * col_count + window),
            transcendentals=0,
        ),
    )(meta, momentum, *received, choose)


def pack_pair_kernel(col_count, meta_ref, *refs):
    pieces, choose, keep, give = refs[:col_count], refs[-3], refs[-2], refs[-1]
    other = pl.program_id(0) == 0

    total = jnp.dot(choose[0], pieces[0][...], preferred_element_type=jnp.float32)
    for k in range(1, col_count):
        total += jnp.dot(choose[k], pieces[k][...], preferred_element_type=jnp.float32)

    @pl.when(other)
    def _():
        give[...] = total.astype(jnp.bfloat16)

    @pl.when(jnp.logical_not(other))
    def _():
        keep[...] = total.astype(jnp.bfloat16)


def selections(meta, col_count, slots, window):
    begin, length = meta[2 : 2 + col_count], meta[2 + col_count :]
    row = jnp.arange(window, dtype=jnp.int32)[None, :, None]
    slot = jnp.arange(slots, dtype=jnp.int32)[None, None, :]
    hit = (row == slot + begin[:, None, None]) & (slot < length[:, None, None])
    return hit.astype(jnp.bfloat16)


def pack_pair(meta, choose, momentum, received, base, width, row_count, window):
    slots = momentum.shape[0]
    col_count = len(received) + 1
    pairs = row_count // 2
    first = base // width
    block = lambda e, q, meta: meta[0] ^ (2 * q + 1 - e)
    shape = jax.ShapeDtypeStruct((pairs * window, width), jnp.bfloat16)
    return pl.pallas_call(
        lambda *refs: pack_pair_kernel(col_count, *refs),
        out_shape=[shape, shape],
        grid_spec=pltpu.PrefetchScalarGridSpec(
            num_scalar_prefetch=1,
            grid=(2, pairs),
            in_specs=[
                pl.BlockSpec(
                    (slots, width),
                    lambda e, q, meta: (0, first + meta[1] * row_count + block(e, q, meta)),
                )
            ]
            + [pl.BlockSpec((slots, width), lambda e, q, meta: (0, block(e, q, meta)))]
            * (col_count - 1)
            + [pl.BlockSpec(choose.shape, lambda e, q, meta: (0, 0, 0))],
            out_specs=[
                pl.BlockSpec((window, width), lambda e, q, meta: (jnp.where(e == 0, 0, q), 0)),
                pl.BlockSpec(
                    (window, width), lambda e, q, meta: (jnp.where(e == 0, q, pairs - 1), 0)
                ),
            ],
        ),
        compiler_params=pltpu.CompilerParams(vmem_limit_bytes=VMEM_LIMIT),
        cost_estimate=pl.CostEstimate(
            flops=2 * window * slots * col_count * width * row_count,
            bytes_accessed=2 * row_count * width * (slots * col_count + window),
            transcendentals=0,
        ),
    )(meta, momentum, *received, choose)


def join_kernel(even, window, meta_ref, keep, got, *outs):
    def write(low, high):
        for q, out in enumerate(outs):
            base = q * window
            lap = window - even
            out[:even, :] = low[base : base + even, :]
            out[even:window, :] = (
                low[base + even : base + window, :].astype(jnp.float32)
                + high[base : base + lap, :].astype(jnp.float32)
            ).astype(jnp.bfloat16)
            out[window:, :] = high[base + lap : base + window, :]

    @pl.when(meta_ref[0] % 2 == 0)
    def _():
        write(keep, got)

    @pl.when(meta_ref[0] % 2 == 1)
    def _():
        write(got, keep)


def local_call(kernel, out_shape, operands, moved, scratch=()):
    whole = pl.BlockSpec(memory_space=pltpu.VMEM)
    return pl.pallas_call(
        kernel,
        out_shape=out_shape,
        in_specs=[pl.BlockSpec(memory_space=pltpu.SMEM)] + [whole] * (len(operands) - 1),
        out_specs=jax.tree.map(lambda _: whole, out_shape),
        scratch_shapes=list(scratch),
        compiler_params=pltpu.CompilerParams(vmem_limit_bytes=VMEM_LIMIT),
        cost_estimate=pl.CostEstimate(flops=moved, bytes_accessed=moved, transcendentals=0),
    )(*operands)


def join(meta, keep, got, even, window, pairs):
    width = keep.shape[1]
    shape = jax.ShapeDtypeStruct((even + window, width), jnp.bfloat16)
    return local_call(
        lambda *refs: join_kernel(even, window, *refs),
        [shape] * pairs,
        (meta, keep, got),
        8 * pairs * window * width,
    )


def cut_kernel(even, window, meta_ref, *refs):
    pieces, out = refs[:-1], refs[-1]
    place = pl.ds(pl.multiple_of((1 - meta_ref[0] % 2) * even, 16), window)
    for q, piece in enumerate(pieces):
        out[q * window : (q + 1) * window, :] = piece[place, :]


def cut(meta, pieces, even, window):
    width = pieces[0].shape[1]
    return local_call(
        lambda *refs: cut_kernel(even, window, *refs),
        jax.ShapeDtypeStruct((len(pieces) * window, width), jnp.bfloat16),
        (meta, *pieces),
        4 * len(pieces) * window * width,
    )


def unpack_pair_kernel(col_count, even, window, meta_ref, *refs):
    pieces, outs = refs[: -2 - col_count], refs[-col_count:]
    got, choose = refs[-2 - col_count], refs[-1 - col_count]
    turn = pl.program_id(0)

    def place(block):
        for k in range(col_count):
            outs[k][...] = jnp.dot(
                choose[k], block, preferred_element_type=jnp.float32
            ).astype(jnp.bfloat16)

    for q, piece in enumerate(pieces):

        @pl.when(turn == 2 * q)
        def _():
            own = pl.ds(pl.multiple_of(meta_ref[0] % 2 * even, 16), window)
            place(piece[own, :])

    @pl.when(turn % 2 == 1)
    def _():
        part = pl.ds(pl.multiple_of(turn // 2 * window, 16), window)
        place(got[part, :])


def unpack_pair(meta, choose, pieces, got, col_count, slots, even, window):
    width = got.shape[1]
    count = 2 * len(pieces)
    return pl.pallas_call(
        lambda *refs: unpack_pair_kernel(col_count, even, window, *refs),
        out_shape=[jax.ShapeDtypeStruct((slots, count * width), jnp.bfloat16)] * col_count,
        grid_spec=pltpu.PrefetchScalarGridSpec(
            num_scalar_prefetch=1,
            grid=(count,),
            in_specs=[pl.BlockSpec(x.shape, lambda q, meta: (0, 0)) for x in (*pieces, got)]
            + [pl.BlockSpec(choose.shape, lambda q, meta: (0, 0, 0))],
            out_specs=[pl.BlockSpec((slots, width), lambda q, meta: (0, meta[0] ^ q))]
            * col_count,
        ),
        compiler_params=pltpu.CompilerParams(vmem_limit_bytes=VMEM_LIMIT),
        cost_estimate=pl.CostEstimate(
            flops=2 * window * slots * col_count * width * count,
            bytes_accessed=2 * count * width * (slots * col_count + window),
            transcendentals=0,
        ),
    )(meta, *pieces, got, choose)


def unpack_kernel(col_count, meta_ref, *refs):
    pieces, choose, outs = refs[: -1 - col_count], refs[-1 - col_count], refs[-col_count:]
    turn = pl.program_id(0)

    for q, piece in enumerate(pieces):

        @pl.when(turn == q)
        def _():
            for k in range(col_count):
                outs[k][...] = jnp.dot(
                    choose[k], piece[...], preferred_element_type=jnp.float32
                ).astype(jnp.bfloat16)


def unpack(meta, choose, pieces, col_count, slots, step):
    window, width = pieces[0].shape
    count = len(pieces)
    return pl.pallas_call(
        lambda *refs: unpack_kernel(col_count, *refs),
        out_shape=[jax.ShapeDtypeStruct((slots, count * width), jnp.bfloat16)] * col_count,
        grid_spec=pltpu.PrefetchScalarGridSpec(
            num_scalar_prefetch=1,
            grid=(count,),
            in_specs=[pl.BlockSpec((window, width), lambda q, meta: (0, 0))] * count
            + [pl.BlockSpec(choose.shape, lambda q, meta: (0, 0, 0))],
            out_specs=[pl.BlockSpec((slots, width), lambda q, meta: (0, (meta[0] // step) ^ q))]
            * col_count,
        ),
        compiler_params=pltpu.CompilerParams(vmem_limit_bytes=VMEM_LIMIT),
        cost_estimate=pl.CostEstimate(
            flops=2 * window * slots * col_count * width * count,
            bytes_accessed=2 * count * width * (slots * col_count + window),
            transcendentals=0,
        ),
    )(meta, *pieces, choose)


def merge_kernel(unit, share, distances, meta_ref, *refs):
    pieces, out_ref, total = refs[:-2], refs[-2], refs[-1]
    jitter = (total.shape[0] - M) // 2
    total[...] = jnp.zeros_like(total)
    for places, piece in zip(distances, pieces):
        rows = piece.shape[0] // len(places)
        for n, distance in enumerate(places):
            place = pl.ds(pl.multiple_of(((meta_ref[0] // share) ^ distance) * unit, 8), rows)
            total[place, :] += piece[n * rows : (n + 1) * rows, :].astype(jnp.float32)

    @pl.loop(0, BLOCKS)
    def _(b):
        source = pl.ds(pl.multiple_of(b * TILE + jitter, 8), TILE)
        out_ref[tile_rows(b), :] = total[source, :].astype(jnp.bfloat16)


def merge(meta, pieces, distances, unit, share, jitter):
    width = pieces[0].shape[1]
    return local_call(
        lambda *refs: merge_kernel(unit, share, distances, *refs),
        jax.ShapeDtypeStruct((M, width), jnp.bfloat16),
        (meta, *pieces),
        5 * M * width,
        [pltpu.VMEM((M + 2 * jitter, width), jnp.float32)],
    )


def collect_kernel(meta_ref, *refs):
    matrices, joined = refs[:-1], refs[-1]
    place = 0
    for matrix in matrices[:-1]:
        joined[:, place : place + matrix.shape[1]] = matrix[...]
        place += matrix.shape[1]
    lane = lax.broadcasted_iota(jnp.int32, (TILE, LAST), 1)
    own = lane // (LAST // 2) == meta_ref[0] % 2

    @pl.loop(0, BLOCKS)
    def _(b):
        block = matrices[-1][tile_rows(b), :].astype(jnp.float32)
        joined[tile_rows(b), place:] = jnp.where(own, block, 0.0).astype(jnp.bfloat16)


def collect(meta, chunks):
    width = sum(x.shape[1] for x in chunks)
    return local_call(
        collect_kernel,
        jax.ShapeDtypeStruct((M, width), jnp.bfloat16),
        (meta, *chunks),
        4 * M * width,
    )


PIECES = 2
HALF = len(PAIRS) // 2
PART = HALF // PIECES


def half_gram_kernel(flip, first, rows_ref, cols_ref, meta_ref, joined, *outs):
    turn = pl.program_id(0)
    pair = (meta_ref[0] % 2 ^ flip) * HALF + first * PART + turn
    here = pl.ds(pl.multiple_of(rows_ref[pair] * TILE, TILE), TILE)
    there = pl.ds(pl.multiple_of(cols_ref[pair] * TILE, TILE), TILE)
    tile = lax.dot_general(
        joined[here, :],
        joined[there, :],
        (((1,), (1,)), ((), ())),
        preferred_element_type=jnp.float32,
    ).astype(jnp.bfloat16)
    for n, out in enumerate(outs):

        @pl.when(turn // PART == n)
        def _():
            out[...] = tile


def half_gram(meta, joined, flip, first, pieces):
    count = pieces * PART
    width = joined.shape[1]
    place = lambda n: lambda p, rows, cols, meta: (jnp.clip(p - n * PART, 0, PART - 1), 0)
    return pl.pallas_call(
        lambda *refs: half_gram_kernel(flip, first, *refs),
        out_shape=[jax.ShapeDtypeStruct((PART * TILE, TILE), jnp.bfloat16)] * pieces,
        grid_spec=pltpu.PrefetchScalarGridSpec(
            num_scalar_prefetch=3,
            grid=(count,),
            in_specs=[pl.BlockSpec((M, width), lambda p, rows, cols, meta: (0, 0))],
            out_specs=[pl.BlockSpec((TILE, TILE), place(n)) for n in range(pieces)],
        ),
        compiler_params=pltpu.CompilerParams(vmem_limit_bytes=VMEM_LIMIT),
        cost_estimate=pl.CostEstimate(
            flops=2 * count * TILE * TILE * width,
            bytes_accessed=2 * count * TILE * TILE + 2 * M * width,
            transcendentals=0,
        ),
    )(jnp.asarray(PAIR_ROWS), jnp.asarray(PAIR_COLS), meta, joined)


def lane_block(block, lanes):
    return pl.ds(pl.multiple_of(block * lanes, lanes), lanes)


def add_halves_kernel(meta_ref, *refs):
    count = len(refs) // 3
    for keep, got, out in zip(refs[:count], refs[count : 2 * count], refs[2 * count :]):
        out[...] = keep[...] + got[...]


def add_halves(meta, keep, got, col_count):
    rows, lanes = keep.shape
    lanes //= col_count
    tall = rows // 4
    place = lambda k: lambda t, meta: (t, meta[1] ^ k)
    return pl.pallas_call(
        add_halves_kernel,
        out_shape=[jax.ShapeDtypeStruct((rows, lanes), jnp.bfloat16)] * col_count,
        grid_spec=pltpu.PrefetchScalarGridSpec(
            num_scalar_prefetch=1,
            grid=(rows // tall,),
            in_specs=[pl.BlockSpec((tall, lanes), place(k)) for k in range(col_count)] * 2,
            out_specs=[pl.BlockSpec((tall, lanes), lambda t, meta: (t, 0))] * col_count,
        ),
        compiler_params=pltpu.CompilerParams(vmem_limit_bytes=VMEM_LIMIT),
        cost_estimate=pl.CostEstimate(
            flops=keep.size, bytes_accessed=6 * keep.size, transcendentals=0
        ),
    )(meta, *[keep] * col_count, *[got] * col_count)


def total_of(refs, part):
    total = refs[0][part, :].astype(jnp.float32)
    for ref in refs[1:]:
        total += ref[part, :].astype(jnp.float32)
    return total.astype(jnp.bfloat16)


def add_quarters_kernel(col_count, meta_ref, *refs):
    blocks, outs = refs[:col_count], refs[col_count:]
    rows = outs[0].shape[0]
    for q, out in enumerate(outs):
        place = (meta_ref[0] // 2 ^ q) * rows
        out[...] = total_of(blocks, pl.ds(pl.multiple_of(place, rows), rows))


def add_quarters(meta, blocks, pair_count):
    rows, lanes = blocks[0].shape
    shape = jax.ShapeDtypeStruct((rows // pair_count, lanes), jnp.bfloat16)
    return local_call(
        lambda *refs: add_quarters_kernel(len(blocks), *refs),
        [shape] * pair_count,
        (meta, *blocks),
        10 * rows * lanes,
    )


def add_parts_kernel(meta_ref, *refs):
    rows = refs[-1].shape[0]
    refs[-1][...] = total_of(refs[:-1], pl.ds(0, rows))


def add_parts(meta, parts):
    return local_call(
        add_parts_kernel,
        jax.ShapeDtypeStruct(parts[0].shape, jnp.bfloat16),
        (meta, *parts),
        10 * parts[0].size,
    )


def stack_kernel(meta_ref, *refs):
    parts, out = refs[:-1], refs[-1]
    rows = parts[0].shape[0]
    for q, part in enumerate(parts):
        out[pl.ds(pl.multiple_of((meta_ref[0] // 2 ^ q) * rows, rows), rows), :] = part[...]


def stack(meta, parts):
    rows, lanes = parts[0].shape
    return local_call(
        stack_kernel,
        jax.ShapeDtypeStruct((rows * len(parts), lanes), jnp.bfloat16),
        (meta, *parts),
        4 * rows * lanes * len(parts),
    )


def tile_rows(b):
    return pl.ds(pl.multiple_of(b * TILE, TILE), TILE)


def first_product(panel, b, jitter, matrix, total, factor):
    product = jnp.dot(panel, matrix[...], preferred_element_type=jnp.float32)
    factor[tile_rows(b), :] = (coef_three * product).astype(jnp.bfloat16)
    total[pl.ds(pl.multiple_of(b * TILE + jitter, 8), TILE), :] = (
        coef_one * matrix[tile_rows(b), :].astype(jnp.float32) + coef_two * product
    )


def second_product(panel, b, jitter, total, factor):
    place = pl.ds(pl.multiple_of(b * TILE + jitter, 8), TILE)
    total[place, :] = math.sqrt(N) * (
        total[place, :] + jnp.dot(panel, factor[...], preferred_element_type=jnp.float32)
    )


def clear_edges(total, jitter):
    edge = jnp.zeros((jitter, total.shape[1]), jnp.float32)
    total[pl.ds(0, jitter), :] = edge
    total[pl.ds(M + jitter, jitter), :] = edge


def store_windows(row, send, total, outs):
    unit, share, rows, distances = send
    for distance, out in zip(distances, outs):
        place = pl.ds(pl.multiple_of(((row // share) ^ distance) * unit, 8), rows)
        out[...] = total[place, :].astype(jnp.bfloat16)


def first_apply_kernel(jitter, send, col_count, rows_ref, cols_ref, meta_ref, *refs):
    count = 2 * PIECES * col_count
    blocks, matrix, outs, gram_out = refs[:count], refs[count], refs[count + 1 : -6], refs[-6]
    gram, total, factor, tile_sems, out_sem = refs[-5:]
    lanes = TILE // col_count
    tiles = []
    for n in range(2 * HALF):
        half, part = divmod(n, HALF)
        pair = (meta_ref[0] % 2 ^ half) * HALF + part
        i, j = rows_ref[pair], cols_ref[pair]
        rows = pl.ds(part % PART * TILE, TILE)
        first = (half * PIECES + part // PART) * col_count
        moves = [
            (
                blocks[first + k].at[rows, :],
                gram.at[i, :, lane_block(j * col_count + (meta_ref[1] ^ k), lanes)],
            )
            for k in range(col_count)
        ]
        copies = [
            pltpu.make_async_copy(source, target, tile_sems.at[n, k])
            for k, (source, target) in enumerate(moves)
        ]
        for copy in copies:
            copy.start()
        tiles.append((copies, i, j))
    clear_edges(total, jitter)
    for copies, i, j in tiles:
        for copy in copies:
            copy.wait()

        @pl.when(i != j)
        def _():
            gram[j, :, lane_block(i, TILE)] = gram[i, :, lane_block(j, TILE)].T

    back = pltpu.make_async_copy(gram, gram_out, out_sem)
    back.start()

    @pl.loop(0, BLOCKS)
    def _(b):
        first_product(gram[b], b, jitter, matrix, total, factor)

    @pl.loop(0, BLOCKS)
    def _(b):
        second_product(gram[b], b, jitter, total, factor)

    store_windows(meta_ref[0], send, total, outs)
    back.wait()


def first_apply(meta, own, twin, matrix, send, jitter):
    pieces = [*own, *twin]
    col_count = len(own) // PIECES
    width = matrix.shape[1]
    whole = pl.BlockSpec(memory_space=pltpu.VMEM)
    outs = pl.pallas_call(
        lambda *refs: first_apply_kernel(jitter, send, col_count, *refs),
        out_shape=[jax.ShapeDtypeStruct((send[2], width), jnp.bfloat16)] * len(send[3])
        + [jax.ShapeDtypeStruct((BLOCKS, TILE, M), jnp.bfloat16)],
        in_specs=[pl.BlockSpec(memory_space=pltpu.SMEM)] * 3
        + [pl.BlockSpec(memory_space=pl.ANY)] * len(pieces)
        + [whole],
        out_specs=[whole] * len(send[3]) + [pl.BlockSpec(memory_space=pl.ANY)],
        scratch_shapes=[
            pltpu.VMEM((BLOCKS, TILE, M), jnp.bfloat16),
            pltpu.VMEM((M + 2 * jitter, width), jnp.float32),
            pltpu.VMEM((M, width), jnp.bfloat16),
            pltpu.SemaphoreType.DMA((len(PAIRS), col_count)),
            pltpu.SemaphoreType.DMA,
        ],
        compiler_params=pltpu.CompilerParams(vmem_limit_bytes=VMEM_LIMIT),
        cost_estimate=pl.CostEstimate(
            flops=4 * M * M * width, bytes_accessed=4 * M * width + 4 * M * M, transcendentals=0
        ),
    )(jnp.asarray(PAIR_ROWS), jnp.asarray(PAIR_COLS), meta, *pieces, matrix)
    return outs[:-1], outs[-1]


def next_apply_kernel(jitter, sends, meta_ref, panel_ref, *refs):
    chunks = len(sends)
    outs_count = sum(len(s[3]) for s in sends)
    matrices = refs[:chunks]
    outs = refs[chunks : chunks + outs_count]
    totals = refs[chunks + outs_count : 2 * chunks + outs_count]
    factors = refs[2 * chunks + outs_count :]
    turn = pl.program_id(0)

    @pl.when(turn < BLOCKS)
    def _():
        for matrix, total, factor in zip(matrices, totals, factors):
            first_product(panel_ref[0], turn, jitter, matrix, total, factor)

    @pl.when(turn >= BLOCKS)
    def _():
        for total, factor in zip(totals, factors):
            second_product(panel_ref[0], turn - BLOCKS, jitter, total, factor)

    @pl.when(turn == 2 * BLOCKS - 1)
    def _():
        place = 0
        for total, send in zip(totals, sends):
            clear_edges(total, jitter)
            store_windows(meta_ref[0], send, total, outs[place : place + len(send[3])])
            place += len(send[3])


def next_apply(meta, gram, matrices, sends, jitter):
    widths = [x.shape[1] for x in matrices]
    shapes = [(send[2], width) for width, send in zip(widths, sends) for _ in send[3]]
    whole = lambda t, meta: (0, 0)
    outs = pl.pallas_call(
        lambda *refs: next_apply_kernel(jitter, sends, *refs),
        out_shape=[jax.ShapeDtypeStruct(shape, jnp.bfloat16) for shape in shapes],
        grid_spec=pltpu.PrefetchScalarGridSpec(
            num_scalar_prefetch=1,
            grid=(2 * BLOCKS,),
            in_specs=[pl.BlockSpec((1, TILE, M), lambda t, meta: (t % BLOCKS, 0, 0))]
            + [pl.BlockSpec((M, width), whole) for width in widths],
            out_specs=[pl.BlockSpec(shape, whole) for shape in shapes],
            scratch_shapes=[pltpu.VMEM((M + 2 * jitter, width), jnp.float32) for width in widths]
            + [pltpu.VMEM((M, width), jnp.bfloat16) for width in widths],
        ),
        compiler_params=pltpu.CompilerParams(vmem_limit_bytes=VMEM_LIMIT),
        cost_estimate=pl.CostEstimate(
            flops=4 * M * M * sum(widths),
            bytes_accessed=4 * M * sum(widths) + 4 * M * M,
            transcendentals=0,
        ),
    )(meta, gram, *matrices)
    result = []
    for send in sends:
        result.append(outs[: len(send[3])])
        outs = outs[len(send[3]) :]
    return result


def sum_tiles(meta, joined, row_count, col_count):
    pair_count = row_count // 2
    tie = lax.optimization_barrier

    def over_cols(blocks):
        return [swap(blocks[k], "col", col_count, k) for k in range(1, col_count)]

    def over_pairs(blocks):
        return [swap(blocks[q], "row", row_count, 2 * q) for q in range(1, pair_count)]

    give = half_gram(meta, joined, 1, 0, PIECES)
    got = [swap(piece, "row", row_count, 1) for piece in give]
    keep = half_gram(meta, joined, 0, 0, 1)
    early = add_halves(meta, keep[0], got[0], col_count)
    early, joined = tie((early, joined))
    early_in = over_cols(early)
    keep = half_gram(meta, joined, 0, 1, 1)
    late = add_halves(meta, keep[0], got[1], col_count)
    late, early_in = tie((late, early_in))
    late_in = over_cols(late)
    early_parts = add_quarters(meta, [early[0]] + early_in, pair_count)
    early_in = over_pairs(early_parts)
    early_part = add_parts(meta, [early_parts[0]] + early_in)
    early_in = over_pairs([early_part] * pair_count)
    late_in, early_in = tie((late_in, early_in))
    late_parts = add_quarters(meta, [late[0]] + late_in, pair_count)
    early_block = stack(meta, [early_part] + early_in)
    early_in = over_cols([early_block] * col_count)
    late_in = over_pairs(late_parts)
    late_part = add_parts(meta, [late_parts[0]] + late_in)
    late_in = over_pairs([late_part] * pair_count)
    late_in, early_in = tie((late_in, early_in))
    late_block = stack(meta, [late_part] + late_in)
    late_in = over_cols([late_block] * col_count)
    early = [early_block] + early_in
    early_twin = [swap(block, "row", row_count, 1) for block in early]
    late = [late_block] + late_in
    late_twin = [swap(block, "row", row_count, 1) for block in late]
    return early + late, early_twin + late_twin


def chunk_body(momentum_shards, shard_starts):
    col_count = lax.axis_size("col")
    row_count = lax.axis_size("row")
    pair_count = row_count // 2
    slots = momentum_shards.shape[0]
    mean_rows = M // (row_count * col_count)
    jitter = 4 * (mean_rows // 8)
    even = col_count * mean_rows
    window = even + 2 * jitter
    row = lax.axis_index("row").astype(jnp.int32)
    col = lax.axis_index("col").astype(jnp.int32)
    shard_ends = jnp.concatenate([shard_starts[1:], jnp.full((1,), M, jnp.int32)])
    members = row * col_count + (col ^ jnp.arange(col_count, dtype=jnp.int32))
    begins = shard_starts[members]
    meta = jnp.concatenate(
        [row[None], col[None], begins - (row * even - jitter), shard_ends[members] - begins]
    )

    choose = selections(meta, col_count, slots, window)
    spread = jnp.swapaxes(choose, 1, 2)

    wide = row_count * col_count * CHUNK
    number = (N // (row_count * col_count)) // CHUNK
    distances = list(range(pair_count))

    def fetch(base, span, after):
        place, after = lax.optimization_barrier((col, after))
        received = [
            swap(
                lax.dynamic_slice_in_dim(
                    momentum_shards, base + (place ^ k) * span, span, axis=1
                ),
                "col",
                col_count,
                k,
            )
            for k in range(1, col_count)
        ]
        return received, after

    def across(pieces):
        return [pieces[0]] + [swap(pieces[q], "row", row_count, 2 * q) for q in distances[1:]]

    far_first = distances[pair_count // 2 :] + distances[: pair_count // 2]

    def tie(crossed, other):
        ordered, other = lax.optimization_barrier(([crossed[q] for q in far_first], other))
        return [ordered[far_first.index(q)] for q in distances], other

    def gather_chunk(c, received):
        keep, give = pack_pair(
            meta, choose, momentum_shards, received, c * wide, CHUNK, row_count, window
        )
        return join(meta, keep, swap(give, "row", row_count, 1), even, window, pair_count)

    last, _ = fetch(number * wide, pair_count * LAST, shard_starts)
    received, last = fetch(0, row_count * CHUNK, last)
    pieces = pack(
        meta, choose, momentum_shards, last, number * wide, LAST, 2, pair_count, window
    )
    crossed_last, received = tie(across(pieces), received)
    joined = gather_chunk(0, received)
    landed = []
    for c in range(1, number):
        received, joined = fetch(c * wide, row_count * CHUNK, joined)
        crossed, received = tie(across(joined), received)
        landed.append(crossed)
        joined = gather_chunk(c, received)
    landed.append(across(joined))
    matrices = [
        merge(meta, pieces, [[q] for q in distances], 2 * even, 2, jitter) for pieces in landed
    ]
    twin = [swap(piece, "row", row_count, 1) for piece in crossed_last]
    matrices.append(
        merge(
            meta,
            crossed_last + twin,
            [[2 * q] for q in distances] + [[2 * q + 1] for q in distances],
            even,
            1,
            jitter,
        )
    )

    tiles = sum_tiles(meta, collect(meta, matrices), row_count, col_count)

    sends = [(2 * even, 2, even + window, distances)] * number
    sends.append((even, 1, window, [2 * q for q in distances]))
    first, gram = first_apply(meta, *tiles, matrices[0], sends[0], jitter)
    results = [first] + next_apply(meta, gram, matrices[1:], sends[1:], jitter)

    crossed = [across(results[0])]
    crossed[0], results[1:] = tie(crossed[0], results[1:])
    for pieces in results[1:]:
        crossed[-1], pieces = tie(crossed[-1], pieces)
        crossed.append(across(pieces))
    backs = []
    for c in range(number + 1):
        if c < number:
            got = swap(cut(meta, crossed[c], even, window), "row", row_count, 1)
            parts = list(
                unpack_pair(meta, spread, crossed[c], got, col_count, slots, even, window)
            )
        else:
            parts = unpack(meta, spread, crossed[c], col_count, slots, 2)
        if c + 1 == number:
            crossed[c + 1], parts[0] = tie(crossed[c + 1], parts[0])
        back = [parts[0]] + [swap(parts[k], "col", col_count, k) for k in range(1, col_count)]
        if c + 1 < number:
            crossed[c + 1], back = tie(crossed[c + 1], back)
        backs.append(back)
    out = jnp.zeros(momentum_shards.shape, jnp.bfloat16)
    for c, back in enumerate(backs):
        span = row_count * CHUNK if c < number else pair_count * LAST
        for k in range(col_count):
            out = lax.dynamic_update_slice_in_dim(
                out, back[k], c * wide + (col ^ k) * span, axis=1
            )
    return out


def body(momentum_shards, shard_starts):
    devices = lax.axis_size("col") * lax.axis_size("row")
    chunks = (N // devices) % CHUNK == LAST // 2 and N // devices > CHUNK
    powers = all(lax.axis_size(a) & (lax.axis_size(a) - 1) == 0 for a in ("row", "col"))
    jitter = 4 * (M // devices // 8)
    if chunks and powers and jitter % 8 == 0:
        return chunk_body(momentum_shards, shard_starts)
    return plain_body(momentum_shards, shard_starts)


def solution(mesh):
    in_specs = (P(("row", "col"), None), P())
    out_specs = P(("row", "col"), None)
    return jax.shard_map(body, mesh=mesh, in_specs=in_specs, out_specs=out_specs, check_vma=False)
```

```python
import math

import jax
import jax.numpy as jnp
import numpy as np
from jax import lax
from jax.experimental import pallas as pl
from jax.experimental.pallas import tpu as pltpu
from jax.sharding import PartitionSpec as P

M = 3584
N = 18432
TILE = 512
BLOCKS = M // TILE

coef_one = 3.4445
coef_two = -4.775
coef_three = 2.0315

PAIRS = [(i, j) for i in range(BLOCKS) for j in range(i, BLOCKS)]
PAIR_ROWS = np.array([i for i, _ in PAIRS], np.int32)
PAIR_COLS = np.array([j for _, j in PAIRS], np.int32)


def packing(shard_starts, row_block, col_count, shard_rows, window, first_row):
    shard_ends = jnp.concatenate([shard_starts[1:], jnp.full((1,), M, jnp.int32)])
    first_starts = lax.dynamic_slice_in_dim(shard_starts, row_block * col_count, col_count)
    last_ends = lax.dynamic_slice_in_dim(shard_ends, row_block * col_count, col_count)
    slot_index = jnp.arange(col_count * shard_rows, dtype=jnp.int32)
    member = slot_index // shard_rows
    offset = slot_index % shard_rows
    pick = member[:, None] == jnp.arange(col_count, dtype=jnp.int32)[None, :]
    shard_begin = jnp.sum(jnp.where(pick, first_starts[None, :], 0), axis=1)
    length = jnp.sum(jnp.where(pick, (last_ends - first_starts)[None, :], 0), axis=1)
    target = shard_begin - first_row + offset
    is_valid = offset < length
    window_rows = jnp.arange(window, dtype=jnp.int32)
    return ((window_rows[:, None] == target[None, :]) & is_valid[None, :]).astype(jnp.bfloat16)


def gram_kernel(rows_ref, cols_ref, left_ref, right_ref, out_ref):
    out_ref[...] = lax.dot_general(
        left_ref[...], right_ref[...], (((1,), (1,)), ((), ())), preferred_element_type=jnp.float32
    ).astype(jnp.bfloat16)


def gram_tiles(matrix):
    width = matrix.shape[1]
    count = len(PAIRS)
    return pl.pallas_call(
        gram_kernel,
        out_shape=jax.ShapeDtypeStruct((count * TILE, TILE), jnp.bfloat16),
        grid_spec=pltpu.PrefetchScalarGridSpec(
            num_scalar_prefetch=2,
            grid=(count,),
            in_specs=[
                pl.BlockSpec((TILE, width), lambda p, rows, cols: (rows[p], 0)),
                pl.BlockSpec((TILE, width), lambda p, rows, cols: (cols[p], 0)),
            ],
            out_specs=pl.BlockSpec((TILE, TILE), lambda p, rows, cols: (p, 0)),
        ),
        compiler_params=pltpu.CompilerParams(vmem_limit_bytes=32 * 1024 * 1024),
        cost_estimate=pl.CostEstimate(
            flops=2 * count * TILE * TILE * width,
            bytes_accessed=2 * count * TILE * (TILE + width),
            transcendentals=0,
        ),
    )(jnp.asarray(PAIR_ROWS), jnp.asarray(PAIR_COLS), matrix, matrix)


def apply_kernel(rows_ref, cols_ref, tile_ref, matrix_ref, out_ref, total, factor):
    turn = pl.program_id(0)
    pair = pl.program_id(1)
    i = rows_ref[pair]
    j = cols_ref[pair]
    here = pl.ds(pl.multiple_of(i * TILE, TILE), TILE)
    there = pl.ds(pl.multiple_of(j * TILE, TILE), TILE)

    @pl.when((turn == 0) & (pair == 0))
    def _():
        total[...] = jnp.zeros_like(total)
        factor[...] = matrix_ref[...]

    @pl.when((turn == 1) & (pair == 0))
    def _():
        @pl.loop(0, BLOCKS)
        def _(b):
            part = pl.ds(pl.multiple_of(b * TILE, TILE), TILE)
            product = total[part, :]
            factor[part, :] = (coef_three * product).astype(jnp.bfloat16)
            total[part, :] = coef_one * matrix_ref[part, :].astype(jnp.float32) + coef_two * product

    total[here, :] += jnp.dot(tile_ref[...], factor[there, :], preferred_element_type=jnp.float32)

    @pl.when(i != j)
    def _():
        total[there, :] += lax.dot_general(
            tile_ref[...], factor[here, :], (((0,), (0,)), ((), ())), preferred_element_type=jnp.float32
        )

    @pl.when((turn == 1) & (pair == pl.num_programs(1) - 1))
    def _():
        @pl.loop(0, BLOCKS)
        def _(b):
            part = pl.ds(pl.multiple_of(b * TILE, TILE), TILE)
            out_ref[part, :] = (math.sqrt(N) * total[part, :]).astype(jnp.bfloat16)


def apply_polynomial(tiles, matrix):
    rows, width = matrix.shape
    count = len(PAIRS)
    return pl.pallas_call(
        apply_kernel,
        out_shape=jax.ShapeDtypeStruct((rows, width), jnp.bfloat16),
        grid_spec=pltpu.PrefetchScalarGridSpec(
            num_scalar_prefetch=2,
            grid=(2, count),
            in_specs=[
                pl.BlockSpec((TILE, TILE), lambda t, p, rows, cols: (p, 0)),
                pl.BlockSpec((rows, width), lambda t, p, rows, cols: (0, 0)),
            ],
            out_specs=pl.BlockSpec((rows, width), lambda t, p, rows, cols: (0, 0)),
            scratch_shapes=[
                pltpu.VMEM((rows, width), jnp.float32),
                pltpu.VMEM((rows, width), jnp.bfloat16),
            ],
        ),
        compiler_params=pltpu.CompilerParams(vmem_limit_bytes=48 * 1024 * 1024),
        cost_estimate=pl.CostEstimate(
            flops=4 * rows * rows * width,
            bytes_accessed=4 * rows * width + 4 * count * TILE * TILE,
            transcendentals=0,
        ),
    )(jnp.asarray(PAIR_ROWS), jnp.asarray(PAIR_COLS), tiles, matrix)


def plain_body(momentum_shards, shard_starts):
    col_count = lax.axis_size("col")
    row_count = lax.axis_size("row")
    shard_rows = momentum_shards.shape[0]
    mean_rows = M // (row_count * col_count)
    jitter = 4 * (mean_rows // 8)
    even = col_count * mean_rows
    window = even + 2 * jitter
    row_block = lax.axis_index("row")
    packer = packing(
        shard_starts, row_block, col_count, shard_rows, window, row_block * even - jitter
    )
    columns = lax.all_to_all(momentum_shards, "col", split_axis=1, concat_axis=0, tiled=True)
    local_tile = jnp.dot(packer, columns, preferred_element_type=jnp.float32).astype(jnp.bfloat16)
    windows = lax.all_to_all(local_tile, "row", split_axis=1, concat_axis=0, tiled=True)
    width = windows.shape[1]
    windows = windows.reshape(row_count, window, width)
    nothing = jnp.zeros((1, jitter, width), jnp.bfloat16)
    head = jnp.concatenate([nothing, windows[:-1, jitter + even :]], axis=0)
    tail = jnp.concatenate([windows[1:, :jitter], nothing], axis=0)
    middle = windows[:, jitter : jitter + even]
    matrix = jnp.concatenate(
        [
            middle[:, :jitter] + head,
            middle[:, jitter : even - jitter],
            middle[:, even - jitter :] + tail,
        ],
        axis=1,
    ).reshape(M, width)

    tiles = lax.psum(gram_tiles(matrix), ("row", "col"))
    update = apply_polynomial(tiles, matrix).reshape(row_count, even, width)

    before = jnp.concatenate([nothing, update[:-1, even - jitter :]], axis=0)
    after = jnp.concatenate([update[1:, :jitter], nothing], axis=0)
    spread = jnp.concatenate([before, update, after], axis=1).reshape(row_count * window, width)
    own_rows = lax.all_to_all(spread, "row", split_axis=0, concat_axis=1, tiled=True)
    back_rows = lax.dot_general(
        packer, own_rows, (((0,), (0,)), ((), ())), preferred_element_type=jnp.float32
    ).astype(jnp.bfloat16)
    return lax.all_to_all(back_rows, "col", split_axis=0, concat_axis=1, tiled=True)


CHUNK = 256
LAST = 128
VMEM_LIMIT = 56 * 1024 * 1024


def swap(value, axis, size, distance):
    return lax.ppermute(value, axis, perm=[(i, i ^ distance) for i in range(size)])


def pack_kernel(step, col_count, meta_ref, *refs):
    pieces, choose, outs = refs[:col_count], refs[col_count], refs[col_count + 1 :]
    turn = pl.program_id(0)

    total = jnp.dot(choose[0], pieces[0][...], preferred_element_type=jnp.float32)
    for k in range(1, col_count):
        total += jnp.dot(choose[k], pieces[k][...], preferred_element_type=jnp.float32)
    for q, out in enumerate(outs):

        @pl.when(turn == q)
        def _():
            out[...] = total.astype(jnp.bfloat16)


def pack(meta, choose, momentum, received, base, width, step, count, window):
    slots = momentum.shape[0]
    col_count = len(received) + 1
    first = base // width
    return pl.pallas_call(
        lambda *refs: pack_kernel(step, col_count, *refs),
        out_shape=[jax.ShapeDtypeStruct((window, width), jnp.bfloat16)] * count,
        grid_spec=pltpu.PrefetchScalarGridSpec(
            num_scalar_prefetch=1,
            grid=(count,),
            in_specs=[
                pl.BlockSpec(
                    (slots, width),
                    lambda q, meta: (0, first + meta[1] * count + ((meta[0] // step) ^ q)),
                )
            ]
            + [pl.BlockSpec((slots, width), lambda q, meta: (0, (meta[0] // step) ^ q))]
            * (col_count - 1)
            + [pl.BlockSpec(choose.shape, lambda q, meta: (0, 0, 0))],
            out_specs=[pl.BlockSpec((window, width), lambda q, meta: (0, 0))] * count,
        ),
        compiler_params=pltpu.CompilerParams(vmem_limit_bytes=VMEM_LIMIT),
        cost_estimate=pl.CostEstimate(
            flops=2 * window * slots * col_count * width * count,
            bytes_accessed=2 * count * width * (slots * col_count + window),
            transcendentals=0,
        ),
    )(meta, momentum, *received, choose)


def pack_pair_kernel(col_count, meta_ref, *refs):
    pieces, choose, keep, give = refs[:col_count], refs[-3], refs[-2], refs[-1]
    width = keep.shape[1]
    total = jnp.dot(choose[0], pieces[0][...], preferred_element_type=jnp.float32)
    for k in range(1, col_count):
        total += jnp.dot(choose[k], pieces[k][...], preferred_element_type=jnp.float32)
    block = total.astype(jnp.bfloat16)
    for core, (low, high) in enumerate(((keep, give), (give, keep))):

        @pl.when(meta_ref[0] % 2 == core)
        def _():
            low[...] = block[:, :width]
            high[...] = block[:, width:]


def selections(meta, col_count, slots, window):
    begin, length = meta[2 : 2 + col_count], meta[2 + col_count :]
    row = jnp.arange(window, dtype=jnp.int32)[None, :, None]
    slot = jnp.arange(slots, dtype=jnp.int32)[None, None, :]
    hit = (row == slot + begin[:, None, None]) & (slot < length[:, None, None])
    return hit.astype(jnp.bfloat16)


def pack_pair(meta, choose, momentum, received, base, width, row_count, window):
    slots = momentum.shape[0]
    col_count = len(received) + 1
    pairs = row_count // 2
    first = base // (2 * width)
    block = lambda q, meta: (meta[0] // 2) ^ q
    shape = jax.ShapeDtypeStruct((pairs * window, width), jnp.bfloat16)
    return pl.pallas_call(
        lambda *refs: pack_pair_kernel(col_count, *refs),
        out_shape=[shape, shape],
        grid_spec=pltpu.PrefetchScalarGridSpec(
            num_scalar_prefetch=1,
            grid=(pairs,),
            in_specs=[
                pl.BlockSpec(
                    (slots, 2 * width),
                    lambda q, meta: (0, first + meta[1] * pairs + block(q, meta)),
                )
            ]
            + [pl.BlockSpec((slots, 2 * width), lambda q, meta: (0, block(q, meta)))]
            * (col_count - 1)
            + [pl.BlockSpec(choose.shape, lambda q, meta: (0, 0, 0))],
            out_specs=[pl.BlockSpec((window, width), lambda q, meta: (q, 0))] * 2,
        ),
        compiler_params=pltpu.CompilerParams(vmem_limit_bytes=VMEM_LIMIT),
        cost_estimate=pl.CostEstimate(
            flops=2 * window * slots * col_count * width * row_count,
            bytes_accessed=2 * row_count * width * (slots * col_count + window),
            transcendentals=0,
        ),
    )(meta, momentum, *received, choose)


def join_kernel(even, window, meta_ref, keep, got, *outs):
    def write(low, high):
        for q, out in enumerate(outs):
            base = q * window
            lap = window - even
            out[:even, :] = low[base : base + even, :]
            out[even:window, :] = (
                low[base + even : base + window, :].astype(jnp.float32)
                + high[base : base + lap, :].astype(jnp.float32)
            ).astype(jnp.bfloat16)
            out[window:, :] = high[base + lap : base + window, :]

    @pl.when(meta_ref[0] % 2 == 0)
    def _():
        write(keep, got)

    @pl.when(meta_ref[0] % 2 == 1)
    def _():
        write(got, keep)


def local_call(kernel, out_shape, operands, moved, scratch=()):
    whole = pl.BlockSpec(memory_space=pltpu.VMEM)
    return pl.pallas_call(
        kernel,
        out_shape=out_shape,
        in_specs=[pl.BlockSpec(memory_space=pltpu.SMEM)] + [whole] * (len(operands) - 1),
        out_specs=jax.tree.map(lambda _: whole, out_shape),
        scratch_shapes=list(scratch),
        compiler_params=pltpu.CompilerParams(vmem_limit_bytes=VMEM_LIMIT),
        cost_estimate=pl.CostEstimate(flops=moved, bytes_accessed=moved, transcendentals=0),
    )(*operands)


def join(meta, keep, got, even, window, pairs):
    width = keep.shape[1]
    shape = jax.ShapeDtypeStruct((even + window, width), jnp.bfloat16)
    return local_call(
        lambda *refs: join_kernel(even, window, *refs),
        [shape] * pairs,
        (meta, keep, got),
        8 * pairs * window * width,
    )


def cut_kernel(even, window, meta_ref, *refs):
    pieces, out = refs[:-1], refs[-1]
    place = pl.ds(pl.multiple_of((1 - meta_ref[0] % 2) * even, 16), window)
    for q, piece in enumerate(pieces):
        out[q * window : (q + 1) * window, :] = piece[place, :]


def cut(meta, pieces, even, window):
    width = pieces[0].shape[1]
    return local_call(
        lambda *refs: cut_kernel(even, window, *refs),
        jax.ShapeDtypeStruct((len(pieces) * window, width), jnp.bfloat16),
        (meta, *pieces),
        4 * len(pieces) * window * width,
    )


def unpack_pair_kernel(col_count, even, window, meta_ref, *refs):
    pieces, outs = refs[: -2 - col_count], refs[-col_count:]
    got, choose = refs[-2 - col_count], refs[-1 - col_count]
    turn = pl.program_id(0)

    def place(block):
        for k in range(col_count):
            outs[k][...] = jnp.dot(
                choose[k], block, preferred_element_type=jnp.float32
            ).astype(jnp.bfloat16)

    for q, piece in enumerate(pieces):

        @pl.when(turn == 2 * q)
        def _():
            own = pl.ds(pl.multiple_of(meta_ref[0] % 2 * even, 16), window)
            place(piece[own, :])

    @pl.when(turn % 2 == 1)
    def _():
        part = pl.ds(pl.multiple_of(turn // 2 * window, 16), window)
        place(got[part, :])


def unpack_pair(meta, choose, pieces, got, col_count, slots, even, window):
    width = got.shape[1]
    count = 2 * len(pieces)
    return pl.pallas_call(
        lambda *refs: unpack_pair_kernel(col_count, even, window, *refs),
        out_shape=[jax.ShapeDtypeStruct((slots, count * width), jnp.bfloat16)] * col_count,
        grid_spec=pltpu.PrefetchScalarGridSpec(
            num_scalar_prefetch=1,
            grid=(count,),
            in_specs=[pl.BlockSpec(x.shape, lambda q, meta: (0, 0)) for x in (*pieces, got)]
            + [pl.BlockSpec(choose.shape, lambda q, meta: (0, 0, 0))],
            out_specs=[pl.BlockSpec((slots, width), lambda q, meta: (0, meta[0] ^ q))]
            * col_count,
        ),
        compiler_params=pltpu.CompilerParams(vmem_limit_bytes=VMEM_LIMIT),
        cost_estimate=pl.CostEstimate(
            flops=2 * window * slots * col_count * width * count,
            bytes_accessed=2 * count * width * (slots * col_count + window),
            transcendentals=0,
        ),
    )(meta, *pieces, got, choose)


def unpack_kernel(col_count, meta_ref, *refs):
    pieces, choose, outs = refs[: -1 - col_count], refs[-1 - col_count], refs[-col_count:]
    turn = pl.program_id(0)

    for q, piece in enumerate(pieces):

        @pl.when(turn == q)
        def _():
            for k in range(col_count):
                outs[k][...] = jnp.dot(
                    choose[k], piece[...], preferred_element_type=jnp.float32
                ).astype(jnp.bfloat16)


def unpack(meta, choose, pieces, col_count, slots, step):
    window, width = pieces[0].shape
    count = len(pieces)
    return pl.pallas_call(
        lambda *refs: unpack_kernel(col_count, *refs),
        out_shape=[jax.ShapeDtypeStruct((slots, count * width), jnp.bfloat16)] * col_count,
        grid_spec=pltpu.PrefetchScalarGridSpec(
            num_scalar_prefetch=1,
            grid=(count,),
            in_specs=[pl.BlockSpec((window, width), lambda q, meta: (0, 0))] * count
            + [pl.BlockSpec(choose.shape, lambda q, meta: (0, 0, 0))],
            out_specs=[pl.BlockSpec((slots, width), lambda q, meta: (0, (meta[0] // step) ^ q))]
            * col_count,
        ),
        compiler_params=pltpu.CompilerParams(vmem_limit_bytes=VMEM_LIMIT),
        cost_estimate=pl.CostEstimate(
            flops=2 * window * slots * col_count * width * count,
            bytes_accessed=2 * count * width * (slots * col_count + window),
            transcendentals=0,
        ),
    )(meta, *pieces, choose)


def merge_kernel(unit, share, distances, meta_ref, *refs):
    pieces, out_ref, total = refs[:-2], refs[-2], refs[-1]
    jitter = (total.shape[0] - M) // 2
    total[...] = jnp.zeros_like(total)
    for places, piece in zip(distances, pieces):
        rows = piece.shape[0] // len(places)
        for n, distance in enumerate(places):
            place = pl.ds(pl.multiple_of(((meta_ref[0] // share) ^ distance) * unit, 8), rows)
            total[place, :] += piece[n * rows : (n + 1) * rows, :].astype(jnp.float32)

    @pl.loop(0, BLOCKS)
    def _(b):
        source = pl.ds(pl.multiple_of(b * TILE + jitter, 8), TILE)
        out_ref[tile_rows(b), :] = total[source, :].astype(jnp.bfloat16)


def merge(meta, pieces, distances, unit, share, jitter):
    width = pieces[0].shape[1]
    return local_call(
        lambda *refs: merge_kernel(unit, share, distances, *refs),
        jax.ShapeDtypeStruct((M, width), jnp.bfloat16),
        (meta, *pieces),
        5 * M * width,
        [pltpu.VMEM((M + 2 * jitter, width), jnp.float32)],
    )


def collect_kernel(meta_ref, *refs):
    matrices, joined = refs[:-1], refs[-1]
    place = 0
    for matrix in matrices[:-1]:
        joined[:, place : place + matrix.shape[1]] = matrix[...]
        place += matrix.shape[1]
    lane = lax.broadcasted_iota(jnp.int32, (TILE, LAST), 1)
    own = lane // (LAST // 2) == meta_ref[0] % 2

    @pl.loop(0, BLOCKS)
    def _(b):
        block = matrices[-1][tile_rows(b), :].astype(jnp.float32)
        joined[tile_rows(b), place:] = jnp.where(own, block, 0.0).astype(jnp.bfloat16)


def collect(meta, chunks):
    width = sum(x.shape[1] for x in chunks)
    return local_call(
        collect_kernel,
        jax.ShapeDtypeStruct((M, width), jnp.bfloat16),
        (meta, *chunks),
        4 * M * width,
    )


PIECES = 2
HALF = len(PAIRS) // 2
PART = HALF // PIECES


def half_gram_kernel(flip, first, rows_ref, cols_ref, meta_ref, joined, *outs):
    turn = pl.program_id(0)
    pair = (meta_ref[0] % 2 ^ flip) * HALF + first * PART + turn
    here = pl.ds(pl.multiple_of(rows_ref[pair] * TILE, TILE), TILE)
    there = pl.ds(pl.multiple_of(cols_ref[pair] * TILE, TILE), TILE)
    tile = lax.dot_general(
        joined[here, :],
        joined[there, :],
        (((1,), (1,)), ((), ())),
        preferred_element_type=jnp.float32,
    ).astype(jnp.bfloat16)
    for n, out in enumerate(outs):

        @pl.when(turn // PART == n)
        def _():
            out[...] = tile


def half_gram(meta, joined, flip, first, pieces):
    count = pieces * PART
    width = joined.shape[1]
    place = lambda n: lambda p, rows, cols, meta: (jnp.clip(p - n * PART, 0, PART - 1), 0)
    return pl.pallas_call(
        lambda *refs: half_gram_kernel(flip, first, *refs),
        out_shape=[jax.ShapeDtypeStruct((PART * TILE, TILE), jnp.bfloat16)] * pieces,
        grid_spec=pltpu.PrefetchScalarGridSpec(
            num_scalar_prefetch=3,
            grid=(count,),
            in_specs=[pl.BlockSpec((M, width), lambda p, rows, cols, meta: (0, 0))],
            out_specs=[pl.BlockSpec((TILE, TILE), place(n)) for n in range(pieces)],
        ),
        compiler_params=pltpu.CompilerParams(vmem_limit_bytes=VMEM_LIMIT),
        cost_estimate=pl.CostEstimate(
            flops=2 * count * TILE * TILE * width,
            bytes_accessed=2 * count * TILE * TILE + 2 * M * width,
            transcendentals=0,
        ),
    )(jnp.asarray(PAIR_ROWS), jnp.asarray(PAIR_COLS), meta, joined)


def lane_block(block, lanes):
    return pl.ds(pl.multiple_of(block * lanes, lanes), lanes)


def add_halves_kernel(meta_ref, *refs):
    count = len(refs) // 3
    for keep, got, out in zip(refs[:count], refs[count : 2 * count], refs[2 * count :]):
        out[...] = keep[...] + got[...]


def add_halves(meta, keep, got, col_count):
    rows, lanes = keep.shape
    lanes //= col_count
    tall = rows // 4
    place = lambda k: lambda t, meta: (t, meta[1] ^ k)
    return pl.pallas_call(
        add_halves_kernel,
        out_shape=[jax.ShapeDtypeStruct((rows, lanes), jnp.bfloat16)] * col_count,
        grid_spec=pltpu.PrefetchScalarGridSpec(
            num_scalar_prefetch=1,
            grid=(rows // tall,),
            in_specs=[pl.BlockSpec((tall, lanes), place(k)) for k in range(col_count)] * 2,
            out_specs=[pl.BlockSpec((tall, lanes), lambda t, meta: (t, 0))] * col_count,
        ),
        compiler_params=pltpu.CompilerParams(vmem_limit_bytes=VMEM_LIMIT),
        cost_estimate=pl.CostEstimate(
            flops=keep.size, bytes_accessed=6 * keep.size, transcendentals=0
        ),
    )(meta, *[keep] * col_count, *[got] * col_count)


def total_of(refs, part):
    total = refs[0][part, :].astype(jnp.float32)
    for ref in refs[1:]:
        total += ref[part, :].astype(jnp.float32)
    return total.astype(jnp.bfloat16)


def add_quarters_kernel(col_count, meta_ref, *refs):
    blocks, outs = refs[:col_count], refs[col_count:]
    rows = outs[0].shape[0]
    for q, out in enumerate(outs):
        place = (meta_ref[0] // 2 ^ q) * rows
        out[...] = total_of(blocks, pl.ds(pl.multiple_of(place, rows), rows))


def add_quarters(meta, blocks, pair_count):
    rows, lanes = blocks[0].shape
    shape = jax.ShapeDtypeStruct((rows // pair_count, lanes), jnp.bfloat16)
    return local_call(
        lambda *refs: add_quarters_kernel(len(blocks), *refs),
        [shape] * pair_count,
        (meta, *blocks),
        10 * rows * lanes,
    )


def add_parts_kernel(meta_ref, *refs):
    rows = refs[-1].shape[0]
    refs[-1][...] = total_of(refs[:-1], pl.ds(0, rows))


def add_parts(meta, parts):
    return local_call(
        add_parts_kernel,
        jax.ShapeDtypeStruct(parts[0].shape, jnp.bfloat16),
        (meta, *parts),
        10 * parts[0].size,
    )


def stack_kernel(meta_ref, *refs):
    parts, out = refs[:-1], refs[-1]
    rows = parts[0].shape[0]
    for q, part in enumerate(parts):
        out[pl.ds(pl.multiple_of((meta_ref[0] // 2 ^ q) * rows, rows), rows), :] = part[...]


def stack(meta, parts):
    rows, lanes = parts[0].shape
    return local_call(
        stack_kernel,
        jax.ShapeDtypeStruct((rows * len(parts), lanes), jnp.bfloat16),
        (meta, *parts),
        4 * rows * lanes * len(parts),
    )


def tile_rows(b):
    return pl.ds(pl.multiple_of(b * TILE, TILE), TILE)


def first_product(panel, b, jitter, matrix, total, factor):
    product = jnp.dot(panel, matrix[...], preferred_element_type=jnp.float32)
    factor[tile_rows(b), :] = (coef_three * product).astype(jnp.bfloat16)
    total[pl.ds(pl.multiple_of(b * TILE + jitter, 8), TILE), :] = (
        coef_one * matrix[tile_rows(b), :].astype(jnp.float32) + coef_two * product
    )


def second_product(panel, b, jitter, total, factor):
    place = pl.ds(pl.multiple_of(b * TILE + jitter, 8), TILE)
    total[place, :] = math.sqrt(N) * (
        total[place, :] + jnp.dot(panel, factor[...], preferred_element_type=jnp.float32)
    )


def clear_edges(total, jitter):
    edge = jnp.zeros((jitter, total.shape[1]), jnp.float32)
    total[pl.ds(0, jitter), :] = edge
    total[pl.ds(M + jitter, jitter), :] = edge


def store_windows(row, send, total, outs):
    unit, share, rows, distances = send
    for distance, out in zip(distances, outs):
        place = pl.ds(pl.multiple_of(((row // share) ^ distance) * unit, 8), rows)
        out[...] = total[place, :].astype(jnp.bfloat16)


def first_apply_kernel(jitter, send, col_count, rows_ref, cols_ref, meta_ref, *refs):
    count = 2 * PIECES * col_count
    blocks, matrix, outs, gram_out = refs[:count], refs[count], refs[count + 1 : -6], refs[-6]
    gram, total, factor, tile_sems, out_sem = refs[-5:]
    lanes = TILE // col_count
    tiles = []
    for n in range(2 * HALF):
        half, part = divmod(n, HALF)
        pair = (meta_ref[0] % 2 ^ half) * HALF + part
        i, j = rows_ref[pair], cols_ref[pair]
        rows = pl.ds(part % PART * TILE, TILE)
        first = (half * PIECES + part // PART) * col_count
        moves = [
            (
                blocks[first + k].at[rows, :],
                gram.at[i, :, lane_block(j * col_count + (meta_ref[1] ^ k), lanes)],
            )
            for k in range(col_count)
        ]
        copies = [
            pltpu.make_async_copy(source, target, tile_sems.at[n, k])
            for k, (source, target) in enumerate(moves)
        ]
        for copy in copies:
            copy.start()
        tiles.append((copies, i, j))
    clear_edges(total, jitter)
    for copies, i, j in tiles:
        for copy in copies:
            copy.wait()

        @pl.when(i != j)
        def _():
            gram[j, :, lane_block(i, TILE)] = gram[i, :, lane_block(j, TILE)].T

    back = pltpu.make_async_copy(gram, gram_out, out_sem)
    back.start()

    @pl.loop(0, BLOCKS)
    def _(b):
        first_product(gram[b], b, jitter, matrix, total, factor)

    @pl.loop(0, BLOCKS)
    def _(b):
        second_product(gram[b], b, jitter, total, factor)

    store_windows(meta_ref[0], send, total, outs)
    back.wait()


def first_apply(meta, own, twin, matrix, send, jitter):
    pieces = [*own, *twin]
    col_count = len(own) // PIECES
    width = matrix.shape[1]
    whole = pl.BlockSpec(memory_space=pltpu.VMEM)
    outs = pl.pallas_call(
        lambda *refs: first_apply_kernel(jitter, send, col_count, *refs),
        out_shape=[jax.ShapeDtypeStruct((send[2], width), jnp.bfloat16)] * len(send[3])
        + [jax.ShapeDtypeStruct((BLOCKS, TILE, M), jnp.bfloat16)],
        in_specs=[pl.BlockSpec(memory_space=pltpu.SMEM)] * 3
        + [pl.BlockSpec(memory_space=pl.ANY)] * len(pieces)
        + [whole],
        out_specs=[whole] * len(send[3]) + [pl.BlockSpec(memory_space=pl.ANY)],
        scratch_shapes=[
            pltpu.VMEM((BLOCKS, TILE, M), jnp.bfloat16),
            pltpu.VMEM((M + 2 * jitter, width), jnp.float32),
            pltpu.VMEM((M, width), jnp.bfloat16),
            pltpu.SemaphoreType.DMA((len(PAIRS), col_count)),
            pltpu.SemaphoreType.DMA,
        ],
        compiler_params=pltpu.CompilerParams(vmem_limit_bytes=VMEM_LIMIT),
        cost_estimate=pl.CostEstimate(
            flops=4 * M * M * width, bytes_accessed=4 * M * width + 4 * M * M, transcendentals=0
        ),
    )(jnp.asarray(PAIR_ROWS), jnp.asarray(PAIR_COLS), meta, *pieces, matrix)
    return outs[:-1], outs[-1]


def next_apply_kernel(jitter, sends, meta_ref, panel_ref, *refs):
    chunks = len(sends)
    outs_count = sum(len(s[3]) for s in sends)
    matrices = refs[:chunks]
    outs = refs[chunks : chunks + outs_count]
    totals = refs[chunks + outs_count : 2 * chunks + outs_count]
    factors = refs[2 * chunks + outs_count :]
    turn = pl.program_id(0)

    @pl.when(turn < BLOCKS)
    def _():
        for matrix, total, factor in zip(matrices, totals, factors):
            first_product(panel_ref[0], turn, jitter, matrix, total, factor)

    @pl.when(turn >= BLOCKS)
    def _():
        for total, factor in zip(totals, factors):
            second_product(panel_ref[0], turn - BLOCKS, jitter, total, factor)

    @pl.when(turn == 2 * BLOCKS - 1)
    def _():
        place = 0
        for total, send in zip(totals, sends):
            clear_edges(total, jitter)
            store_windows(meta_ref[0], send, total, outs[place : place + len(send[3])])
            place += len(send[3])


def next_apply(meta, gram, matrices, sends, jitter):
    widths = [x.shape[1] for x in matrices]
    shapes = [(send[2], width) for width, send in zip(widths, sends) for _ in send[3]]
    whole = lambda t, meta: (0, 0)
    outs = pl.pallas_call(
        lambda *refs: next_apply_kernel(jitter, sends, *refs),
        out_shape=[jax.ShapeDtypeStruct(shape, jnp.bfloat16) for shape in shapes],
        grid_spec=pltpu.PrefetchScalarGridSpec(
            num_scalar_prefetch=1,
            grid=(2 * BLOCKS,),
            in_specs=[pl.BlockSpec((1, TILE, M), lambda t, meta: (t % BLOCKS, 0, 0))]
            + [pl.BlockSpec((M, width), whole) for width in widths],
            out_specs=[pl.BlockSpec(shape, whole) for shape in shapes],
            scratch_shapes=[pltpu.VMEM((M + 2 * jitter, width), jnp.float32) for width in widths]
            + [pltpu.VMEM((M, width), jnp.bfloat16) for width in widths],
        ),
        compiler_params=pltpu.CompilerParams(vmem_limit_bytes=VMEM_LIMIT),
        cost_estimate=pl.CostEstimate(
            flops=4 * M * M * sum(widths),
            bytes_accessed=4 * M * sum(widths) + 4 * M * M,
            transcendentals=0,
        ),
    )(meta, gram, *matrices)
    result = []
    for send in sends:
        result.append(outs[: len(send[3])])
        outs = outs[len(send[3]) :]
    return result


def sum_tiles(meta, joined, row_count, col_count):
    pair_count = row_count // 2
    tie = lax.optimization_barrier

    def over_cols(blocks):
        return [swap(blocks[k], "col", col_count, k) for k in range(1, col_count)]

    def over_pairs(blocks):
        return [swap(blocks[q], "row", row_count, 2 * q) for q in range(1, pair_count)]

    give = half_gram(meta, joined, 1, 0, PIECES)
    got = [swap(piece, "row", row_count, 1) for piece in give]
    keep = half_gram(meta, joined, 0, 0, 1)
    early = add_halves(meta, keep[0], got[0], col_count)
    early, joined = tie((early, joined))
    early_in = over_cols(early)
    keep = half_gram(meta, joined, 0, 1, 1)
    late = add_halves(meta, keep[0], got[1], col_count)
    late, early_in = tie((late, early_in))
    late_in = over_cols(late)
    early_parts = add_quarters(meta, [early[0]] + early_in, pair_count)
    early_in = over_pairs(early_parts)
    early_part = add_parts(meta, [early_parts[0]] + early_in)
    early_in = over_pairs([early_part] * pair_count)
    late_in, early_in = tie((late_in, early_in))
    late_parts = add_quarters(meta, [late[0]] + late_in, pair_count)
    early_block = stack(meta, [early_part] + early_in)
    early_in = over_cols([early_block] * col_count)
    late_in = over_pairs(late_parts)
    late_part = add_parts(meta, [late_parts[0]] + late_in)
    late_in = over_pairs([late_part] * pair_count)
    late_in, early_in = tie((late_in, early_in))
    late_block = stack(meta, [late_part] + late_in)
    late_in = over_cols([late_block] * col_count)
    early = [early_block] + early_in
    early_twin = [swap(block, "row", row_count, 1) for block in early]
    late = [late_block] + late_in
    late_twin = [swap(block, "row", row_count, 1) for block in late]
    return early + late, early_twin + late_twin


def chunk_body(momentum_shards, shard_starts):
    col_count = lax.axis_size("col")
    row_count = lax.axis_size("row")
    pair_count = row_count // 2
    slots = momentum_shards.shape[0]
    mean_rows = M // (row_count * col_count)
    jitter = 4 * (mean_rows // 8)
    even = col_count * mean_rows
    window = even + 2 * jitter
    row = lax.axis_index("row").astype(jnp.int32)
    col = lax.axis_index("col").astype(jnp.int32)
    shard_ends = jnp.concatenate([shard_starts[1:], jnp.full((1,), M, jnp.int32)])
    members = row * col_count + (col ^ jnp.arange(col_count, dtype=jnp.int32))
    begins = shard_starts[members]
    meta = jnp.concatenate(
        [row[None], col[None], begins - (row * even - jitter), shard_ends[members] - begins]
    )

    choose = selections(meta, col_count, slots, window)
    spread = jnp.swapaxes(choose, 1, 2)

    wide = row_count * col_count * CHUNK
    number = (N // (row_count * col_count)) // CHUNK
    distances = list(range(pair_count))

    def fetch(base, span, after):
        place, after = lax.optimization_barrier((col, after))
        received = [
            swap(
                lax.dynamic_slice_in_dim(
                    momentum_shards, base + (place ^ k) * span, span, axis=1
                ),
                "col",
                col_count,
                k,
            )
            for k in range(1, col_count)
        ]
        return received, after

    def across(pieces):
        return [pieces[0]] + [swap(pieces[q], "row", row_count, 2 * q) for q in distances[1:]]

    far_first = distances[pair_count // 2 :] + distances[: pair_count // 2]

    def tie(crossed, other):
        ordered, other = lax.optimization_barrier(([crossed[q] for q in far_first], other))
        return [ordered[far_first.index(q)] for q in distances], other

    def gather_chunk(c, received):
        keep, give = pack_pair(
            meta, choose, momentum_shards, received, c * wide, CHUNK, row_count, window
        )
        return join(meta, keep, swap(give, "row", row_count, 1), even, window, pair_count)

    last, _ = fetch(number * wide, pair_count * LAST, shard_starts)
    received, last = fetch(0, row_count * CHUNK, last)
    pieces = pack(
        meta, choose, momentum_shards, last, number * wide, LAST, 2, pair_count, window
    )
    crossed_last, received = tie(across(pieces), received)
    joined = gather_chunk(0, received)
    landed = []
    for c in range(1, number):
        received, joined = fetch(c * wide, row_count * CHUNK, joined)
        crossed, received = tie(across(joined), received)
        landed.append(crossed)
        joined = gather_chunk(c, received)
    landed.append(across(joined))
    matrices = [
        merge(meta, pieces, [[q] for q in distances], 2 * even, 2, jitter) for pieces in landed
    ]
    twin = [swap(piece, "row", row_count, 1) for piece in crossed_last]
    matrices.append(
        merge(
            meta,
            crossed_last + twin,
            [[2 * q] for q in distances] + [[2 * q + 1] for q in distances],
            even,
            1,
            jitter,
        )
    )

    tiles = sum_tiles(meta, collect(meta, matrices), row_count, col_count)

    sends = [(2 * even, 2, even + window, distances)] * number
    sends.append((even, 1, window, [2 * q for q in distances]))
    first, gram = first_apply(meta, *tiles, matrices[0], sends[0], jitter)
    results = [first] + next_apply(meta, gram, matrices[1:], sends[1:], jitter)

    crossed = [across(results[0])]
    crossed[0], results[1:] = tie(crossed[0], results[1:])
    for pieces in results[1:]:
        crossed[-1], pieces = tie(crossed[-1], pieces)
        crossed.append(across(pieces))
    backs = []
    for c in range(number + 1):
        if c < number:
            got = swap(cut(meta, crossed[c], even, window), "row", row_count, 1)
            parts = list(
                unpack_pair(meta, spread, crossed[c], got, col_count, slots, even, window)
            )
        else:
            parts = unpack(meta, spread, crossed[c], col_count, slots, 2)
        if c + 1 == number:
            crossed[c + 1], parts[0] = tie(crossed[c + 1], parts[0])
        back = [parts[0]] + [swap(parts[k], "col", col_count, k) for k in range(1, col_count)]
        if c + 1 < number:
            crossed[c + 1], back = tie(crossed[c + 1], back)
        backs.append(back)
    out = jnp.zeros(momentum_shards.shape, jnp.bfloat16)
    for c, back in enumerate(backs):
        span = row_count * CHUNK if c < number else pair_count * LAST
        for k in range(col_count):
            out = lax.dynamic_update_slice_in_dim(
                out, back[k], c * wide + (col ^ k) * span, axis=1
            )
    return out


def body(momentum_shards, shard_starts):
    devices = lax.axis_size("col") * lax.axis_size("row")
    chunks = (N // devices) % CHUNK == LAST // 2 and N // devices > CHUNK
    powers = all(lax.axis_size(a) & (lax.axis_size(a) - 1) == 0 for a in ("row", "col"))
    jitter = 4 * (M // devices // 8)
    if chunks and powers and jitter % 8 == 0:
        return chunk_body(momentum_shards, shard_starts)
    return plain_body(momentum_shards, shard_starts)


def solution(mesh):
    in_specs = (P(("row", "col"), None), P())
    out_specs = P(("row", "col"), None)
    return jax.shard_map(body, mesh=mesh, in_specs=in_specs, out_specs=out_specs, check_vma=False)
```
